32 devices in a mesh: grp: 2 (over x), seq: 16 (over z, y, core).
Axes of the slice: x: 2, y: 2, z: 4, core: 2. Of those that a mesh axis runs over, the one named last changes fastest.
Arguments:
- activations: bfloat16 [1024, 2, 2048], P('seq', 'grp'), parts along dimension 1, may hold values from -6 to 6
- queries: bfloat16 [1024, 2, 4096], P('seq', 'grp'), parts along dimension 1, may hold values from -160 to 160
- keys: bfloat16 [1024, 2, 256], P('seq', 'grp'), parts along dimension 1, may hold values from -4 to 4
- norm_gain: float32 [2048], replicated, may hold values from 0.5 to 1.5
- value_weight: bfloat16 [2048, 256], P('seq'), may hold values from -0.125 to 0.125
- expert_ids: int32 [1024, 2, 4], P('seq', 'grp'), parts along dimension 1, may hold values from 0 to 15, all different within a row; in each aligned block of 64 rows (0 to 63, 64 to 127, ..., all dimensions but the last counted through in order) at most 24 rows name the same one
- gate_weights: float32 [1024, 2, 4], P('seq', 'grp'), parts along dimension 1, may hold values from 0.05 to 0.5
- w_gate_up: bfloat16 [16, 2048, 1536], P('seq'), may hold values from -0.125 to 0.125
- w_down: bfloat16 [16, 768, 2048], P('seq'), may hold values from -0.21875 to 0.21875
Outputs:
- context: bfloat16 [1024, 2, 4096], P('seq', 'grp'), parts along dimension 1
- layer_out: bfloat16 [1024, 2, 2048], P('seq', 'grp'), parts along dimension 1
The draws below stay inside these ranges and needn't reach their ends.
There are 2 independent parts, one for each index of `grp`. The reference program is written for one: setup_inputs(seed, part) draws one part's arguments, and reference() takes and returns one part's arrays. A program takes and returns all parts, laid end to end along the dimension named above; an argument that names none is the same for every part. Nothing has to cross between parts.
Inputs may be any that keep to these rules, and one draw needn't show every extreme that they name: `expert_ids`: each row names 4 different experts. Of the 64 rows of one device (64 positions of the one sequence), at most 24 name any one expert, a bound that some block reaches of them.
All inputs are finite; a program needn't handle non-finite values.
Results may differ from the reference program's by a relative error of at most 0.006.
Values may be sent and summed in bfloat16 or wider, within the bound.
No kernel may reach another device: no remote copies, remote signals or barrier semaphores. Data moves between devices by JAX's collectives and lax.ppermute only.
A program may use at most 128 MiB of HBM per device.

```python
import math
import jax
import jax.numpy as jnp
import numpy as np
from jax import lax

MODEL_DIMENSION = 2048
QUERY_HEADS = 32
KEY_VALUE_HEADS = 2
HEAD_DIMENSION = 128
FFW = 768
TOPK = 4
GROUP_SEQUENCES = 1
TOK_DEV = 64
EXPERTS = 16
CAP = 24
SEQUENCE_LENGTH = 1024
TOKENS = 1024
N_SEQ = 16


def drawn_rows(key):
    starting_keys = jnp.clip(jax.random.normal(jax.random.fold_in(key, 103), (SEQUENCE_LENGTH, GROUP_SEQUENCES, KEY_VALUE_HEADS, HEAD_DIMENSION), dtype=jnp.float32), -4.0, 4.0)
    return starting_keys


def draw_keys(key, part):
    starting_keys = drawn_rows(key)
    return starting_keys.reshape(SEQUENCE_LENGTH, GROUP_SEQUENCES, KEY_VALUE_HEADS * HEAD_DIMENSION).astype(jnp.bfloat16)


def draw_queries(key, part):
    key = jax.random.fold_in(key, 2)
    drawn = 2.5 * jnp.clip(jax.random.normal(key, (SEQUENCE_LENGTH, GROUP_SEQUENCES, QUERY_HEADS, HEAD_DIMENSION), dtype=jnp.float32), -5.0, 5.0)
    return drawn.reshape(SEQUENCE_LENGTH, GROUP_SEQUENCES, QUERY_HEADS * HEAD_DIMENSION).astype(jnp.bfloat16)


def level_of(own_key, extent, cuts, least, top_value):
    def one(axis_at, blocks):
        heights = jax.random.uniform(jax.random.fold_in(jax.random.fold_in(own_key, 6), axis_at), (blocks,), jnp.float32, least / len(cuts), top_value / len(cuts))
        return jnp.repeat(jnp.exp(heights), extent[axis_at] // blocks).reshape((-1,) + (1,) * (len(extent) - axis_at - 1))

    gain = one(*cuts[0])
    for cut in cuts[1:]:
        gain = gain * one(*cut)
    return gain


def deal_out(stream_key, own, number, rows, count, top, limit, slope):
    order = jax.random.permutation(stream_key, count)
    packed, common = load_shares(count, rows * top, limit, slope, True), load_shares(count, rows * top, limit, slope, False)
    places = jnp.arange(count)

    def named(sizes, rotation):
        used = int((sizes > 0).sum())
        fixed = max(1, used // 4)
        shifted = fixed + (places - fixed + rotation * (used - fixed)) % max(1, count - fixed)
        return jnp.zeros((count,), jnp.int32).at[order[jnp.where(places < fixed, places, shifted)]].set(jnp.asarray(sizes, jnp.int32))

    sizes = jnp.where(number % 4 == 0, named(packed, number // 4), named(common, number - number // 4 - 1))
    mixed = jax.random.permutation(jax.random.fold_in(own, 3), count)
    source_of, sink = mixed[0:count // 2 * 2:2], mixed[1:count // 2 * 2:2]
    room = jnp.minimum(sizes[source_of] - 1, limit - sizes[sink]) // 2
    room = jnp.where((source_of == order[0]) | (sink == order[0]) | (sizes[sink] == 0), 0, jnp.maximum(room, 0))
    shifted = jax.random.randint(jax.random.fold_in(own, 4), (count // 2,), 0, 1 << 20) % (room + 1)
    sizes = sizes.at[source_of].add(-shifted).at[sink].add(shifted)
    items = jnp.searchsorted(jnp.cumsum(sizes), jnp.arange(rows * top), side="right").astype(jnp.int32)
    grid = items.reshape(top, rows).T
    grid = grid[jax.random.permutation(jax.random.fold_in(own, 1), rows)]
    rotation = jax.random.randint(jax.random.fold_in(own, 2), (rows, 1), 0, top)
    return jnp.take_along_axis(grid, (jnp.arange(top)[None, :] + rotation) % top, axis=1)


def load_shares(amount, total, bound, slope, full):
    portions = [(1 << 20) // math.isqrt(grade ** slope) + 1 for grade in range(1, amount + 1)]
    largest = bound if full else min(bound, max(-(-total // amount), total * portions[0] // sum(portions)))
    least = 1 if total - largest >= amount - 1 else 0
    given, surplus = [largest] + [least] * (amount - 1), total - largest - least * (amount - 1)
    while surplus > 0:
        free = [i for i in range(1, amount) if given[i] < largest] or [i for i in range(1, amount) if given[i] < bound]
        mass, left = sum([portions[i] for i in free]), surplus
        for i in free:
            addition = min(bound - given[i], max(1, left * portions[i] // mass), surplus)
            given[i] = given[i] + addition
            surplus = surplus - addition
    return np.array(given)


def normal_values(stream_key, shape, spread, reach, cuts=(), kind=jnp.bfloat16):
    entries = jax.random.normal(stream_key, shape, jnp.float32) * spread
    if len(cuts) > 0:
        entries = level_of(stream_key, shape, cuts, -0.22, 0.18) * entries
    return jnp.clip(entries, min=-reach, max=reach).astype(kind)


def setup_inputs(seed: int = 0, part: int = 0) -> dict:
    key_list = jax.random.split(jax.random.key(seed), 10)
    part_splits = jax.random.split(jax.random.fold_in(key_list[9], part), 10)
    activations = normal_values(part_splits[0], (SEQUENCE_LENGTH, GROUP_SEQUENCES, MODEL_DIMENSION), 1.0, 6.0, ((0, 16),))
    queries = draw_queries(jax.random.fold_in(jax.random.fold_in(key_list[9], part), 71), part)
    keys = draw_keys(jax.random.fold_in(jax.random.fold_in(key_list[9], part), 71), part)
    norm_gain = jnp.clip(1.0 + 0.1 * jax.random.normal(key_list[3], (MODEL_DIMENSION,), jnp.float32), 0.5, 1.5)
    value_weight = normal_values(key_list[4], (MODEL_DIMENSION, KEY_VALUE_HEADS * HEAD_DIMENSION), MODEL_DIMENSION ** -0.5, 0.125, ((0, 16),))
    expert_ids_keys = jax.random.split(jax.random.fold_in(part_splits[5], 1), SEQUENCE_LENGTH * GROUP_SEQUENCES // TOK_DEV)
    expert_ids_turns = jax.random.permutation(jax.random.fold_in(part_splits[5], 3), SEQUENCE_LENGTH * GROUP_SEQUENCES // TOK_DEV)
    expert_ids = jax.vmap(lambda own, number: deal_out(jax.random.fold_in(part_splits[5], 2), own, number, TOK_DEV, EXPERTS, TOPK, CAP, 2))(expert_ids_keys, expert_ids_turns).reshape((SEQUENCE_LENGTH, GROUP_SEQUENCES, TOPK))
    gate_weights = jnp.clip(jnp.exp(math.log(0.5) - 2.3025851 * jax.random.uniform(part_splits[6], (SEQUENCE_LENGTH, GROUP_SEQUENCES, TOPK), jnp.float32) ** level_of(part_splits[6], (SEQUENCE_LENGTH, GROUP_SEQUENCES, TOPK), ((0, 16),), -0.2, 0.2)), 0.05, 0.5)
    w_gate_up = normal_values(key_list[7], (EXPERTS, MODEL_DIMENSION, 2 * FFW), MODEL_DIMENSION ** -0.5, 0.125, ((0, 16),))
    w_down = normal_values(key_list[8], (EXPERTS, FFW, MODEL_DIMENSION), FFW ** -0.5, 0.21875, ((0, 16),))
    return dict(activations=activations, queries=queries, keys=keys, norm_gain=norm_gain, value_weight=value_weight, expert_ids=expert_ids, gate_weights=gate_weights, w_gate_up=w_gate_up, w_down=w_down)


def normalize(activations, norm_gain):
    features = activations.astype(jnp.float32)
    inverse = lax.rsqrt(lax.optimization_barrier(jnp.mean(features * features, axis=-1, keepdims=True)) + 1e-06)
    return (features * inverse * norm_gain.astype(jnp.float32)).astype(jnp.bfloat16)

def attention(queries, keys, value_tensor):
    query_group = QUERY_HEADS // KEY_VALUE_HEADS
    rows_per_block = math.gcd(SEQUENCE_LENGTH, 64)
    key_head_rows = keys.astype(jnp.float32).reshape(SEQUENCE_LENGTH, GROUP_SEQUENCES, KEY_VALUE_HEADS, HEAD_DIMENSION)
    value_head_rows = value_tensor.astype(jnp.float32).reshape(SEQUENCE_LENGTH, GROUP_SEQUENCES, KEY_VALUE_HEADS, HEAD_DIMENSION)
    key_positions = jnp.arange(SEQUENCE_LENGTH).astype(jnp.int32)
    score_scale = 1.0 / math.sqrt(HEAD_DIMENSION)

    def one_block(block_index):
        first = (block_index * rows_per_block).astype(jnp.int32)
        query_block_size = lax.dynamic_slice_in_dim(queries, first, rows_per_block, 0)
        grouped_rows = query_block_size.astype(jnp.float32).reshape(rows_per_block, GROUP_SEQUENCES, KEY_VALUE_HEADS, query_group, HEAD_DIMENSION)
        scores = jnp.einsum('rskgd,pskd->rskgp', grouped_rows, key_head_rows, precision=lax.Precision.HIGHEST) * score_scale
        query_positions = first + jnp.arange(rows_per_block).astype(jnp.int32)
        visible = (query_positions[:, None] >= key_positions[None, :])[:, None, None, None, :]
        scores = jnp.where(visible, scores, -1e+30)
        top_score = lax.optimization_barrier(jnp.max(scores, axis=-1, keepdims=True))
        weights = jnp.where(visible, jnp.exp(scores - top_score), 0.0)
        total = lax.optimization_barrier(jnp.sum(weights, axis=-1))
        rounded = lax.optimization_barrier(weights.astype(jnp.bfloat16)).astype(jnp.float32)
        summed = jnp.einsum('rskgp,pskd->rskgd', rounded, value_head_rows, precision=lax.Precision.HIGHEST)
        return (summed / total[..., None]).reshape(rows_per_block, GROUP_SEQUENCES, QUERY_HEADS * HEAD_DIMENSION).astype(jnp.bfloat16)
    blocks = lax.map(one_block, jnp.arange(SEQUENCE_LENGTH // rows_per_block).astype(jnp.int32))
    return blocks.reshape(SEQUENCE_LENGTH, GROUP_SEQUENCES, QUERY_HEADS * HEAD_DIMENSION)

def experts_branch(normed, expert_ids, gate_weights, w_gate_up, w_down):
    pair_count = TOKENS * TOPK
    flat_rows = normed.reshape(TOKENS, MODEL_DIMENSION)
    flat_ids = expert_ids.reshape(-1).astype(jnp.int32)
    onehot = (flat_ids[:, None] == jnp.arange(EXPERTS).astype(jnp.int32)[None, :]).astype(jnp.int32)
    per_device = onehot.reshape(N_SEQ, TOK_DEV * TOPK, EXPERTS)
    earlier = (jnp.cumsum(per_device, axis=1) - per_device).reshape(pair_count, EXPERTS)
    slot_rank = lax.optimization_barrier(jnp.sum(earlier * onehot, axis=1)).astype(jnp.int32)
    source_device = (jnp.arange(pair_count).astype(jnp.int32) // (TOK_DEV * TOPK)).astype(jnp.int32)
    slot_index = (source_device * CAP + slot_rank).astype(jnp.int32)
    owner = jnp.full((EXPERTS, N_SEQ * CAP), pair_count, dtype=jnp.int32)
    owner = owner.at[flat_ids, slot_index].set(jnp.arange(pair_count).astype(jnp.int32))
    padded = jnp.concatenate([flat_rows, jnp.zeros((1, MODEL_DIMENSION), dtype=jnp.bfloat16)], axis=0)

    def one_expert(expert):
        expert_rows = padded[owner[expert] // TOPK]
        gate_up = jnp.dot(expert_rows, w_gate_up[expert], preferred_element_type=jnp.float32)
        hidden = (jax.nn.silu(gate_up[:, :FFW]) * gate_up[:, FFW:]).astype(jnp.bfloat16)
        return jnp.dot(hidden, w_down[expert], preferred_element_type=jnp.float32).astype(jnp.bfloat16)
    outputs = lax.map(one_expert, jnp.arange(EXPERTS).astype(jnp.int32))
    routed = outputs[flat_ids, slot_index].astype(jnp.float32).reshape(TOKENS, TOPK, MODEL_DIMENSION)
    weights = gate_weights.astype(jnp.float32).reshape(TOKENS, TOPK)
    return lax.optimization_barrier(jnp.sum(routed * weights[..., None], axis=1)).reshape(SEQUENCE_LENGTH, GROUP_SEQUENCES, MODEL_DIMENSION)

def reference(activations, queries, keys, norm_gain, value_weight, expert_ids, gate_weights, w_gate_up, w_down):
    normed = normalize(activations, norm_gain)
    value_tensor = jnp.dot(normed.reshape(TOKENS, MODEL_DIMENSION), value_weight, preferred_element_type=jnp.float32).astype(jnp.bfloat16)
    value_tensor = value_tensor.reshape(SEQUENCE_LENGTH, GROUP_SEQUENCES, KEY_VALUE_HEADS * HEAD_DIMENSION)
    context = attention(queries, keys, value_tensor)
    combined = experts_branch(normed, expert_ids, gate_weights, w_gate_up, w_down)
    layer_out = (activations.astype(jnp.float32) + combined).astype(jnp.bfloat16)
    return (context, layer_out)
```

```python
import functools
import math

import jax
import jax.numpy as jnp
from jax import lax
from jax.experimental import pallas as pl
from jax.experimental.pallas import tpu as pltpu
from jax.sharding import PartitionSpec as P

QUERY_HEADS = 32
KEY_VALUE_HEADS = 2
HEAD_DIMENSION = 128
GROUPS = 4
META = 128
F32 = jnp.float32
BF16 = jnp.bfloat16


def dot(a, b):
    return jnp.dot(a, b, preferred_element_type=F32)


def pack_kernel(act_ref, gain_ref, ids_ref, gates_ref, out_ref, meta_ref):
    width = act_ref.shape[1]
    rows = act_ref.shape[0]
    top = ids_ref.shape[0]
    features = act_ref[...].astype(F32)
    inverse = lax.rsqrt(jnp.mean(features * features, axis=-1, keepdims=True) + 1e-06)
    out_ref[:, :width] = (features * inverse * gain_ref[...]).astype(BF16)
    gates = gates_ref[...]
    high = gates.astype(BF16).astype(F32)
    rest = gates - high
    middle = rest.astype(BF16).astype(F32)
    meta_ref[...] = jnp.zeros_like(meta_ref)
    meta_ref[0:top, 0:rows] = ids_ref[...].astype(F32)
    meta_ref[8 : 8 + top, 0:rows] = high
    meta_ref[16 : 16 + top, 0:rows] = middle
    meta_ref[24 : 24 + top, 0:rows] = rest - middle
    out_ref[:, width:] = meta_ref[...].T[:rows, :].astype(BF16)


def pack(activations, norm_gain, ids, gates):
    rows, width = activations.shape
    assert rows <= META and ids.shape[0] <= 8
    return pl.pallas_call(
        pack_kernel,
        out_shape=jax.ShapeDtypeStruct((rows, width + META), BF16),
        scratch_shapes=[pltpu.VMEM((META, META), F32)],
        cost_estimate=pl.CostEstimate(
            flops=4 * rows * width, bytes_accessed=4 * rows * width, transcendentals=0
        ),
        name="normalize_and_pack",
    )(activations, norm_gain.reshape(1, width), ids, gates)


def expert_kernel(
    top,
    tok_rows,
    capacity,
    x_hbm,
    up_hbm,
    down_hbm,
    out_hbm,
    x_buf,
    up_buf,
    down_buf,
    slot_rows,
    slot_gates,
    places,
    hidden,
    result,
    x_sem,
    w_sem,
    out_sem,
):
    groups, rows, packed = x_buf.shape
    width = packed - META
    slots = slot_rows.shape[0] // groups
    units = down_buf.shape[0]
    tile = 256
    me = lax.axis_index("seq").astype(F32)

    def load(group):
        return pltpu.make_async_copy(
            x_hbm.at[pl.ds(group * rows, rows)], x_buf.at[group], x_sem.at[group]
        )

    def load_up(index):
        part = pl.ds(index * tile, tile)
        return pltpu.make_async_copy(up_hbm.at[:, part], up_buf.at[:, part], w_sem.at[index])

    up_parts = 2 * units // tile
    load_down = pltpu.make_async_copy(down_hbm, down_buf, w_sem.at[up_parts])

    def store(group):
        return pltpu.make_async_copy(
            x_buf.at[group, :, pl.ds(0, width)],
            out_hbm.at[pl.ds(group * rows, rows)],
            out_sem.at[group],
        )

    half = up_parts // 2
    for group in range(groups):
        load(group).start()
    for index in range(half):
        load_up(index).start()
        load_up(half + index).start()
    load_down.start()

    chunk = tok_rows * META // math.gcd(tok_rows, META)
    first = lax.broadcasted_iota(jnp.int32, (chunk, chunk), 0)
    second = lax.broadcasted_iota(jnp.int32, (chunk, chunk), 1)
    earlier = ((first < second) & (first // tok_rows == second // tok_rows)).astype(F32).astype(BF16)
    block = lax.broadcasted_iota(jnp.int32, (1, rows), 1) // tok_rows
    for group in range(groups):
        load(group).wait()
        meta = x_buf[group, :, width:].astype(F32).T
        gate = jnp.zeros((1, rows), F32)
        named = jnp.zeros((1, rows), F32)
        for k in range(top):
            match = meta[k : k + 1] == me
            value = meta[8 + k : 9 + k] + (meta[16 + k : 17 + k] + meta[24 + k : 25 + k])
            gate = jnp.where(match, value, gate)
            named = jnp.where(match, 1.0, named)
        marks = jnp.broadcast_to(named, (8, rows)).astype(BF16)
        rank = jnp.concatenate(
            [
                dot(marks[:, at : at + chunk], earlier)
                for at in range(0, rows, chunk)
            ],
            axis=1,
        )[0:1]
        slot = jnp.where(named > 0.0, (block * capacity).astype(F32) + rank, -1.0)
        spots = lax.broadcasted_iota(jnp.int32, (slots, rows), 0).astype(F32)
        chosen = spots == slot
        slot_gates[pl.ds(group * slots, slots)] = jnp.broadcast_to(
            jnp.sum(jnp.where(chosen, gate, 0.0), axis=1, keepdims=True), (slots, META)
        )
        pick = chosen.astype(F32).astype(BF16)
        for at in range(0, width, 512):
            slot_rows[pl.ds(group * slots, slots), at : at + 512] = dot(
                pick, x_buf[group, :, at : at + 512]
            ).astype(BF16)
        by_row = jnp.broadcast_to(slot, (META, rows)).T
        spots = lax.broadcasted_iota(jnp.int32, (rows, META), 1).astype(F32)
        places[group] = (spots == by_row).astype(F32).astype(BF16)

    for index in range(half):
        load_up(index).wait()
        load_up(half + index).wait()
        gate = dot(slot_rows[...], up_buf[:, index * tile : (index + 1) * tile])
        up = dot(slot_rows[...], up_buf[:, units + index * tile : units + (index + 1) * tile])
        hidden[:, index * tile : (index + 1) * tile] = (
            gate / (1.0 + jnp.exp(-gate)) * up
        ).astype(BF16)
    load_down.wait()
    for at in range(0, width, 256):
        out = dot(hidden[...], down_buf[:, at : at + 256]).astype(BF16).astype(F32)
        result[:, at : at + 256] = (out * slot_gates[:, 0:1]).astype(BF16)
    for group in range(groups):
        for at in range(0, width, 512):
            x_buf[group, :, at : at + 512] = dot(
                places[group, :, :slots],
                result[pl.ds(group * slots, slots), at : at + 512],
            ).astype(BF16)
        store(group).start()
    for group in range(groups):
        store(group).wait()


def run_experts(gathered, w_gate_up, w_down, top, tok_rows, capacity):
    total, packed = gathered.shape
    width = packed - META
    units = w_down.shape[0]
    rows = total // GROUPS
    slots = rows // tok_rows * capacity
    assert slots % 16 == 0 and slots <= META and units % 256 == 0 and width % 512 == 0
    all_slots = GROUPS * slots
    held = (
        2 * total * packed
        + 6 * units * width
        + all_slots * (4 * width + 2 * units + 4 * META)
        + 2 * total * META
    )
    return pl.pallas_call(
        functools.partial(expert_kernel, top, tok_rows, capacity),
        out_shape=jax.ShapeDtypeStruct((total, width), BF16),
        in_specs=[pl.BlockSpec(memory_space=pl.ANY)] * 3,
        out_specs=pl.BlockSpec(memory_space=pl.ANY),
        scratch_shapes=[
            pltpu.VMEM((GROUPS, rows, packed), BF16),
            pltpu.VMEM((width, 2 * units), BF16),
            pltpu.VMEM((units, width), BF16),
            pltpu.VMEM((all_slots, width), BF16),
            pltpu.VMEM((all_slots, META), F32),
            pltpu.VMEM((GROUPS, rows, META), BF16),
            pltpu.VMEM((all_slots, units), BF16),
            pltpu.VMEM((all_slots, width), BF16),
            pltpu.SemaphoreType.DMA((GROUPS,)),
            pltpu.SemaphoreType.DMA((2 * units // 256 + 1,)),
            pltpu.SemaphoreType.DMA((GROUPS,)),
        ],
        compiler_params=pltpu.CompilerParams(vmem_limit_bytes=held + 8 * 2**20),
        cost_estimate=pl.CostEstimate(
            flops=6 * all_slots * width * units + 4 * all_slots * rows * width,
            bytes_accessed=4 * total * width + 6 * units * width,
            transcendentals=all_slots * units,
        ),
        name="experts",
    )(gathered, w_gate_up, w_down)


def attention_kernel(
    key_rows,
    q_ref,
    x_ref,
    small_hbm,
    out_ref,
    keys,
    weight,
    values,
    top_score,
    run_sum,
    run_acc,
    sems,
):
    step = pl.program_id(0)
    steps = pl.num_programs(0)
    chunk = x_ref.shape[0]
    q_rows, q_width = q_ref.shape
    width = x_ref.shape[1] - META
    heads = q_width // HEAD_DIMENSION
    together = 4
    per_kv = heads // KEY_VALUE_HEADS
    blocks = chunk // key_rows
    kv_width = KEY_VALUE_HEADS * HEAD_DIMENSION
    q_start = lax.axis_index("seq") * q_rows
    factor = math.log2(math.e) / math.sqrt(HEAD_DIMENSION)

    load_keys = pltpu.make_async_copy(
        small_hbm.at[pl.ds(step * blocks, blocks), pl.ds(0, key_rows)], keys, sems.at[0]
    )
    load_weight = pltpu.make_async_copy(
        small_hbm.at[:, pl.ds(key_rows, small_hbm.shape[1] - key_rows)], weight, sems.at[1]
    )
    load_keys.start()

    @pl.when(step == 0)
    def _():
        load_weight.start()
        load_weight.wait()
        if top_score is not None:
            top_score[...] = jnp.full_like(top_score, -1e30)
            run_sum[...] = jnp.zeros_like(run_sum)
            run_acc[...] = jnp.zeros_like(run_acc)

    load_keys.wait()

    def attend():
        values[...] = dot(x_ref[:, :width], weight[...].reshape(width, kv_width)).astype(BF16)
        all_keys = keys[...].reshape(chunk, kv_width)
        q_at = q_start + lax.broadcasted_iota(jnp.int32, (q_rows, chunk), 0)
        k_at = step * chunk + lax.broadcasted_iota(jnp.int32, (q_rows, chunk), 1)
        bias = jnp.where(q_at >= k_at, 0.0, -1e30)[None]
        for at in range(0, heads, together):
            kv = at // per_kv * HEAD_DIMENSION
            rows = jnp.concatenate(
                [
                    q_ref[:, h * HEAD_DIMENSION : (h + 1) * HEAD_DIMENSION]
                    for h in range(at, at + together)
                ],
                axis=0,
            )
            scores = lax.dot_general(
                rows,
                all_keys[:, kv : kv + HEAD_DIMENSION],
                (((1,), (1,)), ((), ())),
                preferred_element_type=F32,
            )
            scores = (scores.reshape(together, q_rows, chunk) + bias).reshape(
                together * q_rows, chunk
            )
            best = jnp.max(scores, axis=1, keepdims=True)
            place = slice(at * q_rows, (at + together) * q_rows)
            if top_score is not None:
                before = top_score[place, 0:1]
                best = jnp.maximum(best, before)
                rescale = jnp.exp2((before - best) * factor)
                top_score[place] = jnp.broadcast_to(best, (together * q_rows, HEAD_DIMENSION))
            weights = jnp.exp2((scores - best) * factor)
            total = jnp.sum(weights, axis=1, keepdims=True)
            added = dot(weights.astype(BF16), values[:, kv : kv + HEAD_DIMENSION])
            if top_score is not None:
                total = run_sum[place, 0:1] * rescale + total
                added = run_acc[place] * rescale + added
                run_sum[place] = jnp.broadcast_to(total, (together * q_rows, HEAD_DIMENSION))
                run_acc[place] = added
            context = (added / total).astype(BF16)
            for h in range(together):
                out_ref[:, (at + h) * HEAD_DIMENSION : (at + h + 1) * HEAD_DIMENSION] = context[
                    h * q_rows : (h + 1) * q_rows
                ]

    if top_score is None:
        attend()
    else:
        pl.when(step * chunk <= q_start + q_rows - 1)(attend)


def attend_all(queries, gathered, small, key_rows):
    q_rows, q_width = queries.shape
    total, packed = gathered.shape
    width = packed - META
    chunk = math.gcd(total, 1024)
    steps = total // chunk
    kv_width = small.shape[2]
    heads = q_width // HEAD_DIMENSION
    weight_rows = small.shape[1] - key_rows
    state = [pltpu.VMEM((heads * q_rows, HEAD_DIMENSION), F32)] * 3
    kernel = functools.partial(attention_kernel, key_rows)
    if steps == 1:
        state = []

        def kernel(q_ref, x_ref, small_hbm, out_ref, keys, weight, values, sems):
            attention_kernel(
                key_rows, q_ref, x_ref, small_hbm, out_ref, keys, weight, values, None, None, None, sems
            )

    return pl.pallas_call(
        kernel,
        grid=(steps,),
        out_shape=jax.ShapeDtypeStruct((q_rows, q_width), BF16),
        in_specs=[
            pl.BlockSpec((q_rows, q_width), lambda i: (0, 0)),
            pl.BlockSpec((chunk, packed), lambda i: (i, 0)),
            pl.BlockSpec(memory_space=pl.ANY),
        ],
        out_specs=pl.BlockSpec((q_rows, q_width), lambda i: (0, 0)),
        scratch_shapes=[
            pltpu.VMEM((chunk // key_rows, key_rows, kv_width), BF16),
            pltpu.VMEM((small.shape[0], weight_rows, kv_width), BF16),
            pltpu.VMEM((chunk, kv_width), BF16),
            *state,
            pltpu.SemaphoreType.DMA((2,)),
        ],
        compiler_params=pltpu.CompilerParams(vmem_limit_bytes=40 * 2**20),
        cost_estimate=pl.CostEstimate(
            flops=4 * q_rows * q_width * total + 2 * total * width * kv_width,
            bytes_accessed=2 * total * packed + 4 * q_rows * q_width,
            transcendentals=heads * q_rows * total,
        ),
        name="attention",
    )(queries, gathered, small)


def per_device(
    activations, queries, keys, norm_gain, value_weight, expert_ids, gate_weights, w_gate_up, w_down
):
    pos_rows, sequence_count, model_width = activations.shape
    assert sequence_count == 1 and w_down.shape[0] == 1
    top = expert_ids.shape[2]
    devices = lax.axis_size("seq")
    capacity = max(2, 3 * pos_rows * top // (2 * devices))
    acts = activations.reshape(pos_rows, model_width)
    packed = pack(
        acts,
        norm_gain,
        expert_ids.transpose(1, 2, 0).reshape(top, pos_rows),
        gate_weights.transpose(1, 2, 0).reshape(top, pos_rows),
    )
    gathered = lax.all_gather(packed, "seq", axis=0, tiled=True)
    small = jnp.concatenate([keys.reshape(pos_rows, -1), value_weight], axis=0)
    small = lax.all_gather(small, "seq", axis=0, tiled=False)
    partial = run_experts(gathered, w_gate_up[0], w_down[0], top, pos_rows, capacity)
    combined = lax.psum_scatter(partial, "seq", scatter_dimension=0, tiled=True)
    context = attend_all(queries.reshape(pos_rows, -1), gathered, small, pos_rows)
    layer_out = (acts.astype(F32) + combined.astype(F32)).astype(BF16)
    return (context.reshape(queries.shape), layer_out.reshape(activations.shape))


def solution(mesh):
    placed = (
        P("seq", "grp", None),
        P("seq", "grp", None),
        P("seq", "grp", None),
        P(),
        P("seq", None),
        P("seq", "grp", None),
        P("seq", "grp", None),
        P("seq", None, None),
        P("seq", None, None),
    )
    return jax.shard_map(
        per_device,
        mesh=mesh,
        in_specs=placed,
        out_specs=(P("seq", "grp", None), P("seq", "grp", None)),
        check_vma=False,
    )
```

```python
import functools
import math

import jax
import jax.numpy as jnp
from jax import lax
from jax.experimental import pallas as pl
from jax.experimental.pallas import tpu as pltpu
from jax.sharding import PartitionSpec as P

QUERY_HEADS = 32
KEY_VALUE_HEADS = 2
HEAD_DIMENSION = 128
GROUPS = 4
META = 128
LINE = 4
VMEM_LIMIT = 60 * 2**20
F32 = jnp.float32
BF16 = jnp.bfloat16
ANY = pl.BlockSpec(memory_space=pl.ANY)
IN_VMEM = pl.BlockSpec(memory_space=pltpu.VMEM)


def dot(a, b):
    return jnp.dot(a, b, preferred_element_type=F32)


RING = (0, 1, 3, 2)


def device_index(place, y, core):
    return (RING[place % LINE] * 2 + y) * 2 + core


def swaps(flip_y, flip_core):
    return [
        (device_index(p, y, c), device_index(p, y ^ flip_y, c ^ flip_core))
        for p in range(LINE)
        for y in range(2)
        for c in range(2)
    ]


def ring_step():
    return [
        (device_index(p, y, c), device_index(p + 1, y, c))
        for p in range(LINE)
        for y in range(2)
        for c in range(2)
    ]


def along_ring(x):
    return lax.ppermute(x, "seq", ring_step())


def across(x):
    return lax.ppermute(x, "seq", swaps(1, 0))


def other_core(x):
    return lax.ppermute(x, "seq", swaps(0, 1))


def from_device(steps, flip_y, flip_core):
    me = lax.axis_index("seq")
    core, y, line = me % 2, me // 2 % 2, me // 4
    place = sum(jnp.where(line == RING[p], p, 0) for p in range(LINE))
    place = (place + LINE - steps) % LINE
    line = sum(jnp.where(place == p, RING[p], 0) for p in range(LINE))
    y = 1 - y if flip_y else y
    core = 1 - core if flip_core else core
    return (line * 2 + y) * 2 + core


def pack_kernel(act_ref, gain_ref, ids_ref, gates_ref, out_ref, meta_ref):
    width = act_ref.shape[1]
    rows = act_ref.shape[0]
    top = ids_ref.shape[0]
    features = act_ref[...].astype(F32)
    inverse = lax.rsqrt(jnp.mean(features * features, axis=-1, keepdims=True) + 1e-06)
    out_ref[:, :width] = (features * inverse * gain_ref[...]).astype(BF16)
    gates = gates_ref[...]
    high = gates.astype(BF16).astype(F32)
    rest = gates - high
    middle = rest.astype(BF16).astype(F32)
    meta_ref[...] = jnp.zeros_like(meta_ref)
    meta_ref[0:top, 0:rows] = ids_ref[...].astype(F32)
    meta_ref[8 : 8 + top, 0:rows] = high
    meta_ref[16 : 16 + top, 0:rows] = middle
    meta_ref[24 : 24 + top, 0:rows] = rest - middle
    out_ref[:, width:] = meta_ref[...].T[:rows, :].astype(BF16)


def pack(activations, norm_gain, ids, gates):
    rows, width = activations.shape
    assert rows <= META and ids.shape[0] <= 8
    return pl.pallas_call(
        pack_kernel,
        out_shape=jax.ShapeDtypeStruct((rows, width + META), BF16),
        scratch_shapes=[pltpu.VMEM((META, META), F32)],
        cost_estimate=pl.CostEstimate(
            flops=4 * rows * width, bytes_accessed=4 * rows * width, transcendentals=0
        ),
        name="normalize_and_pack",
    )(activations, norm_gain.reshape(1, width), ids, gates)


def expert_kernel(top, tok_rows, capacity, sources, targets, *refs):
    inputs = 1 + max(s[0] for group in sources for s in group)
    outputs = 1 + max(t[0] for group in targets for t in group)
    x_hbm = refs[:inputs]
    up_hbm, down_hbm = refs[inputs : inputs + 2]
    out_hbm = refs[inputs + 2 : inputs + 2 + outputs]
    (
        x_buf,
        up_buf,
        down_buf,
        slot_rows,
        slot_gates,
        places,
        hidden,
        result,
        x_sem,
        w_sem,
        out_sem,
    ) = refs[inputs + 2 + outputs :]
    groups, rows, packed = x_buf.shape
    width = packed - META
    slots = slot_rows.shape[0] // groups
    units = down_buf.shape[0]
    tile = 256
    me = lax.axis_index("seq").astype(F32)

    def loads(group):
        copies, at = [], 0
        for number, (operand, first, count) in enumerate(sources[group]):
            copies.append(
                pltpu.make_async_copy(
                    x_hbm[operand].at[pl.ds(first, count)],
                    x_buf.at[group, pl.ds(at, count)],
                    x_sem.at[group, number],
                )
            )
            at += count
        return copies

    def stores(group):
        copies, at = [], 0
        for number, (operand, first, count) in enumerate(targets[group]):
            copies.append(
                pltpu.make_async_copy(
                    x_buf.at[group, pl.ds(at, count), pl.ds(0, width)],
                    out_hbm[operand].at[pl.ds(first, count)],
                    out_sem.at[group, number],
                )
            )
            at += count
        return copies

    def load_up(index):
        part = pl.ds(index * tile, tile)
        return pltpu.make_async_copy(up_hbm.at[:, part], up_buf.at[:, part], w_sem.at[index])

    up_parts = 2 * units // tile
    load_down = pltpu.make_async_copy(down_hbm, down_buf, w_sem.at[up_parts])
    half = up_parts // 2
    for group in range(groups):
        for copy in loads(group):
            copy.start()
    for index in range(half):
        load_up(index).start()
        load_up(half + index).start()
    load_down.start()

    chunk = tok_rows * META // math.gcd(tok_rows, META)
    first = lax.broadcasted_iota(jnp.int32, (chunk, chunk), 0)
    second = lax.broadcasted_iota(jnp.int32, (chunk, chunk), 1)
    earlier = ((first < second) & (first // tok_rows == second // tok_rows)).astype(F32).astype(BF16)
    block = lax.broadcasted_iota(jnp.int32, (1, rows), 1) // tok_rows
    for group in range(groups):
        for copy in loads(group):
            copy.wait()
        meta = x_buf[group, :, width:].astype(F32).T
        gate = jnp.zeros((1, rows), F32)
        named = jnp.zeros((1, rows), F32)
        for k in range(top):
            match = meta[k : k + 1] == me
            value = meta[8 + k : 9 + k] + (meta[16 + k : 17 + k] + meta[24 + k : 25 + k])
            gate = jnp.where(match, value, gate)
            named = jnp.where(match, 1.0, named)
        marks = jnp.broadcast_to(named, (8, rows)).astype(BF16)
        rank = jnp.concatenate(
            [dot(marks[:, at : at + chunk], earlier) for at in range(0, rows, chunk)], axis=1
        )[0:1]
        slot = jnp.where(named > 0.0, (block * capacity).astype(F32) + rank, -1.0)
        spots = lax.broadcasted_iota(jnp.int32, (slots, rows), 0).astype(F32)
        chosen = spots == slot
        slot_gates[pl.ds(group * slots, slots)] = jnp.broadcast_to(
            jnp.sum(jnp.where(chosen, gate, 0.0), axis=1, keepdims=True), (slots, META)
        )
        pick = chosen.astype(F32).astype(BF16)
        for at in range(0, width, 512):
            slot_rows[pl.ds(group * slots, slots), at : at + 512] = dot(
                pick, x_buf[group, :, at : at + 512]
            ).astype(BF16)
        by_row = jnp.broadcast_to(slot, (META, rows)).T
        spots = lax.broadcasted_iota(jnp.int32, (rows, META), 1).astype(F32)
        places[group] = (spots == by_row).astype(F32).astype(BF16)

    for index in range(half):
        load_up(index).wait()
        load_up(half + index).wait()
        gate = dot(slot_rows[...], up_buf[:, index * tile : (index + 1) * tile])
        up = dot(slot_rows[...], up_buf[:, units + index * tile : units + (index + 1) * tile])
        hidden[:, index * tile : (index + 1) * tile] = (gate / (1.0 + jnp.exp(-gate)) * up).astype(
            BF16
        )
    load_down.wait()
    for at in range(0, width, 256):
        out = dot(hidden[...], down_buf[:, at : at + 256]).astype(BF16).astype(F32)
        result[:, at : at + 256] = (out * slot_gates[:, 0:1]).astype(BF16)
    for group in range(groups):
        for at in range(0, width, 512):
            x_buf[group, :, at : at + 512] = dot(
                places[group, :, :slots], result[pl.ds(group * slots, slots), at : at + 512]
            ).astype(BF16)
        for copy in stores(group):
            copy.start()
    for group in range(groups):
        for copy in stores(group):
            copy.wait()


def run_experts(arrays, sources, targets, out_rows, w_gate_up, w_down, top, tok_rows, capacity):
    groups = len(sources)
    rows = sum(count for _, _, count in sources[0])
    packed = arrays[0].shape[1]
    total = groups * rows
    width = packed - META
    units = w_down.shape[0]
    slots = rows // tok_rows * capacity
    assert slots % 16 == 0 and slots <= META and units % 256 == 0 and width % 512 == 0
    all_slots = groups * slots
    return pl.pallas_call(
        functools.partial(expert_kernel, top, tok_rows, capacity, sources, targets),
        out_shape=[jax.ShapeDtypeStruct((count, width), BF16) for count in out_rows],
        in_specs=[ANY] * (len(arrays) + 2),
        out_specs=[ANY] * len(out_rows),
        scratch_shapes=[
            pltpu.VMEM((groups, rows, packed), BF16),
            pltpu.VMEM((width, 2 * units), BF16),
            pltpu.VMEM((units, width), BF16),
            pltpu.VMEM((all_slots, width), BF16),
            pltpu.VMEM((all_slots, META), F32),
            pltpu.VMEM((groups, rows, META), BF16),
            pltpu.VMEM((all_slots, units), BF16),
            pltpu.VMEM((all_slots, width), BF16),
            pltpu.SemaphoreType.DMA((groups, max(len(s) for s in sources))),
            pltpu.SemaphoreType.DMA((2 * units // 256 + 1,)),
            pltpu.SemaphoreType.DMA((groups, max(len(t) for t in targets))),
        ],
        compiler_params=pltpu.CompilerParams(vmem_limit_bytes=VMEM_LIMIT),
        cost_estimate=pl.CostEstimate(
            flops=6 * all_slots * width * units + 4 * all_slots * rows * width,
            bytes_accessed=4 * total * width + 6 * units * width,
            transcendentals=all_slots * units,
        ),
        name="experts",
    )(*arrays, w_gate_up, w_down)


def value_kernel(key_rows, blocks, small_blocks, *refs):
    inputs = 1 + max(b[0] for b in blocks)
    smalls = 1 + max(b[0] for b in small_blocks)
    x_hbm = refs[:inputs]
    small_hbm = refs[inputs : inputs + smalls]
    key_ref, value_ref, x_buf, weight, sems = refs[inputs + smalls :]
    width = x_buf.shape[1]
    weight_rows = width // len(small_blocks)
    copies = []
    for number, (operand, first, device) in enumerate(blocks):
        copies.append(
            pltpu.make_async_copy(
                x_hbm[operand].at[pl.ds(first, key_rows), pl.ds(0, width)],
                x_buf.at[pl.ds(device() * key_rows, key_rows)],
                sems.at[0, number],
            )
        )
    for number, (operand, first, device) in enumerate(small_blocks):
        place = device()
        copies.append(
            pltpu.make_async_copy(
                small_hbm[operand].at[pl.ds(first, key_rows)],
                key_ref.at[pl.ds(place * key_rows, key_rows)],
                sems.at[1, number],
            )
        )
        copies.append(
            pltpu.make_async_copy(
                small_hbm[operand].at[pl.ds(first + key_rows, weight_rows)],
                weight.at[pl.ds(place * weight_rows, weight_rows)],
                sems.at[2, number],
            )
        )
    for copy in copies:
        copy.start()
    for copy in copies:
        copy.wait()
    value_ref[...] = dot(x_buf[...], weight[...]).astype(BF16)


def make_values(arrays, blocks, smalls, small_blocks, key_rows, width):
    kv_width = smalls[0].shape[1]
    total = key_rows * len(blocks)
    kv = jax.ShapeDtypeStruct((total, kv_width), BF16)
    return pl.pallas_call(
        functools.partial(value_kernel, key_rows, blocks, small_blocks),
        out_shape=[kv, kv],
        in_specs=[ANY] * (len(arrays) + len(smalls)),
        out_specs=[IN_VMEM] * 2,
        scratch_shapes=[
            pltpu.VMEM((total, width), BF16),
            pltpu.VMEM((width, kv_width), BF16),
            pltpu.SemaphoreType.DMA((3, len(blocks))),
        ],
        compiler_params=pltpu.CompilerParams(vmem_limit_bytes=VMEM_LIMIT),
        cost_estimate=pl.CostEstimate(
            flops=2 * total * width * kv_width,
            bytes_accessed=2 * total * width + 2 * width * kv_width,
            transcendentals=0,
        ),
        name="values",
    )(*arrays, *smalls)


def attention_kernel(chunk, q_ref, k_ref, v_ref, *refs):
    out_ref = refs[-1]
    q_rows, q_width = q_ref.shape
    heads = q_width // HEAD_DIMENSION
    together = 4
    q_start = lax.axis_index("seq") * q_rows
    factor = math.log2(math.e) / math.sqrt(HEAD_DIMENSION)
    steps = k_ref.shape[0] // chunk
    tall = together * q_rows

    def scored(rows, start):
        scores = lax.dot_general(
            rows, k_ref[pl.ds(start, chunk)], (((1,), (1,)), ((), ())), preferred_element_type=F32
        )
        q_at = q_start + lax.broadcasted_iota(jnp.int32, (q_rows, chunk), 0)
        k_at = start + lax.broadcasted_iota(jnp.int32, (q_rows, chunk), 1)
        bias = jnp.where(q_at >= k_at, 0.0, -1e30)[None]
        return (scores.reshape(together, q_rows, chunk) + bias).reshape(tall, chunk)

    for at in range(0, heads, together):
        rows = jnp.concatenate(
            [
                q_ref[:, h * HEAD_DIMENSION : (h + 1) * HEAD_DIMENSION]
                for h in range(at, at + together)
            ],
            axis=0,
        )

        def one(step, state):
            top_score, run_sum, run_acc = state
            start = pl.multiple_of(step * chunk, chunk)
            scores = scored(rows, start)
            best = jnp.maximum(jnp.max(scores, axis=1, keepdims=True), top_score)
            rescale = jnp.exp2((top_score - best) * factor)
            weights = jnp.exp2((scores - best) * factor)
            total = run_sum * rescale + jnp.sum(weights, axis=1, keepdims=True)
            added = dot(weights.astype(BF16), v_ref[pl.ds(start, chunk)])
            return (best, total, run_acc * rescale + added)

        if steps == 1:
            scores = scored(rows, 0)
            best = jnp.max(scores, axis=1, keepdims=True)
            weights = jnp.exp2((scores - best) * factor)
            total = jnp.sum(weights, axis=1, keepdims=True)
            added = dot(weights.astype(BF16), v_ref[...])
        else:
            best, total, added = lax.fori_loop(
                0,
                (q_start + q_rows + chunk - 1) // chunk,
                one,
                (
                    jnp.full((tall, 1), -1e30, F32),
                    jnp.zeros((tall, 1), F32),
                    jnp.zeros((tall, HEAD_DIMENSION), F32),
                ),
            )
        context = (added / total).astype(BF16)
        for h in range(together):
            out_ref[:, (at + h) * HEAD_DIMENSION : (at + h + 1) * HEAD_DIMENSION] = context[
                h * q_rows : (h + 1) * q_rows
            ]


def attend_all(queries, keys, values, parts):
    q_rows, q_width = queries.shape
    total = keys.shape[0]
    part_width = q_width // parts
    per_kv = parts // KEY_VALUE_HEADS
    chunk = math.gcd(total, 1024)
    context = ()
    for part in range(parts):
        context = (
            pl.pallas_call(
                functools.partial(attention_kernel, chunk),
                grid=(1,),
                out_shape=jax.ShapeDtypeStruct((q_rows, q_width), BF16),
                in_specs=[
                    pl.BlockSpec((q_rows, part_width), lambda i, part=part: (0, part)),
                    pl.BlockSpec((total, HEAD_DIMENSION), lambda i, part=part: (0, part // per_kv)),
                    pl.BlockSpec((total, HEAD_DIMENSION), lambda i, part=part: (0, part // per_kv)),
                    *[ANY for _ in context],
                ],
                out_specs=pl.BlockSpec((q_rows, part_width), lambda i, part=part: (0, part)),
                input_output_aliases={3: 0} if context else {},
                compiler_params=pltpu.CompilerParams(vmem_limit_bytes=VMEM_LIMIT),
                cost_estimate=pl.CostEstimate(
                    flops=4 * q_rows * part_width * total,
                    bytes_accessed=4 * total * HEAD_DIMENSION + 4 * q_rows * part_width,
                    transcendentals=part_width // HEAD_DIMENSION * q_rows * total,
                ),
                name="attention",
            )(queries, keys, values, *context),
        )
    return context[0]


def summed(*terms):
    return sum(term.astype(F32) for term in terms).astype(BF16)


def on_line(acts, packed, keys, value_weight, queries, w_gate_up, w_down, top, capacity):
    rows, width = acts.shape
    pair = jnp.concatenate([keys, value_weight], axis=0)
    small_rows = pair.shape[0]
    pair = jnp.concatenate([pair, across(pair)], axis=0)
    small = [pair]
    for _ in range(LINE - 1):
        small.append(along_ring(small[-1]))
    own_core = jnp.concatenate(small, axis=0)
    small = [own_core, other_core(own_core)]
    small_blocks = [
        (core, (step * 2 + y) * small_rows, functools.partial(from_device, step, y, core))
        for core in range(2)
        for step in range(LINE)
        for y in range(2)
    ]
    arrays, blocks, sources, targets = [], [], [], []
    moving = packed
    for step in range(LINE):
        if step > 0:
            moving = along_ring(moving)
        crossed = across(moving)
        arrays += [moving, crossed, other_core(moving), other_core(crossed)]
        sources.append([(4 * step + i, 0, rows) for i in range(4)])
        targets.append([(2 * step + i, 0, 2 * rows) for i in range(2)])
        blocks += [
            (4 * step + core * 2 + y, 0, functools.partial(from_device, step, y, core))
            for core in range(2)
            for y in range(2)
        ]
    partial = run_experts(
        arrays, sources, targets, [2 * rows] * (2 * LINE), w_gate_up, w_down, top, rows, capacity
    )
    new_keys, values = make_values(arrays, blocks, small, small_blocks, rows, width)
    context = attend_all(queries, new_keys, values, 4)
    moving = None
    for step in (1, 2, 3, 0):
        keep, send = partial[2 * step], partial[2 * step + 1]
        came = other_core(send)
        mine = summed(keep[:rows], came[:rows])
        theirs = across(summed(keep[rows:], came[rows:]))
        if step == 0:
            break
        total = summed(mine, theirs) if moving is None else summed(mine, theirs, moving)
        moving = along_ring(total)
    layer_out = summed(acts, mine, theirs, moving)
    return context, layer_out


def on_any(acts, packed, keys, value_weight, queries, w_gate_up, w_down, top, capacity):
    rows, width = acts.shape
    gathered = lax.all_gather(packed, "seq", axis=0, tiled=True)
    all_keys = lax.all_gather(keys, "seq", axis=0, tiled=True)
    weight = lax.all_gather(value_weight, "seq", axis=0, tiled=True)
    total = gathered.shape[0]
    part = total // GROUPS
    pieces = [[(0, group * part, part)] for group in range(GROUPS)]
    (partial,) = run_experts(
        [gathered], pieces, pieces, [total], w_gate_up, w_down, top, rows, capacity
    )
    values = dot(gathered[:, :width], weight).astype(BF16)
    context = attend_all(queries, all_keys, values, KEY_VALUE_HEADS)
    combined = lax.psum_scatter(partial, "seq", scatter_dimension=0, tiled=True)
    return context, summed(acts, combined)


def per_device(
    activations, queries, keys, norm_gain, value_weight, expert_ids, gate_weights, w_gate_up, w_down
):
    pos_rows, sequence_count, model_width = activations.shape
    assert sequence_count == 1 and w_down.shape[0] == 1
    top = expert_ids.shape[2]
    devices = lax.axis_size("seq")
    capacity = max(2, 3 * pos_rows * top // (2 * devices))
    acts = activations.reshape(pos_rows, model_width)
    packed = pack(
        acts,
        norm_gain,
        expert_ids.transpose(1, 2, 0).reshape(top, pos_rows),
        gate_weights.transpose(1, 2, 0).reshape(top, pos_rows),
    )
    way = on_line if devices == 4 * LINE else on_any
    context, layer_out = way(
        acts,
        packed,
        keys.reshape(pos_rows, -1),
        value_weight,
        queries.reshape(pos_rows, -1),
        w_gate_up[0],
        w_down[0],
        top,
        capacity,
    )
    return (context.reshape(queries.shape), layer_out.reshape(activations.shape))


def solution(mesh):
    placed = (
        P("seq", "grp", None),
        P("seq", "grp", None),
        P("seq", "grp", None),
        P(),
        P("seq", None),
        P("seq", "grp", None),
        P("seq", "grp", None),
        P("seq", None, None),
        P("seq", None, None),
    )
    return jax.shard_map(
        per_device,
        mesh=mesh,
        in_specs=placed,
        out_specs=(P("seq", "grp", None), P("seq", "grp", None)),
        check_vma=False,
    )
```

```python
import functools
import math

import jax
import jax.numpy as jnp
from jax import lax
from jax.experimental import pallas as pl
from jax.experimental.pallas import tpu as pltpu
from jax.sharding import PartitionSpec as P

QUERY_HEADS = 32
KEY_VALUE_HEADS = 2
HEAD_DIMENSION = 128
GROUPS = 4
META = 128
LINE = 4
VMEM_LIMIT = 60 * 2**20
F32 = jnp.float32
BF16 = jnp.bfloat16
ANY = pl.BlockSpec(memory_space=pl.ANY)
IN_VMEM = pl.BlockSpec(memory_space=pltpu.VMEM)


def dot(a, b):
    return jnp.dot(a, b, preferred_element_type=F32)


RING = (0, 1, 3, 2)


def device_index(place, y, core):
    return (RING[place % LINE] * 2 + y) * 2 + core


def swaps(flip_y, flip_core):
    return [
        (device_index(p, y, c), device_index(p, y ^ flip_y, c ^ flip_core))
        for p in range(LINE)
        for y in range(2)
        for c in range(2)
    ]


def ring_step():
    return [
        (device_index(p, y, c), device_index(p + 1, y, c))
        for p in range(LINE)
        for y in range(2)
        for c in range(2)
    ]


def along_ring(x):
    return lax.ppermute(x, "seq", ring_step())


def across(x):
    return lax.ppermute(x, "seq", swaps(1, 0))


def other_core(x):
    return lax.ppermute(x, "seq", swaps(0, 1))


def from_device(steps, flip_y, flip_core):
    me = lax.axis_index("seq")
    core, y, line = me % 2, me // 2 % 2, me // 4
    place = sum(jnp.where(line == RING[p], p, 0) for p in range(LINE))
    place = (place + LINE - steps) % LINE
    line = sum(jnp.where(place == p, RING[p], 0) for p in range(LINE))
    y = 1 - y if flip_y else y
    core = 1 - core if flip_core else core
    return (line * 2 + y) * 2 + core


def pack_kernel(
    act_ref, gain_ref, ids_ref, gates_ref, key_ref, weight_ref, out_ref, small_ref, meta_ref
):
    width = act_ref.shape[1]
    rows = act_ref.shape[0]
    top = ids_ref.shape[0]
    features = act_ref[...].astype(F32)
    inverse = lax.rsqrt(jnp.mean(features * features, axis=-1, keepdims=True) + 1e-06)
    out_ref[:, :width] = (features * inverse * gain_ref[...]).astype(BF16)
    gates = gates_ref[...]
    high = gates.astype(BF16).astype(F32)
    rest = gates - high
    middle = rest.astype(BF16).astype(F32)
    meta_ref[...] = jnp.zeros_like(meta_ref)
    meta_ref[0:top, 0:rows] = ids_ref[...].astype(F32)
    meta_ref[8 : 8 + top, 0:rows] = high
    meta_ref[16 : 16 + top, 0:rows] = middle
    meta_ref[24 : 24 + top, 0:rows] = rest - middle
    out_ref[:, width:] = meta_ref[...].T[:rows, :].astype(BF16)
    small_ref[:rows] = key_ref[...]
    small_ref[rows:] = weight_ref[...]


def pack(activations, norm_gain, ids, gates, keys, value_weight):
    rows, width = activations.shape
    small_rows = rows + value_weight.shape[0]
    assert rows <= META and ids.shape[0] <= 8
    return pl.pallas_call(
        pack_kernel,
        out_shape=[
            jax.ShapeDtypeStruct((rows, width + META), BF16),
            jax.ShapeDtypeStruct((small_rows, keys.shape[1]), BF16),
        ],
        scratch_shapes=[pltpu.VMEM((META, META), F32)],
        cost_estimate=pl.CostEstimate(
            flops=4 * rows * width, bytes_accessed=4 * rows * width, transcendentals=0
        ),
        name="normalize_and_pack",
    )(activations, norm_gain.reshape(1, width), ids, gates, keys, value_weight)


def expert_kernel(top, tok_rows, capacity, sources, targets, *refs):
    inputs = 1 + max(s[0] for group in sources for s in group)
    outputs = 1 + max(t[0] for group in targets for t in group)
    x_hbm = refs[:inputs]
    up_hbm, down_hbm = refs[inputs : inputs + 2]
    out_hbm = refs[inputs + 2 : inputs + 2 + outputs]
    (
        x_buf,
        up_buf,
        down_buf,
        slot_rows,
        slot_gates,
        places,
        hidden,
        result,
        x_sem,
        w_sem,
        out_sem,
    ) = refs[inputs + 2 + outputs :]
    groups, rows, packed = x_buf.shape
    width = packed - META
    slots = slot_rows.shape[0] // groups
    units = down_buf.shape[0]
    tile = 256
    me = lax.axis_index("seq").astype(F32)

    def loads(group):
        copies, at = [], 0
        for number, (operand, first, count) in enumerate(sources[group]):
            copies.append(
                pltpu.make_async_copy(
                    x_hbm[operand].at[pl.ds(first, count)],
                    x_buf.at[group, pl.ds(at, count)],
                    x_sem.at[group, number],
                )
            )
            at += count
        return copies

    def stores(group):
        copies, at = [], 0
        for number, (operand, first, count) in enumerate(targets[group]):
            copies.append(
                pltpu.make_async_copy(
                    x_buf.at[group, pl.ds(at, count), pl.ds(0, width)],
                    out_hbm[operand].at[pl.ds(first, count)],
                    out_sem.at[group, number],
                )
            )
            at += count
        return copies

    def load_up(index):
        part = pl.ds(index * tile, tile)
        return pltpu.make_async_copy(up_hbm.at[:, part], up_buf.at[:, part], w_sem.at[index])

    up_parts = 2 * units // tile
    load_down = pltpu.make_async_copy(down_hbm, down_buf, w_sem.at[up_parts])
    half = up_parts // 2
    for group in range(groups):
        for copy in loads(group):
            copy.start()
    for index in range(half):
        load_up(index).start()
        load_up(half + index).start()
    load_down.start()

    chunk = tok_rows * META // math.gcd(tok_rows, META)
    first = lax.broadcasted_iota(jnp.int32, (chunk, chunk), 0)
    second = lax.broadcasted_iota(jnp.int32, (chunk, chunk), 1)
    earlier = ((first < second) & (first // tok_rows == second // tok_rows)).astype(F32).astype(BF16)
    block = lax.broadcasted_iota(jnp.int32, (1, rows), 1) // tok_rows
    for group in range(groups):
        for copy in loads(group):
            copy.wait()
        meta = x_buf[group, :, width:].astype(F32).T
        gate = jnp.zeros((1, rows), F32)
        named = jnp.zeros((1, rows), F32)
        for k in range(top):
            match = meta[k : k + 1] == me
            value = meta[8 + k : 9 + k] + (meta[16 + k : 17 + k] + meta[24 + k : 25 + k])
            gate = jnp.where(match, value, gate)
            named = jnp.where(match, 1.0, named)
        marks = jnp.broadcast_to(named, (8, rows)).astype(BF16)
        rank = jnp.concatenate(
            [dot(marks[:, at : at + chunk], earlier) for at in range(0, rows, chunk)], axis=1
        )[0:1]
        slot = jnp.where(named > 0.0, (block * capacity).astype(F32) + rank, -1.0)
        spots = lax.broadcasted_iota(jnp.int32, (slots, rows), 0).astype(F32)
        chosen = spots == slot
        slot_gates[pl.ds(group * slots, slots)] = jnp.broadcast_to(
            jnp.sum(jnp.where(chosen, gate, 0.0), axis=1, keepdims=True), (slots, META)
        )
        pick = chosen.astype(F32).astype(BF16)
        for at in range(0, width, 512):
            slot_rows[pl.ds(group * slots, slots), at : at + 512] = dot(
                pick, x_buf[group, :, at : at + 512]
            ).astype(BF16)
        by_row = jnp.broadcast_to(slot, (META, rows)).T
        spots = lax.broadcasted_iota(jnp.int32, (rows, META), 1).astype(F32)
        places[group] = (spots == by_row).astype(F32).astype(BF16)

    for index in range(half):
        load_up(index).wait()
        load_up(half + index).wait()
        gate = dot(slot_rows[...], up_buf[:, index * tile : (index + 1) * tile])
        up = dot(slot_rows[...], up_buf[:, units + index * tile : units + (index + 1) * tile])
        hidden[:, index * tile : (index + 1) * tile] = (gate / (1.0 + jnp.exp(-gate)) * up).astype(
            BF16
        )
    load_down.wait()
    for at in range(0, width, 256):
        out = dot(hidden[...], down_buf[:, at : at + 256]).astype(BF16).astype(F32)
        result[:, at : at + 256] = (out * slot_gates[:, 0:1]).astype(BF16)
    for group in range(groups):
        for at in range(0, width, 512):
            x_buf[group, :, at : at + 512] = dot(
                places[group, :, :slots], result[pl.ds(group * slots, slots), at : at + 512]
            ).astype(BF16)
        for copy in stores(group):
            copy.start()
    for group in range(groups):
        for copy in stores(group):
            copy.wait()


def run_experts(arrays, sources, targets, out_rows, w_gate_up, w_down, top, tok_rows, capacity):
    groups = len(sources)
    rows = sum(count for _, _, count in sources[0])
    packed = arrays[0].shape[1]
    total = groups * rows
    width = packed - META
    units = w_down.shape[0]
    slots = rows // tok_rows * capacity
    assert slots % 16 == 0 and slots <= META and units % 256 == 0 and width % 512 == 0
    all_slots = groups * slots
    return pl.pallas_call(
        functools.partial(expert_kernel, top, tok_rows, capacity, sources, targets),
        out_shape=[jax.ShapeDtypeStruct((count, width), BF16) for count in out_rows],
        in_specs=[ANY] * (len(arrays) + 2),
        out_specs=[ANY] * len(out_rows),
        scratch_shapes=[
            pltpu.VMEM((groups, rows, packed), BF16),
            pltpu.VMEM((width, 2 * units), BF16),
            pltpu.VMEM((units, width), BF16),
            pltpu.VMEM((all_slots, width), BF16),
            pltpu.VMEM((all_slots, META), F32),
            pltpu.VMEM((groups, rows, META), BF16),
            pltpu.VMEM((all_slots, units), BF16),
            pltpu.VMEM((all_slots, width), BF16),
            pltpu.SemaphoreType.DMA((groups, max(len(s) for s in sources))),
            pltpu.SemaphoreType.DMA((2 * units // 256 + 1,)),
            pltpu.SemaphoreType.DMA((groups, max(len(t) for t in targets))),
        ],
        compiler_params=pltpu.CompilerParams(vmem_limit_bytes=VMEM_LIMIT),
        cost_estimate=pl.CostEstimate(
            flops=6 * all_slots * width * units + 4 * all_slots * rows * width,
            bytes_accessed=4 * total * width + 6 * units * width,
            transcendentals=all_slots * units,
        ),
        name="experts",
    )(*arrays, w_gate_up, w_down)


def value_kernel(key_rows, blocks, small_blocks, *refs):
    inputs = 1 + max(b[0] for b in blocks)
    smalls = 1 + max(b[0] for b in small_blocks)
    x_hbm = refs[:inputs]
    small_hbm = refs[inputs : inputs + smalls]
    key_ref, value_ref, x_buf, weight, sems = refs[inputs + smalls :]
    width = x_buf.shape[1]
    weight_rows = width // len(small_blocks)
    copies = []
    for number, (operand, first, device) in enumerate(blocks):
        copies.append(
            pltpu.make_async_copy(
                x_hbm[operand].at[pl.ds(first, key_rows), pl.ds(0, width)],
                x_buf.at[pl.ds(device() * key_rows, key_rows)],
                sems.at[0, number],
            )
        )
    for number, (operand, first, device) in enumerate(small_blocks):
        place = device()
        copies.append(
            pltpu.make_async_copy(
                small_hbm[operand].at[pl.ds(first, key_rows)],
                key_ref.at[pl.ds(place * key_rows, key_rows)],
                sems.at[1, number],
            )
        )
        copies.append(
            pltpu.make_async_copy(
                small_hbm[operand].at[pl.ds(first + key_rows, weight_rows)],
                weight.at[pl.ds(place * weight_rows, weight_rows)],
                sems.at[2, number],
            )
        )
    for copy in copies:
        copy.start()
    for copy in copies:
        copy.wait()
    value_ref[...] = dot(x_buf[...], weight[...]).astype(BF16)


def make_values(arrays, blocks, smalls, small_blocks, key_rows, width, earlier):
    smalls = [after(smalls[0], earlier), *smalls[1:]]
    kv_width = smalls[0].shape[1]
    total = key_rows * len(blocks)
    kv = jax.ShapeDtypeStruct((total, kv_width), BF16)
    return pl.pallas_call(
        functools.partial(value_kernel, key_rows, blocks, small_blocks),
        out_shape=[kv, kv],
        in_specs=[ANY] * (len(arrays) + len(smalls)),
        out_specs=[IN_VMEM] * 2,
        scratch_shapes=[
            pltpu.VMEM((total, width), BF16),
            pltpu.VMEM((width, kv_width), BF16),
            pltpu.SemaphoreType.DMA((3, len(blocks))),
        ],
        compiler_params=pltpu.CompilerParams(vmem_limit_bytes=VMEM_LIMIT),
        cost_estimate=pl.CostEstimate(
            flops=2 * total * width * kv_width,
            bytes_accessed=2 * total * width + 2 * width * kv_width,
            transcendentals=0,
        ),
        name="values",
    )(*arrays, *smalls)


def attention_kernel(chunk, q_ref, k_ref, v_ref, *refs):
    out_ref = refs[-1]
    q_rows, q_width = q_ref.shape
    heads = q_width // HEAD_DIMENSION
    together = 4
    q_start = lax.axis_index("seq") * q_rows
    factor = math.log2(math.e) / math.sqrt(HEAD_DIMENSION)
    steps = k_ref.shape[0] // chunk
    tall = together * q_rows

    def scored(rows, start):
        scores = lax.dot_general(
            rows, k_ref[pl.ds(start, chunk)], (((1,), (1,)), ((), ())), preferred_element_type=F32
        )
        q_at = q_start + lax.broadcasted_iota(jnp.int32, (q_rows, chunk), 0)
        k_at = start + lax.broadcasted_iota(jnp.int32, (q_rows, chunk), 1)
        bias = jnp.where(q_at >= k_at, 0.0, -1e30)[None]
        return (scores.reshape(together, q_rows, chunk) + bias).reshape(tall, chunk)

    for at in range(0, heads, together):
        rows = jnp.concatenate(
            [
                q_ref[:, h * HEAD_DIMENSION : (h + 1) * HEAD_DIMENSION]
                for h in range(at, at + together)
            ],
            axis=0,
        )

        def one(step, state):
            top_score, run_sum, run_acc = state
            start = pl.multiple_of(step * chunk, chunk)
            scores = scored(rows, start)
            best = jnp.maximum(jnp.max(scores, axis=1, keepdims=True), top_score)
            rescale = jnp.exp2((top_score - best) * factor)
            weights = jnp.exp2((scores - best) * factor)
            total = run_sum * rescale + jnp.sum(weights, axis=1, keepdims=True)
            added = dot(weights.astype(BF16), v_ref[pl.ds(start, chunk)])
            return (best, total, run_acc * rescale + added)

        if steps == 1:
            scores = scored(rows, 0)
            best = jnp.max(scores, axis=1, keepdims=True)
            weights = jnp.exp2((scores - best) * factor)
            total = jnp.sum(weights, axis=1, keepdims=True)
            added = dot(weights.astype(BF16), v_ref[...])
        else:
            best, total, added = lax.fori_loop(
                0,
                (q_start + q_rows + chunk - 1) // chunk,
                one,
                (
                    jnp.full((tall, 1), -1e30, F32),
                    jnp.zeros((tall, 1), F32),
                    jnp.zeros((tall, HEAD_DIMENSION), F32),
                ),
            )
        context = (added / total).astype(BF16)
        for h in range(together):
            out_ref[:, (at + h) * HEAD_DIMENSION : (at + h + 1) * HEAD_DIMENSION] = context[
                h * q_rows : (h + 1) * q_rows
            ]


def attend_part(queries, keys, values, part, parts, context=None):
    q_rows, q_width = queries.shape
    total = keys.shape[0]
    part_width = q_width // parts
    per_kv = parts // KEY_VALUE_HEADS
    chunk = math.gcd(total, 1024)
    before = () if context is None else (context,)
    return pl.pallas_call(
        functools.partial(attention_kernel, chunk),
        grid=(1,),
        out_shape=jax.ShapeDtypeStruct((q_rows, q_width), BF16),
        in_specs=[
            pl.BlockSpec((q_rows, part_width), lambda i: (0, part)),
            pl.BlockSpec((total, HEAD_DIMENSION), lambda i: (0, part // per_kv)),
            pl.BlockSpec((total, HEAD_DIMENSION), lambda i: (0, part // per_kv)),
            *[ANY for _ in before],
        ],
        out_specs=pl.BlockSpec((q_rows, part_width), lambda i: (0, part)),
        input_output_aliases={3: 0} if before else {},
        compiler_params=pltpu.CompilerParams(vmem_limit_bytes=VMEM_LIMIT),
        cost_estimate=pl.CostEstimate(
            flops=4 * q_rows * part_width * total,
            bytes_accessed=4 * total * HEAD_DIMENSION + 4 * q_rows * part_width,
            transcendentals=part_width // HEAD_DIMENSION * q_rows * total,
        ),
        name="attention",
    )(queries, keys, values, *before)


def summed(*terms):
    return sum(term.astype(F32) for term in terms).astype(BF16)


def after(x, *others):
    return lax.optimization_barrier((x, *others))[0]


def on_line(acts, packed, small, queries, w_gate_up, w_down, top, capacity):
    rows, width = acts.shape
    arrays, blocks, sources = [], [], []
    moving = packed
    pair = jnp.concatenate([small, across(small)], axis=0)
    for step in range(LINE):
        if step == 1:
            moving = along_ring(moving)
        elif step == 2:
            moving = along_ring(after(moving, pair, arrays[1]))
        elif step > 2:
            moving = along_ring(after(moving, arrays[4 * step - 7], *arrays[4 * step - 10 : 4 * step - 8]))
        crossed = across(moving)
        arrays += [moving, crossed, other_core(moving), other_core(crossed)]
        sources.append([(4 * step + i, 0, rows) for i in range(4)])
        blocks += [
            (4 * step + core * 2 + y, 0, functools.partial(from_device, step, y, core))
            for core in range(2)
            for y in range(2)
        ]
    small_rows = small.shape[0]
    pair = after(pair, moving, arrays[-7], *arrays[-10:-8])
    smalls, small_blocks = [], []
    for step in range(LINE):
        if step > 0:
            pair = along_ring(pair if step != 2 else after(pair, *arrays[-6:-4]))
        if step == LINE - 2:
            arrays[0] = after(arrays[0], pair)
        smalls += [pair, other_core(pair)]
        small_blocks += [
            (2 * step + core, y * small_rows, functools.partial(from_device, step, y, core))
            for core in range(2)
            for y in range(2)
        ]
    targets = [
        [(0, 0, 2 * rows), (5, 4 * rows, 2 * rows)],
        [(1, 0, 2 * rows), (4, 0, 2 * rows)],
        [(2, 0, 2 * rows), (5, 0, 2 * rows)],
        [(3, 0, 2 * rows), (5, 2 * rows, 2 * rows)],
    ]
    out_rows = [2 * rows] * 5 + [6 * rows]
    *keep, send_first, send_rest = run_experts(
        arrays, sources, targets, out_rows, w_gate_up, w_down, top, rows, capacity
    )
    came_first = other_core(send_first)
    came_rest = other_core(after(send_rest, came_first))
    came = [came_rest[4 * rows :], came_first, came_rest[: 2 * rows], came_rest[2 * rows : 4 * rows]]
    crossing = [summed(keep[step][rows:], came[step][rows:]) for step in range(LINE)]
    theirs = [across(crossing[step]) for step in (1, 2, 3, 0)]
    theirs = [theirs[3], *theirs[:3]]
    new_keys, values = make_values(
        arrays, blocks, smalls, small_blocks, rows, width, crossing[0]
    )
    total = summed(keep[1][:rows], came[1][:rows], after(theirs[1], values))
    moving = along_ring(total)
    context = attend_part(after(queries, total), new_keys, values, 0, 4)
    context = attend_part(queries, new_keys, values, 1, 4, context)
    total = summed(keep[2][:rows], came[2][:rows], theirs[2], after(moving, context))
    moving = along_ring(total)
    context = attend_part(after(queries, total), new_keys, values, 2, 4, context)
    total = summed(keep[3][:rows], came[3][:rows], theirs[3], after(moving, context))
    moving = along_ring(total)
    context = attend_part(after(queries, total), new_keys, values, 3, 4, context)
    layer_out = summed(acts, keep[0][:rows], came[0][:rows], theirs[0], after(moving, context))
    return context, layer_out


def on_any(acts, packed, small, queries, w_gate_up, w_down, top, capacity):
    rows, width = acts.shape
    keys, value_weight = small[:rows], small[rows:]
    gathered = lax.all_gather(packed, "seq", axis=0, tiled=True)
    all_keys = lax.all_gather(keys, "seq", axis=0, tiled=True)
    weight = lax.all_gather(value_weight, "seq", axis=0, tiled=True)
    total = gathered.shape[0]
    part = total // GROUPS
    pieces = [[(0, group * part, part)] for group in range(GROUPS)]
    (partial,) = run_experts(
        [gathered], pieces, pieces, [total], w_gate_up, w_down, top, rows, capacity
    )
    values = dot(gathered[:, :width], weight).astype(BF16)
    context = None
    for part in range(KEY_VALUE_HEADS):
        context = attend_part(queries, all_keys, values, part, KEY_VALUE_HEADS, context)
    combined = lax.psum_scatter(partial, "seq", scatter_dimension=0, tiled=True)
    return context, summed(acts, combined)


def per_device(
    activations, queries, keys, norm_gain, value_weight, expert_ids, gate_weights, w_gate_up, w_down
):
    pos_rows, sequence_count, model_width = activations.shape
    assert sequence_count == 1 and w_down.shape[0] == 1
    top = expert_ids.shape[2]
    devices = lax.axis_size("seq")
    capacity = max(2, 3 * pos_rows * top // (2 * devices))
    acts = activations.reshape(pos_rows, model_width)
    packed, small = pack(
        acts,
        norm_gain,
        expert_ids.transpose(1, 2, 0).reshape(top, pos_rows),
        gate_weights.transpose(1, 2, 0).reshape(top, pos_rows),
        keys.reshape(pos_rows, -1),
        value_weight,
    )
    way = on_line if devices == 4 * LINE else on_any
    context, layer_out = way(
        acts,
        packed,
        small,
        queries.reshape(pos_rows, -1),
        w_gate_up[0],
        w_down[0],
        top,
        capacity,
    )
    return (context.reshape(queries.shape), layer_out.reshape(activations.shape))


def solution(mesh):
    placed = (
        P("seq", "grp", None),
        P("seq", "grp", None),
        P("seq", "grp", None),
        P(),
        P("seq", None),
        P("seq", "grp", None),
        P("seq", "grp", None),
        P("seq", None, None),
        P("seq", None, None),
    )
    return jax.shard_map(
        per_device,
        mesh=mesh,
        in_specs=placed,
        out_specs=(P("seq", "grp", None), P("seq", "grp", None)),
        check_vma=False,
    )
```

```python
import functools
import math

import jax
import jax.numpy as jnp
from jax import lax
from jax.experimental import pallas as pl
from jax.experimental.pallas import tpu as pltpu
from jax.sharding import PartitionSpec as P

QUERY_HEADS = 32
KEY_VALUE_HEADS = 2
HEAD_DIMENSION = 128
GROUPS = 4
META = 128
LINE = 4
VMEM_LIMIT = 60 * 2**20
F32 = jnp.float32
BF16 = jnp.bfloat16
ANY = pl.BlockSpec(memory_space=pl.ANY)
SHORT = pl.CostEstimate(flops=1, bytes_accessed=1, transcendentals=0)
IN_VMEM = pl.BlockSpec(memory_space=pltpu.VMEM)


def dot(a, b):
    return jnp.dot(a, b, preferred_element_type=F32)


RING = (0, 1, 3, 2)


def device_index(place, y, core):
    return (RING[place % LINE] * 2 + y) * 2 + core


def swaps(flip_y, flip_core):
    return [
        (device_index(p, y, c), device_index(p, y ^ flip_y, c ^ flip_core))
        for p in range(LINE)
        for y in range(2)
        for c in range(2)
    ]


def ring_steps(steps):
    return [
        (device_index(p, y, c), device_index(p + steps, y, c))
        for p in range(LINE)
        for y in range(2)
        for c in range(2)
    ]


def forward(x):
    return lax.ppermute(x, "seq", ring_steps(1))


def backward(x):
    return lax.ppermute(x, "seq", ring_steps(LINE - 1))


def across(x):
    return lax.ppermute(x, "seq", swaps(1, 0))


def other_core(x):
    return lax.ppermute(x, "seq", swaps(0, 1))


def from_device(steps, flip_y, flip_core):
    me = lax.axis_index("seq")
    core, y, line = me % 2, me // 2 % 2, me // 4
    place = sum(jnp.where(line == RING[p], p, 0) for p in range(LINE))
    place = (place + LINE - steps) % LINE
    line = sum(jnp.where(place == p, RING[p], 0) for p in range(LINE))
    y = 1 - y if flip_y else y
    core = 1 - core if flip_core else core
    return (line * 2 + y) * 2 + core


def pack_kernel(
    act_ref, gain_ref, ids_ref, gates_ref, key_ref, weight_ref, out_ref, small_ref, meta_ref
):
    width = act_ref.shape[1]
    rows = act_ref.shape[0]
    top = ids_ref.shape[0]
    features = act_ref[...].astype(F32)
    inverse = lax.rsqrt(jnp.mean(features * features, axis=-1, keepdims=True) + 1e-06)
    out_ref[:, :width] = (features * inverse * gain_ref[...]).astype(BF16)
    gates = gates_ref[...]
    high = gates.astype(BF16).astype(F32)
    rest = gates - high
    middle = rest.astype(BF16).astype(F32)
    meta_ref[...] = jnp.zeros_like(meta_ref)
    meta_ref[0:top, 0:rows] = ids_ref[...].astype(F32)
    meta_ref[8 : 8 + top, 0:rows] = high
    meta_ref[16 : 16 + top, 0:rows] = middle
    meta_ref[24 : 24 + top, 0:rows] = rest - middle
    out_ref[:, width:] = meta_ref[...].T[:rows, :].astype(BF16)
    small_ref[:rows] = key_ref[...]
    small_ref[rows:] = weight_ref[...]


def pack(activations, norm_gain, ids, gates, keys, value_weight):
    rows, width = activations.shape
    small_rows = rows + value_weight.shape[0]
    assert rows <= META and ids.shape[0] <= 8
    return pl.pallas_call(
        pack_kernel,
        out_shape=[
            jax.ShapeDtypeStruct((rows, width + META), BF16),
            jax.ShapeDtypeStruct((small_rows, keys.shape[1]), BF16),
        ],
        scratch_shapes=[pltpu.VMEM((META, META), F32)],
        cost_estimate=SHORT,
        name="normalize_and_pack",
    )(activations, norm_gain.reshape(1, width), ids, gates, keys, value_weight)


def expert_kernel(top, tok_rows, capacity, sources, targets, *refs):
    inputs = 1 + max(s[0] for group in sources for s in group)
    outputs = 1 + max(t[0] for group in targets for t in group)
    x_hbm = refs[:inputs]
    up_hbm, down_hbm = refs[inputs : inputs + 2]
    out_hbm = refs[inputs + 2 : inputs + 2 + outputs]
    (
        x_buf,
        up_buf,
        down_buf,
        slot_rows,
        slot_gates,
        places,
        hidden,
        result,
        x_sem,
        w_sem,
        out_sem,
    ) = refs[inputs + 2 + outputs :]
    groups, rows, packed = x_buf.shape
    width = packed - META
    slots = slot_rows.shape[0] // groups
    units = down_buf.shape[0]
    tile = 256
    me = lax.axis_index("seq").astype(F32)

    def loads(group):
        copies, at = [], 0
        for number, (operand, first, count) in enumerate(sources[group]):
            copies.append(
                pltpu.make_async_copy(
                    x_hbm[operand].at[pl.ds(first, count)],
                    x_buf.at[group, pl.ds(at, count)],
                    x_sem.at[group, number],
                )
            )
            at += count
        return copies

    def stores(group):
        copies, at = [], 0
        for number, (operand, first, count) in enumerate(targets[group]):
            copies.append(
                pltpu.make_async_copy(
                    x_buf.at[group, pl.ds(at, count), pl.ds(0, width)],
                    out_hbm[operand].at[pl.ds(first, count)],
                    out_sem.at[group, number],
                )
            )
            at += count
        return copies

    def load_up(index):
        part = pl.ds(index * tile, tile)
        return pltpu.make_async_copy(up_hbm.at[:, part], up_buf.at[:, part], w_sem.at[index])

    up_parts = 2 * units // tile
    load_down = pltpu.make_async_copy(down_hbm, down_buf, w_sem.at[up_parts])
    half = up_parts // 2
    for group in range(groups):
        for copy in loads(group):
            copy.start()
    for index in range(half):
        load_up(index).start()
        load_up(half + index).start()
    load_down.start()

    chunk = tok_rows * META // math.gcd(tok_rows, META)
    first = lax.broadcasted_iota(jnp.int32, (chunk, chunk), 0)
    second = lax.broadcasted_iota(jnp.int32, (chunk, chunk), 1)
    earlier = ((first < second) & (first // tok_rows == second // tok_rows)).astype(F32).astype(BF16)
    block = lax.broadcasted_iota(jnp.int32, (1, rows), 1) // tok_rows
    for group in range(groups):
        for copy in loads(group):
            copy.wait()
        meta = x_buf[group, :, width:].astype(F32).T
        gate = jnp.zeros((1, rows), F32)
        named = jnp.zeros((1, rows), F32)
        for k in range(top):
            match = meta[k : k + 1] == me
            value = meta[8 + k : 9 + k] + (meta[16 + k : 17 + k] + meta[24 + k : 25 + k])
            gate = jnp.where(match, value, gate)
            named = jnp.where(match, 1.0, named)
        marks = jnp.broadcast_to(named, (8, rows)).astype(BF16)
        rank = jnp.concatenate(
            [dot(marks[:, at : at + chunk], earlier) for at in range(0, rows, chunk)], axis=1
        )[0:1]
        slot = jnp.where(named > 0.0, (block * capacity).astype(F32) + rank, -1.0)
        spots = lax.broadcasted_iota(jnp.int32, (slots, rows), 0).astype(F32)
        chosen = spots == slot
        slot_gates[pl.ds(group * slots, slots)] = jnp.broadcast_to(
            jnp.sum(jnp.where(chosen, gate, 0.0), axis=1, keepdims=True), (slots, META)
        )
        pick = chosen.astype(F32).astype(BF16)
        for at in range(0, width, 512):
            slot_rows[pl.ds(group * slots, slots), at : at + 512] = dot(
                pick, x_buf[group, :, at : at + 512]
            ).astype(BF16)
        by_row = jnp.broadcast_to(slot, (META, rows)).T
        spots = lax.broadcasted_iota(jnp.int32, (rows, META), 1).astype(F32)
        places[group] = (spots == by_row).astype(F32).astype(BF16)

    for index in range(half):
        load_up(index).wait()
        load_up(half + index).wait()
        gate = dot(slot_rows[...], up_buf[:, index * tile : (index + 1) * tile])
        up = dot(slot_rows[...], up_buf[:, units + index * tile : units + (index + 1) * tile])
        hidden[:, index * tile : (index + 1) * tile] = (gate / (1.0 + jnp.exp(-gate)) * up).astype(
            BF16
        )
    load_down.wait()
    for at in range(0, width, 256):
        out = dot(hidden[...], down_buf[:, at : at + 256]).astype(BF16).astype(F32)
        result[:, at : at + 256] = (out * slot_gates[:, 0:1]).astype(BF16)
    for group in range(groups):
        for at in range(0, width, 512):
            x_buf[group, :, at : at + 512] = dot(
                places[group, :, :slots], result[pl.ds(group * slots, slots), at : at + 512]
            ).astype(BF16)
        for copy in stores(group):
            copy.start()
    for group in range(groups):
        for copy in stores(group):
            copy.wait()


def run_experts(arrays, sources, targets, out_rows, w_gate_up, w_down, top, tok_rows, capacity):
    groups = len(sources)
    rows = sum(count for _, _, count in sources[0])
    packed = arrays[0].shape[1]
    total = groups * rows
    width = packed - META
    units = w_down.shape[0]
    slots = rows // tok_rows * capacity
    assert slots % 16 == 0 and slots <= META and units % 256 == 0 and width % 512 == 0
    all_slots = groups * slots
    return pl.pallas_call(
        functools.partial(expert_kernel, top, tok_rows, capacity, sources, targets),
        out_shape=[jax.ShapeDtypeStruct((count, width), BF16) for count in out_rows],
        in_specs=[ANY] * (len(arrays) + 2),
        out_specs=[ANY] * len(out_rows),
        scratch_shapes=[
            pltpu.VMEM((groups, rows, packed), BF16),
            pltpu.VMEM((width, 2 * units), BF16),
            pltpu.VMEM((units, width), BF16),
            pltpu.VMEM((all_slots, width), BF16),
            pltpu.VMEM((all_slots, META), F32),
            pltpu.VMEM((groups, rows, META), BF16),
            pltpu.VMEM((all_slots, units), BF16),
            pltpu.VMEM((all_slots, width), BF16),
            pltpu.SemaphoreType.DMA((groups, max(len(s) for s in sources))),
            pltpu.SemaphoreType.DMA((2 * units // 256 + 1,)),
            pltpu.SemaphoreType.DMA((groups, max(len(t) for t in targets))),
        ],
        compiler_params=pltpu.CompilerParams(vmem_limit_bytes=VMEM_LIMIT),
        cost_estimate=SHORT,
        name="experts",
    )(*arrays, w_gate_up, w_down)


def value_kernel(key_rows, blocks, small_blocks, *refs):
    inputs = 1 + max(b[0] for b in blocks)
    smalls = 1 + max(b[0] for b in small_blocks)
    x_hbm = refs[:inputs]
    small_hbm = refs[inputs : inputs + smalls]
    key_ref, value_ref, x_buf, weight, sems = refs[inputs + smalls :]
    width = x_buf.shape[1]
    weight_rows = width // len(small_blocks)
    copies = []
    for number, (operand, first, device) in enumerate(blocks):
        copies.append(
            pltpu.make_async_copy(
                x_hbm[operand].at[pl.ds(first, key_rows), pl.ds(0, width)],
                x_buf.at[pl.ds(device() * key_rows, key_rows)],
                sems.at[0, number],
            )
        )
    for number, (operand, first, device) in enumerate(small_blocks):
        place = device()
        copies.append(
            pltpu.make_async_copy(
                small_hbm[operand].at[pl.ds(first, key_rows)],
                key_ref.at[pl.ds(place * key_rows, key_rows)],
                sems.at[1, number],
            )
        )
        copies.append(
            pltpu.make_async_copy(
                small_hbm[operand].at[pl.ds(first + key_rows, weight_rows)],
                weight.at[pl.ds(place * weight_rows, weight_rows)],
                sems.at[2, number],
            )
        )
    for copy in copies:
        copy.start()
    for copy in copies:
        copy.wait()
    value_ref[...] = dot(x_buf[...], weight[...]).astype(BF16)


def make_values(arrays, blocks, smalls, small_blocks, key_rows, width, earlier):
    smalls = [after(smalls[0], *earlier), *smalls[1:]]
    kv_width = smalls[0].shape[1]
    total = key_rows * len(blocks)
    kv = jax.ShapeDtypeStruct((total, kv_width), BF16)
    return pl.pallas_call(
        functools.partial(value_kernel, key_rows, blocks, small_blocks),
        out_shape=[kv, kv],
        in_specs=[ANY] * (len(arrays) + len(smalls)),
        out_specs=[IN_VMEM] * 2,
        scratch_shapes=[
            pltpu.VMEM((total, width), BF16),
            pltpu.VMEM((width, kv_width), BF16),
            pltpu.SemaphoreType.DMA((3, len(blocks))),
        ],
        compiler_params=pltpu.CompilerParams(vmem_limit_bytes=VMEM_LIMIT),
        cost_estimate=SHORT,
        name="values",
    )(*arrays, *smalls)


def attention_kernel(chunk, q_ref, k_ref, v_ref, *refs):
    out_ref = refs[-1]
    q_rows, q_width = q_ref.shape
    heads = q_width // HEAD_DIMENSION
    together = 4
    q_start = lax.axis_index("seq") * q_rows
    factor = math.log2(math.e) / math.sqrt(HEAD_DIMENSION)
    steps = k_ref.shape[0] // chunk
    tall = together * q_rows

    def scored(rows, start):
        scores = lax.dot_general(
            rows, k_ref[pl.ds(start, chunk)], (((1,), (1,)), ((), ())), preferred_element_type=F32
        )
        q_at = q_start + lax.broadcasted_iota(jnp.int32, (q_rows, chunk), 0)
        k_at = start + lax.broadcasted_iota(jnp.int32, (q_rows, chunk), 1)
        bias = jnp.where(q_at >= k_at, 0.0, -1e30)[None]
        return (scores.reshape(together, q_rows, chunk) + bias).reshape(tall, chunk)

    for at in range(0, heads, together):
        rows = jnp.concatenate(
            [
                q_ref[:, h * HEAD_DIMENSION : (h + 1) * HEAD_DIMENSION]
                for h in range(at, at + together)
            ],
            axis=0,
        )

        def one(step, state):
            top_score, run_sum, run_acc = state
            start = pl.multiple_of(step * chunk, chunk)
            scores = scored(rows, start)
            best = jnp.maximum(jnp.max(scores, axis=1, keepdims=True), top_score)
            rescale = jnp.exp2((top_score - best) * factor)
            weights = jnp.exp2((scores - best) * factor)
            total = run_sum * rescale + jnp.sum(weights, axis=1, keepdims=True)
            added = dot(weights.astype(BF16), v_ref[pl.ds(start, chunk)])
            return (best, total, run_acc * rescale + added)

        if steps == 1:
            scores = scored(rows, 0)
            best = jnp.max(scores, axis=1, keepdims=True)
            weights = jnp.exp2((scores - best) * factor)
            total = jnp.sum(weights, axis=1, keepdims=True)
            added = dot(weights.astype(BF16), v_ref[...])
        else:
            best, total, added = lax.fori_loop(
                0,
                (q_start + q_rows + chunk - 1) // chunk,
                one,
                (
                    jnp.full((tall, 1), -1e30, F32),
                    jnp.zeros((tall, 1), F32),
                    jnp.zeros((tall, HEAD_DIMENSION), F32),
                ),
            )
        context = (added / total).astype(BF16)
        for h in range(together):
            out_ref[:, (at + h) * HEAD_DIMENSION : (at + h + 1) * HEAD_DIMENSION] = context[
                h * q_rows : (h + 1) * q_rows
            ]


def attend_part(queries, keys, values, part, parts, context=None):
    q_rows, q_width = queries.shape
    total = keys.shape[0]
    part_width = q_width // parts
    per_kv = parts // KEY_VALUE_HEADS
    chunk = math.gcd(total, 1024)
    before = () if context is None else (context,)
    return pl.pallas_call(
        functools.partial(attention_kernel, chunk),
        grid=(1,),
        out_shape=jax.ShapeDtypeStruct((q_rows, q_width), BF16),
        in_specs=[
            pl.BlockSpec((q_rows, part_width), lambda i: (0, part)),
            pl.BlockSpec((total, HEAD_DIMENSION), lambda i: (0, part // per_kv)),
            pl.BlockSpec((total, HEAD_DIMENSION), lambda i: (0, part // per_kv)),
            *[ANY for _ in before],
        ],
        out_specs=pl.BlockSpec((q_rows, part_width), lambda i: (0, part)),
        input_output_aliases={3: 0} if before else {},
        compiler_params=pltpu.CompilerParams(vmem_limit_bytes=VMEM_LIMIT),
        cost_estimate=SHORT,
        name="attention",
    )(queries, keys, values, *before)


def summed(*terms):
    return sum(term.astype(F32) for term in terms).astype(BF16)


def after(x, *others):
    return lax.optimization_barrier((x, *others))[0]


def on_line(acts, packed, small, queries, w_gate_up, w_down, top, capacity):
    rows, width = acts.shape
    line = [packed, forward(packed), None, backward(packed)]
    crossed = [across(packed), across(line[1]), None, across(line[3])]
    pair = jnp.concatenate([small, across(small)], axis=0)
    line[2] = forward(after(line[1], pair, crossed[0]))
    crossed[2] = across(line[2])
    arrays = [
        [line[step], crossed[step], other_core(line[step]), other_core(crossed[step])]
        for step in range(LINE)
    ]
    blocks = [
        (4 * step + core * 2 + y, 0, functools.partial(from_device, step, y, core))
        for step in range(LINE)
        for core in range(2)
        for y in range(2)
    ]
    pair = after(pair, line[3])
    pairs = [pair, forward(pair), None, backward(pair)]
    pairs[2] = forward(pairs[1])
    small_rows = small.shape[0]
    small_blocks = [
        (2 * step + core, y * small_rows, functools.partial(from_device, step, y, core))
        for step in range(LINE)
        for core in range(2)
        for y in range(2)
    ]

    keep, mine, crossing = [None] * LINE, [None] * LINE, [None] * LINE

    def experts(first, second, before, beside):
        ready = arrays[first] + arrays[second]
        ready = [after(ready[0], *before), *ready[1:]]
        sources = [[(4 * group + i, 0, rows) for i in range(4)] for group in range(2)]
        targets = [[(group, 0, 2 * rows), (2, group * 2 * rows, 2 * rows)] for group in range(2)]
        keep[first], keep[second], send = run_experts(
            ready,
            sources,
            targets,
            [2 * rows, 2 * rows, 4 * rows],
            w_gate_up,
            w_down,
            top,
            rows,
            capacity,
        )
        came = other_core(after(send, *beside))
        for at, step in ((0, first), (2 * rows, second)):
            mine[step] = (keep[step][:rows], came[at : at + rows])
            crossing[step] = summed(keep[step][rows:], came[at + rows : at + 2 * rows])
        return send

    theirs = [None] * LINE
    experts(1, 0, [line[2], crossed[3]], [crossed[2], pairs[1]])
    theirs[1] = across(crossing[1])
    send = experts(2, 3, [crossing[0], crossing[1]], [theirs[1], pairs[2], pairs[3]])
    total = summed(*mine[1], after(theirs[1], send))
    moving = forward(total)
    smalls = []
    for step in range(LINE):
        smalls += [pairs[step], other_core(after(pairs[step], total))]
    theirs[2], theirs[3] = across(crossing[2]), across(crossing[3])
    new_keys, values = make_values(
        sum(arrays, []), blocks, smalls, small_blocks, rows, width, crossing[2:]
    )
    total = summed(*mine[2], theirs[2], after(moving, values))
    moving = forward(total)
    theirs[0] = across(after(crossing[0], total))
    context = attend_part(after(queries, total), new_keys, values, 0, 4)
    context = attend_part(queries, new_keys, values, 1, 4, context)
    total = summed(*mine[3], theirs[3], after(moving, context))
    moving = forward(total)
    context = attend_part(after(queries, total), new_keys, values, 2, 4, context)
    context = attend_part(queries, new_keys, values, 3, 4, context)
    layer_out = summed(acts, *mine[0], theirs[0], after(moving, context))
    return context, layer_out


def on_any(acts, packed, small, queries, w_gate_up, w_down, top, capacity):
    rows, width = acts.shape
    keys, value_weight = small[:rows], small[rows:]
    gathered = lax.all_gather(packed, "seq", axis=0, tiled=True)
    all_keys = lax.all_gather(keys, "seq", axis=0, tiled=True)
    weight = lax.all_gather(value_weight, "seq", axis=0, tiled=True)
    total = gathered.shape[0]
    part = total // GROUPS
    pieces = [[(0, group * part, part)] for group in range(GROUPS)]
    (partial,) = run_experts(
        [gathered], pieces, pieces, [total], w_gate_up, w_down, top, rows, capacity
    )
    values = dot(gathered[:, :width], weight).astype(BF16)
    context = None
    for part in range(KEY_VALUE_HEADS):
        context = attend_part(queries, all_keys, values, part, KEY_VALUE_HEADS, context)
    combined = lax.psum_scatter(partial, "seq", scatter_dimension=0, tiled=True)
    return context, summed(acts, combined)


def per_device(
    activations, queries, keys, norm_gain, value_weight, expert_ids, gate_weights, w_gate_up, w_down
):
    pos_rows, sequence_count, model_width = activations.shape
    assert sequence_count == 1 and w_down.shape[0] == 1
    top = expert_ids.shape[2]
    devices = lax.axis_size("seq")
    capacity = max(2, 3 * pos_rows * top // (2 * devices))
    acts = activations.reshape(pos_rows, model_width)
    packed, small = pack(
        acts,
        norm_gain,
        expert_ids.transpose(1, 2, 0).reshape(top, pos_rows),
        gate_weights.transpose(1, 2, 0).reshape(top, pos_rows),
        keys.reshape(pos_rows, -1),
        value_weight,
    )
    way = on_line if devices == 4 * LINE else on_any
    context, layer_out = way(
        acts,
        packed,
        small,
        queries.reshape(pos_rows, -1),
        w_gate_up[0],
        w_down[0],
        top,
        capacity,
    )
    return (context.reshape(queries.shape), layer_out.reshape(activations.shape))


def solution(mesh):
    placed = (
        P("seq", "grp", None),
        P("seq", "grp", None),
        P("seq", "grp", None),
        P(),
        P("seq", None),
        P("seq", "grp", None),
        P("seq", "grp", None),
        P("seq", None, None),
        P("seq", None, None),
    )
    return jax.shard_map(
        per_device,
        mesh=mesh,
        in_specs=placed,
        out_specs=(P("seq", "grp", None), P("seq", "grp", None)),
        check_vma=False,
    )
```

```python
import functools
import math

import jax
import jax.numpy as jnp
from jax import lax
from jax.experimental import pallas as pl
from jax.experimental.pallas import tpu as pltpu
from jax.sharding import PartitionSpec as P

QUERY_HEADS = 32
KEY_VALUE_HEADS = 2
HEAD_DIMENSION = 128
GROUPS = 4
META = 128
LINE = 4
VMEM_LIMIT = 24 * 2**20
F32 = jnp.float32
BF16 = jnp.bfloat16
ANY = pl.BlockSpec(memory_space=pl.ANY)
SHORT = pl.CostEstimate(flops=1, bytes_accessed=1, transcendentals=0)
IN_VMEM = pl.BlockSpec(memory_space=pltpu.VMEM)


def dot(a, b):
    return jnp.dot(a, b, preferred_element_type=F32)


RING = (0, 1, 3, 2)


def device_index(place, y, core):
    return (RING[place % LINE] * 2 + y) * 2 + core


def swaps(flip_y, flip_core):
    return [
        (device_index(p, y, c), device_index(p, y ^ flip_y, c ^ flip_core))
        for p in range(LINE)
        for y in range(2)
        for c in range(2)
    ]


def ring_steps(steps):
    return [
        (device_index(p, y, c), device_index(p + steps, y, c))
        for p in range(LINE)
        for y in range(2)
        for c in range(2)
    ]


def forward(x):
    return lax.ppermute(x, "seq", ring_steps(1))


def backward(x):
    return lax.ppermute(x, "seq", ring_steps(LINE - 1))


def across(x):
    return lax.ppermute(x, "seq", swaps(1, 0))


def other_core(x):
    return lax.ppermute(x, "seq", swaps(0, 1))


def from_device(steps, flip_y, flip_core):
    me = lax.axis_index("seq")
    core, y, line = me % 2, me // 2 % 2, me // 4
    place = sum(jnp.where(line == RING[p], p, 0) for p in range(LINE))
    place = (place + LINE - steps) % LINE
    line = sum(jnp.where(place == p, RING[p], 0) for p in range(LINE))
    y = 1 - y if flip_y else y
    core = 1 - core if flip_core else core
    return (line * 2 + y) * 2 + core


def pack_kernel(
    act_ref, gain_ref, ids_ref, gates_ref, key_ref, weight_ref, out_ref, small_ref, meta_ref
):
    width = act_ref.shape[1]
    rows = act_ref.shape[0]
    top = ids_ref.shape[0]
    features = act_ref[...].astype(F32)
    inverse = lax.rsqrt(jnp.mean(features * features, axis=-1, keepdims=True) + 1e-06)
    out_ref[:, :width] = (features * inverse * gain_ref[...]).astype(BF16)
    gates = gates_ref[...]
    high = gates.astype(BF16).astype(F32)
    rest = gates - high
    middle = rest.astype(BF16).astype(F32)
    meta_ref[...] = jnp.zeros_like(meta_ref)
    meta_ref[0:top, 0:rows] = ids_ref[...].astype(F32)
    meta_ref[8 : 8 + top, 0:rows] = high
    meta_ref[16 : 16 + top, 0:rows] = middle
    meta_ref[24 : 24 + top, 0:rows] = rest - middle
    out_ref[:, width:] = meta_ref[...].T[:rows, :].astype(BF16)
    small_ref[:rows] = key_ref[...]
    small_ref[rows:] = weight_ref[...]


def pack(activations, norm_gain, ids, gates, keys, value_weight):
    rows, width = activations.shape
    small_rows = rows + value_weight.shape[0]
    assert rows <= META and ids.shape[0] <= 8
    return pl.pallas_call(
        pack_kernel,
        out_shape=[
            jax.ShapeDtypeStruct((rows, width + META), BF16),
            jax.ShapeDtypeStruct((small_rows, keys.shape[1]), BF16),
        ],
        scratch_shapes=[pltpu.VMEM((META, META), F32)],
        cost_estimate=SHORT,
        name="normalize_and_pack",
    )(activations, norm_gain.reshape(1, width), ids, gates, keys, value_weight)


def hold_kernel(small_ref, up_ref, down_ref, out_ref):
    out_ref[...] = small_ref[...]


def hold(small, weights):
    return pl.pallas_call(
        hold_kernel,
        out_shape=jax.ShapeDtypeStruct(small.shape, small.dtype),
        in_specs=[IN_VMEM] * 3,
        out_specs=IN_VMEM,
        compiler_params=pltpu.CompilerParams(vmem_limit_bytes=4 * 2**20),
        cost_estimate=SHORT,
        name="hold_weights",
    )(small, *weights)


def in_vmem(*arrays):
    return [pltpu.with_memory_space_constraint(x, pltpu.VMEM) for x in arrays]


def expert_kernel(top, tok_rows, capacity, sources, targets, *refs):
    inputs = 1 + max(s[0] for group in sources for s in group)
    outputs = 1 + max(t[0] for group in targets for t in group)
    x_hbm = refs[:inputs]
    up_ref, down_ref = refs[inputs : inputs + 2]
    out_hbm = refs[inputs + 2 : inputs + 2 + outputs]
    (
        x_buf,
        slot_rows,
        slot_gates,
        places,
        hidden,
        result,
        x_sem,
        out_sem,
    ) = refs[inputs + 2 + outputs :]
    groups, rows, packed = x_buf.shape
    width = packed - META
    slots = slot_rows.shape[0] // groups
    units = down_ref.shape[0]
    tile = 256
    me = lax.axis_index("seq").astype(F32)

    def loads(group):
        copies, at = [], 0
        for number, (operand, first, count) in enumerate(sources[group]):
            copies.append(
                pltpu.make_async_copy(
                    x_hbm[operand].at[pl.ds(first, count)],
                    x_buf.at[group, pl.ds(at, count)],
                    x_sem.at[group, number],
                )
            )
            at += count
        return copies

    def stores(group):
        copies, at = [], 0
        for number, (operand, first, count) in enumerate(targets[group]):
            copies.append(
                pltpu.make_async_copy(
                    x_buf.at[group, pl.ds(at, count), pl.ds(0, width)],
                    out_hbm[operand].at[pl.ds(first, count)],
                    out_sem.at[group, number],
                )
            )
            at += count
        return copies

    for group in range(groups):
        for copy in loads(group):
            copy.start()

    chunk = tok_rows * META // math.gcd(tok_rows, META)
    first = lax.broadcasted_iota(jnp.int32, (chunk, chunk), 0)
    second = lax.broadcasted_iota(jnp.int32, (chunk, chunk), 1)
    earlier = ((first < second) & (first // tok_rows == second // tok_rows)).astype(F32).astype(BF16)
    block = lax.broadcasted_iota(jnp.int32, (1, rows), 1) // tok_rows
    for group in range(groups):
        for copy in loads(group):
            copy.wait()
        meta = x_buf[group, :, width:].astype(F32).T
        gate = jnp.zeros((1, rows), F32)
        named = jnp.zeros((1, rows), F32)
        for k in range(top):
            match = meta[k : k + 1] == me
            value = meta[8 + k : 9 + k] + (meta[16 + k : 17 + k] + meta[24 + k : 25 + k])
            gate = jnp.where(match, value, gate)
            named = jnp.where(match, 1.0, named)
        marks = jnp.broadcast_to(named, (8, rows)).astype(BF16)
        rank = jnp.concatenate(
            [dot(marks[:, at : at + chunk], earlier) for at in range(0, rows, chunk)], axis=1
        )[0:1]
        slot = jnp.where(named > 0.0, (block * capacity).astype(F32) + rank, -1.0)
        spots = lax.broadcasted_iota(jnp.int32, (slots, rows), 0).astype(F32)
        chosen = spots == slot
        slot_gates[pl.ds(group * slots, slots)] = jnp.broadcast_to(
            jnp.sum(jnp.where(chosen, gate, 0.0), axis=1, keepdims=True), (slots, META)
        )
        pick = chosen.astype(F32).astype(BF16)
        for at in range(0, width, 512):
            slot_rows[pl.ds(group * slots, slots), at : at + 512] = dot(
                pick, x_buf[group, :, at : at + 512]
            ).astype(BF16)
        by_row = jnp.broadcast_to(slot, (META, rows)).T
        spots = lax.broadcasted_iota(jnp.int32, (rows, META), 1).astype(F32)
        places[group] = (spots == by_row).astype(F32).astype(BF16)

    for at in range(0, units, tile):
        gate = dot(slot_rows[...], up_ref[:, at : at + tile])
        up = dot(slot_rows[...], up_ref[:, units + at : units + at + tile])
        hidden[:, at : at + tile] = (gate / (1.0 + jnp.exp(-gate)) * up).astype(BF16)
    for at in range(0, width, tile):
        out = dot(hidden[...], down_ref[:, at : at + tile]).astype(BF16).astype(F32)
        result[:, at : at + tile] = (out * slot_gates[:, 0:1]).astype(BF16)
    for group in range(groups):
        for at in range(0, width, 512):
            x_buf[group, :, at : at + 512] = dot(
                places[group, :, :slots], result[pl.ds(group * slots, slots), at : at + 512]
            ).astype(BF16)
        for copy in stores(group):
            copy.start()
    for group in range(groups):
        for copy in stores(group):
            copy.wait()


def run_experts(arrays, sources, targets, out_rows, w_gate_up, w_down, top, tok_rows, capacity):
    groups = len(sources)
    rows = sum(count for _, _, count in sources[0])
    packed = arrays[0].shape[1]
    total = groups * rows
    width = packed - META
    units = w_down.shape[0]
    slots = rows // tok_rows * capacity
    assert slots % 16 == 0 and slots <= META and units % 256 == 0 and width % 512 == 0
    all_slots = groups * slots
    weights = in_vmem(w_gate_up, w_down)
    held = 2 * total * (packed + META) + all_slots * (4 * width + 2 * units + 4 * META)
    return pl.pallas_call(
        functools.partial(expert_kernel, top, tok_rows, capacity, sources, targets),
        out_shape=[jax.ShapeDtypeStruct((count, width), BF16) for count in out_rows],
        in_specs=[ANY] * len(arrays) + [IN_VMEM] * 2,
        out_specs=[ANY] * len(out_rows),
        scratch_shapes=[
            pltpu.VMEM((groups, rows, packed), BF16),
            pltpu.VMEM((all_slots, width), BF16),
            pltpu.VMEM((all_slots, META), F32),
            pltpu.VMEM((groups, rows, META), BF16),
            pltpu.VMEM((all_slots, units), BF16),
            pltpu.VMEM((all_slots, width), BF16),
            pltpu.SemaphoreType.DMA((groups, max(len(s) for s in sources))),
            pltpu.SemaphoreType.DMA((groups, max(len(t) for t in targets))),
        ],
        compiler_params=pltpu.CompilerParams(vmem_limit_bytes=held + 8 * 2**20),
        cost_estimate=SHORT,
        name="experts",
    )(*arrays, *weights)


def value_kernel(key_rows, blocks, small_blocks, *refs):
    inputs = 1 + max(b[0] for b in blocks)
    smalls = 1 + max(b[0] for b in small_blocks)
    x_hbm = refs[:inputs]
    small_hbm = refs[inputs : inputs + smalls]
    key_ref, value_ref, x_buf, weight, sems = refs[inputs + smalls :]
    width = x_buf.shape[1]
    weight_rows = width // len(small_blocks)
    copies = []
    for number, (operand, first, device) in enumerate(blocks):
        copies.append(
            pltpu.make_async_copy(
                x_hbm[operand].at[pl.ds(first, key_rows), pl.ds(0, width)],
                x_buf.at[pl.ds(device() * key_rows, key_rows)],
                sems.at[0, number],
            )
        )
    for number, (operand, first, device) in enumerate(small_blocks):
        place = device()
        copies.append(
            pltpu.make_async_copy(
                small_hbm[operand].at[pl.ds(first, key_rows)],
                key_ref.at[pl.ds(place * key_rows, key_rows)],
                sems.at[1, number],
            )
        )
        copies.append(
            pltpu.make_async_copy(
                small_hbm[operand].at[pl.ds(first + key_rows, weight_rows)],
                weight.at[pl.ds(place * weight_rows, weight_rows)],
                sems.at[2, number],
            )
        )
    for copy in copies:
        copy.start()
    for copy in copies:
        copy.wait()
    value_ref[...] = dot(x_buf[...], weight[...]).astype(BF16)


def make_values(arrays, blocks, smalls, small_blocks, key_rows, width, earlier):
    smalls = [after(smalls[0], *earlier), *smalls[1:]]
    kv_width = smalls[0].shape[1]
    total = key_rows * len(blocks)
    kv = jax.ShapeDtypeStruct((total, kv_width), BF16)
    return pl.pallas_call(
        functools.partial(value_kernel, key_rows, blocks, small_blocks),
        out_shape=[kv, kv],
        in_specs=[ANY] * (len(arrays) + len(smalls)),
        out_specs=[IN_VMEM] * 2,
        scratch_shapes=[
            pltpu.VMEM((total, width), BF16),
            pltpu.VMEM((width, kv_width), BF16),
            pltpu.SemaphoreType.DMA((3, len(blocks))),
        ],
        compiler_params=pltpu.CompilerParams(vmem_limit_bytes=VMEM_LIMIT),
        cost_estimate=SHORT,
        name="values",
    )(*arrays, *smalls)


def attention_kernel(chunk, q_ref, k_ref, v_ref, *refs):
    out_ref = refs[-1]
    q_rows, q_width = q_ref.shape
    heads = q_width // HEAD_DIMENSION
    together = 4
    q_start = lax.axis_index("seq") * q_rows
    factor = math.log2(math.e) / math.sqrt(HEAD_DIMENSION)
    steps = k_ref.shape[0] // chunk
    tall = together * q_rows

    def scored(rows, start):
        scores = lax.dot_general(
            rows, k_ref[pl.ds(start, chunk)], (((1,), (1,)), ((), ())), preferred_element_type=F32
        )
        q_at = q_start + lax.broadcasted_iota(jnp.int32, (q_rows, chunk), 0)
        k_at = start + lax.broadcasted_iota(jnp.int32, (q_rows, chunk), 1)
        bias = jnp.where(q_at >= k_at, 0.0, -1e30)[None]
        return (scores.reshape(together, q_rows, chunk) + bias).reshape(tall, chunk)

    for at in range(0, heads, together):
        rows = jnp.concatenate(
            [
                q_ref[:, h * HEAD_DIMENSION : (h + 1) * HEAD_DIMENSION]
                for h in range(at, at + together)
            ],
            axis=0,
        )

        def one(step, state):
            top_score, run_sum, run_acc = state
            start = pl.multiple_of(step * chunk, chunk)
            scores = scored(rows, start)
            best = jnp.maximum(jnp.max(scores, axis=1, keepdims=True), top_score)
            rescale = jnp.exp2((top_score - best) * factor)
            weights = jnp.exp2((scores - best) * factor)
            total = run_sum * rescale + jnp.sum(weights, axis=1, keepdims=True)
            added = dot(weights.astype(BF16), v_ref[pl.ds(start, chunk)])
            return (best, total, run_acc * rescale + added)

        if steps == 1:
            scores = scored(rows, 0)
            best = jnp.max(scores, axis=1, keepdims=True)
            weights = jnp.exp2((scores - best) * factor)
            total = jnp.sum(weights, axis=1, keepdims=True)
            added = dot(weights.astype(BF16), v_ref[...])
        else:
            best, total, added = lax.fori_loop(
                0,
                (q_start + q_rows + chunk - 1) // chunk,
                one,
                (
                    jnp.full((tall, 1), -1e30, F32),
                    jnp.zeros((tall, 1), F32),
                    jnp.zeros((tall, HEAD_DIMENSION), F32),
                ),
            )
        context = (added / total).astype(BF16)
        for h in range(together):
            out_ref[:, (at + h) * HEAD_DIMENSION : (at + h + 1) * HEAD_DIMENSION] = context[
                h * q_rows : (h + 1) * q_rows
            ]


def attend_part(queries, keys, values, part, parts, context=None):
    q_rows, q_width = queries.shape
    total = keys.shape[0]
    part_width = q_width // parts
    per_kv = parts // KEY_VALUE_HEADS
    chunk = math.gcd(total, 1024)
    before = () if context is None else (context,)
    return pl.pallas_call(
        functools.partial(attention_kernel, chunk),
        grid=(1,),
        out_shape=jax.ShapeDtypeStruct((q_rows, q_width), BF16),
        in_specs=[
            pl.BlockSpec((q_rows, part_width), lambda i: (0, part)),
            pl.BlockSpec((total, HEAD_DIMENSION), lambda i: (0, part // per_kv)),
            pl.BlockSpec((total, HEAD_DIMENSION), lambda i: (0, part // per_kv)),
            *[ANY for _ in before],
        ],
        out_specs=pl.BlockSpec((q_rows, part_width), lambda i: (0, part)),
        input_output_aliases={3: 0} if before else {},
        compiler_params=pltpu.CompilerParams(vmem_limit_bytes=VMEM_LIMIT),
        cost_estimate=SHORT,
        name="attention",
    )(queries, keys, values, *before)


def summed(*terms):
    return sum(term.astype(F32) for term in terms).astype(BF16)


def after(x, *others):
    return lax.optimization_barrier((x, *others))[0]


def on_line(acts, packed, small, queries, w_gate_up, w_down, top, capacity):
    rows, width = acts.shape
    line = [packed, forward(packed), None, backward(packed)]
    crossed = [across(packed), across(line[1]), None, across(line[3])]
    to_core = other_core(packed)
    small = hold(after(small, to_core), in_vmem(w_gate_up, w_down))
    pair = jnp.concatenate([small, across(small)], axis=0)
    line[2] = forward(after(line[1], pair, crossed[0]))
    crossed[2] = across(line[2])
    arrays = [
        [
            line[step],
            crossed[step],
            other_core(line[step]) if step else to_core,
            other_core(crossed[step]),
        ]
        for step in range(LINE)
    ]
    blocks = [
        (4 * step + core * 2 + y, 0, functools.partial(from_device, step, y, core))
        for step in range(LINE)
        for core in range(2)
        for y in range(2)
    ]
    pair = after(pair, line[3])
    pairs = [pair, forward(pair), None, backward(pair)]
    pairs[2] = forward(pairs[1])
    small_rows = small.shape[0]
    small_blocks = [
        (2 * step + core, y * small_rows, functools.partial(from_device, step, y, core))
        for step in range(LINE)
        for core in range(2)
        for y in range(2)
    ]

    keep, mine, crossing = [None] * LINE, [None] * LINE, [None] * LINE

    def experts(first, second, before, beside):
        ready = arrays[first] + arrays[second]
        ready = [after(ready[0], *before), *ready[1:]]
        sources = [[(4 * group + i, 0, rows) for i in range(4)] for group in range(2)]
        targets = [[(group, 0, 2 * rows), (2, group * 2 * rows, 2 * rows)] for group in range(2)]
        keep[first], keep[second], send = run_experts(
            ready,
            sources,
            targets,
            [2 * rows, 2 * rows, 4 * rows],
            w_gate_up,
            w_down,
            top,
            rows,
            capacity,
        )
        came = other_core(after(send, *beside))
        for at, step in ((0, first), (2 * rows, second)):
            mine[step] = (keep[step][:rows], came[at : at + rows])
            crossing[step] = summed(keep[step][rows:], came[at + rows : at + 2 * rows])
        return send

    theirs = [None] * LINE
    experts(1, 0, [line[2], crossed[3]], [crossed[2], pairs[1]])
    theirs[1] = across(crossing[1])
    send = experts(2, 3, [crossing[0], crossing[1]], [theirs[1], pairs[2], pairs[3]])
    total = summed(*mine[1], after(theirs[1], send))
    moving = forward(total)
    smalls = []
    for step in range(LINE):
        smalls += [pairs[step], other_core(after(pairs[step], total))]
    theirs[2], theirs[3] = across(crossing[2]), across(crossing[3])
    new_keys, values = make_values(
        sum(arrays, []), blocks, smalls, small_blocks, rows, width, crossing[2:]
    )
    total = summed(*mine[2], theirs[2], after(moving, values))
    moving = forward(total)
    theirs[0] = across(after(crossing[0], total))
    context = attend_part(after(queries, total), new_keys, values, 0, 4)
    context = attend_part(queries, new_keys, values, 1, 4, context)
    total = summed(*mine[3], theirs[3], after(moving, context))
    moving = forward(total)
    context = attend_part(after(queries, total), new_keys, values, 2, 4, context)
    context = attend_part(queries, new_keys, values, 3, 4, context)
    layer_out = summed(acts, *mine[0], theirs[0], after(moving, context))
    return context, layer_out


def on_any(acts, packed, small, queries, w_gate_up, w_down, top, capacity):
    rows, width = acts.shape
    keys, value_weight = small[:rows], small[rows:]
    gathered = lax.all_gather(packed, "seq", axis=0, tiled=True)
    all_keys = lax.all_gather(keys, "seq", axis=0, tiled=True)
    weight = lax.all_gather(value_weight, "seq", axis=0, tiled=True)
    total = gathered.shape[0]
    part = total // GROUPS
    pieces = [[(0, group * part, part)] for group in range(GROUPS)]
    (partial,) = run_experts(
        [gathered], pieces, pieces, [total], w_gate_up, w_down, top, rows, capacity
    )
    values = dot(gathered[:, :width], weight).astype(BF16)
    context = None
    for part in range(KEY_VALUE_HEADS):
        context = attend_part(queries, all_keys, values, part, KEY_VALUE_HEADS, context)
    combined = lax.psum_scatter(partial, "seq", scatter_dimension=0, tiled=True)
    return context, summed(acts, combined)


def per_device(
    activations, queries, keys, norm_gain, value_weight, expert_ids, gate_weights, w_gate_up, w_down
):
    pos_rows, sequence_count, model_width = activations.shape
    assert sequence_count == 1 and w_down.shape[0] == 1
    top = expert_ids.shape[2]
    devices = lax.axis_size("seq")
    capacity = max(2, 3 * pos_rows * top // (2 * devices))
    acts = activations.reshape(pos_rows, model_width)
    packed, small = pack(
        acts,
        norm_gain,
        expert_ids.transpose(1, 2, 0).reshape(top, pos_rows),
        gate_weights.transpose(1, 2, 0).reshape(top, pos_rows),
        keys.reshape(pos_rows, -1),
        value_weight,
    )
    way = on_line if devices == 4 * LINE else on_any
    context, layer_out = way(
        acts,
        packed,
        small,
        queries.reshape(pos_rows, -1),
        w_gate_up[0],
        w_down[0],
        top,
        capacity,
    )
    return (context.reshape(queries.shape), layer_out.reshape(activations.shape))


def solution(mesh):
    placed = (
        P("seq", "grp", None),
        P("seq", "grp", None),
        P("seq", "grp", None),
        P(),
        P("seq", None),
        P("seq", "grp", None),
        P("seq", "grp", None),
        P("seq", None, None),
        P("seq", None, None),
    )
    return jax.shard_map(
        per_device,
        mesh=mesh,
        in_specs=placed,
        out_specs=(P("seq", "grp", None), P("seq", "grp", None)),
        check_vma=False,
    )
```

```python
import functools
import math

import jax
import jax.numpy as jnp
from jax import lax
from jax.experimental import pallas as pl
from jax.experimental.pallas import tpu as pltpu
from jax.sharding import PartitionSpec as P

QUERY_HEADS = 32
KEY_VALUE_HEADS = 2
HEAD_DIMENSION = 128
GROUPS = 4
META = 128
LINE = 4
VMEM_LIMIT = 24 * 2**20
F32 = jnp.float32
BF16 = jnp.bfloat16
ANY = pl.BlockSpec(memory_space=pl.ANY)
SHORT = pl.CostEstimate(flops=1, bytes_accessed=1, transcendentals=0)
IN_VMEM = pl.BlockSpec(memory_space=pltpu.VMEM)


def dot(a, b):
    return jnp.dot(a, b, preferred_element_type=F32)


RING = (0, 1, 3, 2)


def device_index(place, y, core):
    return (RING[place % LINE] * 2 + y) * 2 + core


def swaps(flip_y, flip_core):
    return [
        (device_index(p, y, c), device_index(p, y ^ flip_y, c ^ flip_core))
        for p in range(LINE)
        for y in range(2)
        for c in range(2)
    ]


def ring_steps(steps):
    return [
        (device_index(p, y, c), device_index(p + steps, y, c))
        for p in range(LINE)
        for y in range(2)
        for c in range(2)
    ]


def forward(x):
    return lax.ppermute(x, "seq", ring_steps(1))


def backward(x):
    return lax.ppermute(x, "seq", ring_steps(LINE - 1))


def across(x):
    return lax.ppermute(x, "seq", swaps(1, 0))


def other_core(x):
    return lax.ppermute(x, "seq", swaps(0, 1))


def from_device(steps, flip_y, flip_core):
    me = lax.axis_index("seq")
    core, y, line = me % 2, me // 2 % 2, me // 4
    place = sum(jnp.where(line == RING[p], p, 0) for p in range(LINE))
    place = (place + LINE - steps) % LINE
    line = sum(jnp.where(place == p, RING[p], 0) for p in range(LINE))
    y = 1 - y if flip_y else y
    core = 1 - core if flip_core else core
    return (line * 2 + y) * 2 + core


def pack_kernel(
    act_ref,
    gain_ref,
    ids_ref,
    gates_ref,
    key_ref,
    weight_ref,
    up_hbm,
    out_ref,
    small_ref,
    up_ref,
    meta_ref,
    up_sem,
):
    fetch = pltpu.make_async_copy(up_hbm, up_ref, up_sem)
    fetch.start()
    width = act_ref.shape[1]
    rows = act_ref.shape[0]
    top = ids_ref.shape[0]
    features = act_ref[...].astype(F32)
    inverse = lax.rsqrt(jnp.mean(features * features, axis=-1, keepdims=True) + 1e-06)
    out_ref[:, :width] = (features * inverse * gain_ref[...]).astype(BF16)
    gates = gates_ref[...]
    high = gates.astype(BF16).astype(F32)
    rest = gates - high
    middle = rest.astype(BF16).astype(F32)
    meta_ref[...] = jnp.zeros_like(meta_ref)
    meta_ref[0:top, 0:rows] = ids_ref[...].astype(F32)
    meta_ref[8 : 8 + top, 0:rows] = high
    meta_ref[16 : 16 + top, 0:rows] = middle
    meta_ref[24 : 24 + top, 0:rows] = rest - middle
    out_ref[:, width:] = meta_ref[...].T[:rows, :].astype(BF16)
    small_ref[:rows] = key_ref[...]
    small_ref[rows:] = weight_ref[...]
    fetch.wait()


def pack(activations, norm_gain, ids, gates, keys, value_weight, w_gate_up):
    rows, width = activations.shape
    small_rows = rows + value_weight.shape[0]
    from_hbm = pltpu.with_memory_space_constraint(w_gate_up, pltpu.HBM)
    assert rows <= META and ids.shape[0] <= 8
    return pl.pallas_call(
        pack_kernel,
        out_shape=[
            jax.ShapeDtypeStruct((rows, width + META), BF16),
            jax.ShapeDtypeStruct((small_rows, keys.shape[1]), BF16),
            pltpu.VMEM(w_gate_up.shape, BF16),
        ],
        in_specs=[IN_VMEM] * 6 + [ANY],
        out_specs=[IN_VMEM] * 3,
        scratch_shapes=[pltpu.VMEM((META, META), F32), pltpu.SemaphoreType.DMA(())],
        compiler_params=pltpu.CompilerParams(vmem_limit_bytes=VMEM_LIMIT),
        cost_estimate=SHORT,
        name="normalize_and_pack",
    )(activations, norm_gain.reshape(1, width), ids, gates, keys, value_weight, from_hbm)


def in_vmem(*arrays):
    return [pltpu.with_memory_space_constraint(x, pltpu.VMEM) for x in arrays]


def expert_kernel(top, tok_rows, capacity, sources, targets, *refs):
    inputs = 1 + max(s[0] for group in sources for s in group)
    outputs = 1 + max(t[0] for group in targets for t in group)
    x_hbm = refs[:inputs]
    up_ref, down_hbm = refs[inputs : inputs + 2]
    out_hbm = refs[inputs + 2 : inputs + 2 + outputs]
    (
        x_buf,
        down_buf,
        slot_rows,
        slot_gates,
        places,
        hidden,
        result,
        x_sem,
        down_sem,
        out_sem,
    ) = refs[inputs + 2 + outputs :]
    groups, rows, packed = x_buf.shape
    width = packed - META
    slots = slot_rows.shape[0] // groups
    units = down_buf.shape[0]
    tile = 256
    me = lax.axis_index("seq").astype(F32)

    def loads(group):
        copies, at = [], 0
        for number, (operand, first, count) in enumerate(sources[group]):
            copies.append(
                pltpu.make_async_copy(
                    x_hbm[operand].at[pl.ds(first, count)],
                    x_buf.at[group, pl.ds(at, count)],
                    x_sem.at[group, number],
                )
            )
            at += count
        return copies

    def stores(group):
        copies, at = [], 0
        for number, (operand, first, count) in enumerate(targets[group]):
            copies.append(
                pltpu.make_async_copy(
                    x_buf.at[group, pl.ds(at, count), pl.ds(0, width)],
                    out_hbm[operand].at[pl.ds(first, count)],
                    out_sem.at[group, number],
                )
            )
            at += count
        return copies

    for group in range(groups):
        for copy in loads(group):
            copy.start()
    load_down = pltpu.make_async_copy(down_hbm, down_buf, down_sem)
    load_down.start()

    chunk = tok_rows * META // math.gcd(tok_rows, META)
    first = lax.broadcasted_iota(jnp.int32, (chunk, chunk), 0)
    second = lax.broadcasted_iota(jnp.int32, (chunk, chunk), 1)
    earlier = ((first < second) & (first // tok_rows == second // tok_rows)).astype(F32).astype(BF16)
    block = lax.broadcasted_iota(jnp.int32, (1, rows), 1) // tok_rows
    for group in range(groups):
        for copy in loads(group):
            copy.wait()
        meta = x_buf[group, :, width:].astype(F32).T
        gate = jnp.zeros((1, rows), F32)
        named = jnp.zeros((1, rows), F32)
        for k in range(top):
            match = meta[k : k + 1] == me
            value = meta[8 + k : 9 + k] + (meta[16 + k : 17 + k] + meta[24 + k : 25 + k])
            gate = jnp.where(match, value, gate)
            named = jnp.where(match, 1.0, named)
        marks = jnp.broadcast_to(named, (8, rows)).astype(BF16)
        rank = jnp.concatenate(
            [dot(marks[:, at : at + chunk], earlier) for at in range(0, rows, chunk)], axis=1
        )[0:1]
        slot = jnp.where(named > 0.0, (block * capacity).astype(F32) + rank, -1.0)
        spots = lax.broadcasted_iota(jnp.int32, (slots, rows), 0).astype(F32)
        chosen = spots == slot
        slot_gates[pl.ds(group * slots, slots)] = jnp.broadcast_to(
            jnp.sum(jnp.where(chosen, gate, 0.0), axis=1, keepdims=True), (slots, META)
        )
        pick = chosen.astype(F32).astype(BF16)
        for at in range(0, width, 512):
            slot_rows[pl.ds(group * slots, slots), at : at + 512] = dot(
                pick, x_buf[group, :, at : at + 512]
            ).astype(BF16)
        by_row = jnp.broadcast_to(slot, (META, rows)).T
        spots = lax.broadcasted_iota(jnp.int32, (rows, META), 1).astype(F32)
        places[group] = (spots == by_row).astype(F32).astype(BF16)

    for at in range(0, units, tile):
        gate = dot(slot_rows[...], up_ref[:, at : at + tile])
        up = dot(slot_rows[...], up_ref[:, units + at : units + at + tile])
        hidden[:, at : at + tile] = (gate / (1.0 + jnp.exp(-gate)) * up).astype(BF16)
    load_down.wait()
    for at in range(0, width, tile):
        out = dot(hidden[...], down_buf[:, at : at + tile]).astype(BF16).astype(F32)
        result[:, at : at + tile] = (out * slot_gates[:, 0:1]).astype(BF16)
    for group in range(groups):
        for at in range(0, width, 512):
            x_buf[group, :, at : at + 512] = dot(
                places[group, :, :slots], result[pl.ds(group * slots, slots), at : at + 512]
            ).astype(BF16)
        for copy in stores(group):
            copy.start()
    for group in range(groups):
        for copy in stores(group):
            copy.wait()


def run_experts(arrays, sources, targets, out_rows, w_gate_up, w_down, top, tok_rows, capacity):
    groups = len(sources)
    rows = sum(count for _, _, count in sources[0])
    packed = arrays[0].shape[1]
    total = groups * rows
    width = packed - META
    units = w_down.shape[0]
    slots = rows // tok_rows * capacity
    assert slots % 16 == 0 and slots <= META and units % 256 == 0 and width % 512 == 0
    all_slots = groups * slots
    (w_gate_up,) = in_vmem(w_gate_up)
    held = 2 * units * width + 2 * total * (packed + META) + all_slots * (4 * width + 2 * units + 4 * META)
    return pl.pallas_call(
        functools.partial(expert_kernel, top, tok_rows, capacity, sources, targets),
        out_shape=[jax.ShapeDtypeStruct((count, width), BF16) for count in out_rows],
        in_specs=[ANY] * len(arrays) + [IN_VMEM, ANY],
        out_specs=[ANY] * len(out_rows),
        scratch_shapes=[
            pltpu.VMEM((groups, rows, packed), BF16),
            pltpu.VMEM(w_down.shape, BF16),
            pltpu.VMEM((all_slots, width), BF16),
            pltpu.VMEM((all_slots, META), F32),
            pltpu.VMEM((groups, rows, META), BF16),
            pltpu.VMEM((all_slots, units), BF16),
            pltpu.VMEM((all_slots, width), BF16),
            pltpu.SemaphoreType.DMA((groups, max(len(s) for s in sources))),
            pltpu.SemaphoreType.DMA(()),
            pltpu.SemaphoreType.DMA((groups, max(len(t) for t in targets))),
        ],
        compiler_params=pltpu.CompilerParams(vmem_limit_bytes=held + 8 * 2**20),
        cost_estimate=SHORT,
        name="experts",
    )(*arrays, w_gate_up, w_down)


def value_kernel(key_rows, blocks, small_blocks, *refs):
    inputs = 1 + max(b[0] for b in blocks)
    smalls = 1 + max(b[0] for b in small_blocks)
    x_hbm = refs[:inputs]
    small_hbm = refs[inputs : inputs + smalls]
    key_ref, value_ref, x_buf, weight, sems = refs[inputs + smalls :]
    width = x_buf.shape[1]
    weight_rows = width // len(small_blocks)
    copies = []
    for number, (operand, first, device) in enumerate(blocks):
        copies.append(
            pltpu.make_async_copy(
                x_hbm[operand].at[pl.ds(first, key_rows), pl.ds(0, width)],
                x_buf.at[pl.ds(device() * key_rows, key_rows)],
                sems.at[0, number],
            )
        )
    for number, (operand, first, device) in enumerate(small_blocks):
        place = device()
        copies.append(
            pltpu.make_async_copy(
                small_hbm[operand].at[pl.ds(first, key_rows)],
                key_ref.at[pl.ds(place * key_rows, key_rows)],
                sems.at[1, number],
            )
        )
        copies.append(
            pltpu.make_async_copy(
                small_hbm[operand].at[pl.ds(first + key_rows, weight_rows)],
                weight.at[pl.ds(place * weight_rows, weight_rows)],
                sems.at[2, number],
            )
        )
    for copy in copies:
        copy.start()
    for copy in copies:
        copy.wait()
    value_ref[...] = dot(x_buf[...], weight[...]).astype(BF16)


def make_values(arrays, blocks, smalls, small_blocks, key_rows, width, earlier):
    smalls = [after(smalls[0], *earlier), *smalls[1:]]
    kv_width = smalls[0].shape[1]
    total = key_rows * len(blocks)
    kv = jax.ShapeDtypeStruct((total, kv_width), BF16)
    return pl.pallas_call(
        functools.partial(value_kernel, key_rows, blocks, small_blocks),
        out_shape=[kv, kv],
        in_specs=[ANY] * (len(arrays) + len(smalls)),
        out_specs=[IN_VMEM] * 2,
        scratch_shapes=[
            pltpu.VMEM((total, width), BF16),
            pltpu.VMEM((width, kv_width), BF16),
            pltpu.SemaphoreType.DMA((3, len(blocks))),
        ],
        compiler_params=pltpu.CompilerParams(vmem_limit_bytes=VMEM_LIMIT),
        cost_estimate=SHORT,
        name="values",
    )(*arrays, *smalls)


def attention_kernel(chunk, q_ref, k_ref, v_ref, *refs):
    out_ref = refs[-1]
    q_rows, q_width = q_ref.shape
    heads = q_width // HEAD_DIMENSION
    together = 4
    q_start = lax.axis_index("seq") * q_rows
    factor = math.log2(math.e) / math.sqrt(HEAD_DIMENSION)
    steps = k_ref.shape[0] // chunk
    tall = together * q_rows

    def scored(rows, start):
        scores = lax.dot_general(
            rows, k_ref[pl.ds(start, chunk)], (((1,), (1,)), ((), ())), preferred_element_type=F32
        )
        q_at = q_start + lax.broadcasted_iota(jnp.int32, (q_rows, chunk), 0)
        k_at = start + lax.broadcasted_iota(jnp.int32, (q_rows, chunk), 1)
        bias = jnp.where(q_at >= k_at, 0.0, -1e30)[None]
        return (scores.reshape(together, q_rows, chunk) + bias).reshape(tall, chunk)

    for at in range(0, heads, together):
        rows = jnp.concatenate(
            [
                q_ref[:, h * HEAD_DIMENSION : (h + 1) * HEAD_DIMENSION]
                for h in range(at, at + together)
            ],
            axis=0,
        )

        def one(step, state):
            top_score, run_sum, run_acc = state
            start = pl.multiple_of(step * chunk, chunk)
            scores = scored(rows, start)
            best = jnp.maximum(jnp.max(scores, axis=1, keepdims=True), top_score)
            rescale = jnp.exp2((top_score - best) * factor)
            weights = jnp.exp2((scores - best) * factor)
            total = run_sum * rescale + jnp.sum(weights, axis=1, keepdims=True)
            added = dot(weights.astype(BF16), v_ref[pl.ds(start, chunk)])
            return (best, total, run_acc * rescale + added)

        if steps == 1:
            scores = scored(rows, 0)
            best = jnp.max(scores, axis=1, keepdims=True)
            weights = jnp.exp2((scores - best) * factor)
            total = jnp.sum(weights, axis=1, keepdims=True)
            added = dot(weights.astype(BF16), v_ref[...])
        else:
            best, total, added = lax.fori_loop(
                0,
                (q_start + q_rows + chunk - 1) // chunk,
                one,
                (
                    jnp.full((tall, 1), -1e30, F32),
                    jnp.zeros((tall, 1), F32),
                    jnp.zeros((tall, HEAD_DIMENSION), F32),
                ),
            )
        context = (added / total).astype(BF16)
        for h in range(together):
            out_ref[:, (at + h) * HEAD_DIMENSION : (at + h + 1) * HEAD_DIMENSION] = context[
                h * q_rows : (h + 1) * q_rows
            ]


def attend_part(queries, keys, values, part, parts, context=None):
    q_rows, q_width = queries.shape
    total = keys.shape[0]
    part_width = q_width // parts
    per_kv = parts // KEY_VALUE_HEADS
    chunk = math.gcd(total, 1024)
    before = () if context is None else (context,)
    return pl.pallas_call(
        functools.partial(attention_kernel, chunk),
        grid=(1,),
        out_shape=jax.ShapeDtypeStruct((q_rows, q_width), BF16),
        in_specs=[
            pl.BlockSpec((q_rows, part_width), lambda i: (0, part)),
            pl.BlockSpec((total, HEAD_DIMENSION), lambda i: (0, part // per_kv)),
            pl.BlockSpec((total, HEAD_DIMENSION), lambda i: (0, part // per_kv)),
            *[ANY for _ in before],
        ],
        out_specs=pl.BlockSpec((q_rows, part_width), lambda i: (0, part)),
        input_output_aliases={3: 0} if before else {},
        compiler_params=pltpu.CompilerParams(vmem_limit_bytes=VMEM_LIMIT),
        cost_estimate=SHORT,
        name="attention",
    )(queries, keys, values, *before)


def summed(*terms):
    return sum(term.astype(F32) for term in terms).astype(BF16)


def after(x, *others):
    return lax.optimization_barrier((x, *others))[0]


def on_line(acts, packed, small, queries, w_gate_up, w_down, top, capacity):
    rows, width = acts.shape
    line = [packed, forward(packed), None, backward(packed)]
    small_across = across(small)
    crossed = [across(after(packed, small_across)), across(line[1]), None, across(line[3])]
    pair = jnp.concatenate([small, small_across], axis=0)
    line[2] = forward(line[1])
    arrays = [None] * LINE

    def complete(step):
        arrays[step] = [
            line[step],
            crossed[step],
            other_core(line[step]),
            other_core(crossed[step]),
        ]

    for step in (0, 1, 3):
        complete(step)
    blocks = [
        (4 * step + core * 2 + y, 0, functools.partial(from_device, step, y, core))
        for step in range(LINE)
        for core in range(2)
        for y in range(2)
    ]
    pair = after(pair, line[3])
    pairs = [pair, forward(pair), None, backward(pair)]
    pairs[2] = forward(pairs[1])
    small_rows = small.shape[0]
    small_blocks = [
        (2 * step + core, y * small_rows, functools.partial(from_device, step, y, core))
        for step in range(LINE)
        for core in range(2)
        for y in range(2)
    ]

    keep, mine, crossing = [None] * LINE, [None] * LINE, [None] * LINE

    def experts(first, second, before, beside):
        ready = arrays[first] + arrays[second]
        ready = [after(ready[0], *before), *ready[1:]]
        sources = [[(4 * group + i, 0, rows) for i in range(4)] for group in range(2)]
        targets = [[(group, 0, 2 * rows), (2, group * 2 * rows, 2 * rows)] for group in range(2)]
        keep[first], keep[second], send = run_experts(
            ready,
            sources,
            targets,
            [2 * rows, 2 * rows, 4 * rows],
            w_gate_up,
            w_down,
            top,
            rows,
            capacity,
        )
        came = other_core(after(send, *beside))
        for at, step in ((0, first), (2 * rows, second)):
            mine[step] = (keep[step][:rows], came[at : at + rows])
            crossing[step] = summed(keep[step][rows:], came[at + rows : at + 2 * rows])
        return send

    theirs = [None] * LINE
    crossed[2] = across(line[2])
    complete(2)
    send = experts(1, 0, [line[2], pairs[0]], [crossed[3], crossed[2], pairs[1]])
    theirs[1] = across(crossing[1])
    send = experts(2, 3, [crossing[0], crossing[1]], [theirs[1], pairs[2], pairs[3]])
    total = summed(*mine[1], after(theirs[1], send))
    moving = forward(total)
    smalls = []
    for step in range(LINE):
        smalls += [pairs[step], other_core(after(pairs[step], total))]
    theirs[2], theirs[3] = across(crossing[2]), across(crossing[3])
    new_keys, values = make_values(
        sum(arrays, []), blocks, smalls, small_blocks, rows, width, crossing[2:]
    )
    total = summed(*mine[2], theirs[2], after(moving, values))
    moving = forward(total)
    theirs[0] = across(after(crossing[0], total))
    context = attend_part(after(queries, total), new_keys, values, 0, 4)
    context = attend_part(queries, new_keys, values, 1, 4, context)
    total = summed(*mine[3], theirs[3], after(moving, context))
    moving = forward(total)
    context = attend_part(after(queries, total), new_keys, values, 2, 4, context)
    context = attend_part(queries, new_keys, values, 3, 4, context)
    layer_out = summed(acts, *mine[0], theirs[0], after(moving, context))
    return context, layer_out


def on_any(acts, packed, small, queries, w_gate_up, w_down, top, capacity):
    rows, width = acts.shape
    keys, value_weight = small[:rows], small[rows:]
    gathered = lax.all_gather(packed, "seq", axis=0, tiled=True)
    all_keys = lax.all_gather(keys, "seq", axis=0, tiled=True)
    weight = lax.all_gather(value_weight, "seq", axis=0, tiled=True)
    total = gathered.shape[0]
    part = total // GROUPS
    pieces = [[(0, group * part, part)] for group in range(GROUPS)]
    (partial,) = run_experts(
        [gathered], pieces, pieces, [total], w_gate_up, w_down, top, rows, capacity
    )
    values = dot(gathered[:, :width], weight).astype(BF16)
    context = None
    for part in range(KEY_VALUE_HEADS):
        context = attend_part(queries, all_keys, values, part, KEY_VALUE_HEADS, context)
    combined = lax.psum_scatter(partial, "seq", scatter_dimension=0, tiled=True)
    return context, summed(acts, combined)


def per_device(
    activations, queries, keys, norm_gain, value_weight, expert_ids, gate_weights, w_gate_up, w_down
):
    pos_rows, sequence_count, model_width = activations.shape
    assert sequence_count == 1 and w_down.shape[0] == 1
    top = expert_ids.shape[2]
    devices = lax.axis_size("seq")
    capacity = max(2, 3 * pos_rows * top // (2 * devices))
    acts = activations.reshape(pos_rows, model_width)
    packed, small, up_weights = pack(
        acts,
        norm_gain,
        expert_ids.transpose(1, 2, 0).reshape(top, pos_rows),
        gate_weights.transpose(1, 2, 0).reshape(top, pos_rows),
        keys.reshape(pos_rows, -1),
        value_weight,
        w_gate_up[0],
    )
    way = on_line if devices == 4 * LINE else on_any
    context, layer_out = way(
        acts,
        packed,
        small,
        queries.reshape(pos_rows, -1),
        up_weights,
        w_down[0],
        top,
        capacity,
    )
    return (context.reshape(queries.shape), layer_out.reshape(activations.shape))


def solution(mesh):
    placed = (
        P("seq", "grp", None),
        P("seq", "grp", None),
        P("seq", "grp", None),
        P(),
        P("seq", None),
        P("seq", "grp", None),
        P("seq", "grp", None),
        P("seq", None, None),
        P("seq", None, None),
    )
    return jax.shard_map(
        per_device,
        mesh=mesh,
        in_specs=placed,
        out_specs=(P("seq", "grp", None), P("seq", "grp", None)),
        check_vma=False,
    )
```

```python
import functools
import math

import jax
import jax.numpy as jnp
from jax import lax
from jax.experimental import pallas as pl
from jax.experimental.pallas import tpu as pltpu
from jax.sharding import PartitionSpec as P

QUERY_HEADS = 32
KEY_VALUE_HEADS = 2
HEAD_DIMENSION = 128
GROUPS = 4
META = 128
LINE = 4
VMEM_LIMIT = 24 * 2**20
F32 = jnp.float32
BF16 = jnp.bfloat16
ANY = pl.BlockSpec(memory_space=pl.ANY)
SHORT = pl.CostEstimate(flops=1, bytes_accessed=1, transcendentals=0)
IN_VMEM = pl.BlockSpec(memory_space=pltpu.VMEM)


def dot(a, b):
    return jnp.dot(a, b, preferred_element_type=F32)


RING = (0, 1, 3, 2)


def device_index(place, y, core):
    return (RING[place % LINE] * 2 + y) * 2 + core


def swaps(flip_y, flip_core):
    return [
        (device_index(p, y, c), device_index(p, y ^ flip_y, c ^ flip_core))
        for p in range(LINE)
        for y in range(2)
        for c in range(2)
    ]


def ring_steps(steps):
    return [
        (device_index(p, y, c), device_index(p + steps, y, c))
        for p in range(LINE)
        for y in range(2)
        for c in range(2)
    ]


def forward(x):
    return lax.ppermute(x, "seq", ring_steps(1))


def backward(x):
    return lax.ppermute(x, "seq", ring_steps(LINE - 1))


def across(x):
    return lax.ppermute(x, "seq", swaps(1, 0))


def other_core(x):
    return lax.ppermute(x, "seq", swaps(0, 1))


def from_device(steps, flip_y, flip_core):
    me = lax.axis_index("seq")
    core, y, line = me % 2, me // 2 % 2, me // 4
    place = sum(jnp.where(line == RING[p], p, 0) for p in range(LINE))
    place = (place + LINE - steps) % LINE
    line = sum(jnp.where(place == p, RING[p], 0) for p in range(LINE))
    y = 1 - y if flip_y else y
    core = 1 - core if flip_core else core
    return (line * 2 + y) * 2 + core


def pack_kernel(*refs):
    sources, targets = refs[:7], refs[10:17]
    out_ref, small_ref, up_ref = refs[7:10]
    meta_ref, sems = refs[17:]
    act_ref, gain_ref, ids_ref, gates_ref = targets[:4]
    copies = [
        pltpu.make_async_copy(source, target, sems.at[number])
        for number, (source, target) in enumerate(zip(sources, targets))
    ]
    for copy in copies:
        copy.start()
    meta_ref[...] = jnp.zeros_like(meta_ref)
    for copy in copies[:4]:
        copy.wait()
    width = act_ref.shape[1]
    rows = act_ref.shape[0]
    top = ids_ref.shape[0]
    features = act_ref[...].astype(F32)
    inverse = lax.rsqrt(jnp.mean(features * features, axis=-1, keepdims=True) + 1e-06)
    out_ref[:, :width] = (features * inverse * gain_ref[...]).astype(BF16)
    gates = gates_ref[...]
    high = gates.astype(BF16).astype(F32)
    rest = gates - high
    middle = rest.astype(BF16).astype(F32)
    meta_ref[0:top, 0:rows] = ids_ref[...].astype(F32)
    meta_ref[8 : 8 + top, 0:rows] = high
    meta_ref[16 : 16 + top, 0:rows] = middle
    meta_ref[24 : 24 + top, 0:rows] = rest - middle
    out_ref[:, width:] = meta_ref[...].T[:rows, :].astype(BF16)
    for copy in copies[4:]:
        copy.wait()


def in_vmem(*arrays):
    return [pltpu.with_memory_space_constraint(x, pltpu.VMEM) for x in arrays]


def pack(activations, norm_gain, ids, gates, keys, value_weight, w_gate_up):
    rows, width = activations.shape
    small_rows = rows + value_weight.shape[0]
    assert rows <= META and ids.shape[0] <= 8
    operands = (activations, norm_gain.reshape(1, width), ids, gates, keys, value_weight, w_gate_up)

    def kernel(*refs):
        small_ref, up_ref = refs[8:10]
        loaded = (*refs[10:14], small_ref.at[pl.ds(0, rows)], small_ref.at[pl.ds(rows, small_rows - rows)], up_ref)
        pack_kernel(*refs[:10], *loaded, *refs[14:])

    return pl.pallas_call(
        kernel,
        out_shape=[
            jax.ShapeDtypeStruct((rows, width + META), BF16),
            jax.ShapeDtypeStruct((small_rows, keys.shape[1]), BF16),
            pltpu.VMEM(w_gate_up.shape, BF16),
        ],
        in_specs=[ANY] * 7,
        out_specs=[IN_VMEM] * 3,
        scratch_shapes=[
            *(pltpu.VMEM(x.shape, x.dtype) for x in operands[:4]),
            pltpu.VMEM((META, META), F32),
            pltpu.SemaphoreType.DMA((7,)),
        ],
        compiler_params=pltpu.CompilerParams(vmem_limit_bytes=VMEM_LIMIT),
        cost_estimate=SHORT,
        name="normalize_and_pack",
    )(*(pltpu.with_memory_space_constraint(x, pltpu.HBM) for x in operands))


def expert_kernel(top, tok_rows, capacity, sources, targets, *refs):
    inputs = 1 + max(s[0] for group in sources for s in group)
    outputs = 1 + max(t[0] for group in targets for t in group)
    x_hbm = refs[:inputs]
    up_ref, down_hbm = refs[inputs : inputs + 2]
    out_hbm = refs[inputs + 2 : inputs + 2 + outputs]
    (
        x_buf,
        down_buf,
        slot_rows,
        slot_gates,
        places,
        hidden,
        result,
        x_sem,
        down_sem,
        out_sem,
    ) = refs[inputs + 2 + outputs :]
    groups, rows, packed = x_buf.shape
    width = packed - META
    slots = slot_rows.shape[0] // groups
    units = down_buf.shape[0]
    tile = 256
    me = lax.axis_index("seq").astype(F32)

    def loads(group):
        copies, at = [], 0
        for number, (operand, first, count) in enumerate(sources[group]):
            copies.append(
                pltpu.make_async_copy(
                    x_hbm[operand].at[pl.ds(first, count)],
                    x_buf.at[group, pl.ds(at, count)],
                    x_sem.at[group, number],
                )
            )
            at += count
        return copies

    def stores(group):
        copies, at = [], 0
        for number, (operand, first, count) in enumerate(targets[group]):
            copies.append(
                pltpu.make_async_copy(
                    x_buf.at[group, pl.ds(at, count), pl.ds(0, width)],
                    out_hbm[operand].at[pl.ds(first, count)],
                    out_sem.at[group, number],
                )
            )
            at += count
        return copies

    for group in range(groups):
        for copy in loads(group):
            copy.start()
    load_down = pltpu.make_async_copy(down_hbm, down_buf, down_sem)
    load_down.start()

    chunk = tok_rows * META // math.gcd(tok_rows, META)
    first = lax.broadcasted_iota(jnp.int32, (chunk, chunk), 0)
    second = lax.broadcasted_iota(jnp.int32, (chunk, chunk), 1)
    earlier = ((first < second) & (first // tok_rows == second // tok_rows)).astype(F32).astype(BF16)
    block = lax.broadcasted_iota(jnp.int32, (1, rows), 1) // tok_rows
    for group in range(groups):
        for copy in loads(group):
            copy.wait()
        meta = x_buf[group, :, width:].astype(F32).T
        gate = jnp.zeros((1, rows), F32)
        named = jnp.zeros((1, rows), F32)
        for k in range(top):
            match = meta[k : k + 1] == me
            value = meta[8 + k : 9 + k] + (meta[16 + k : 17 + k] + meta[24 + k : 25 + k])
            gate = jnp.where(match, value, gate)
            named = jnp.where(match, 1.0, named)
        marks = jnp.broadcast_to(named, (8, rows)).astype(BF16)
        rank = jnp.concatenate(
            [dot(marks[:, at : at + chunk], earlier) for at in range(0, rows, chunk)], axis=1
        )[0:1]
        slot = jnp.where(named > 0.0, (block * capacity).astype(F32) + rank, -1.0)
        spots = lax.broadcasted_iota(jnp.int32, (slots, rows), 0).astype(F32)
        chosen = spots == slot
        slot_gates[pl.ds(group * slots, slots)] = jnp.broadcast_to(
            jnp.sum(jnp.where(chosen, gate, 0.0), axis=1, keepdims=True), (slots, META)
        )
        pick = chosen.astype(F32).astype(BF16)
        for at in range(0, width, 512):
            slot_rows[pl.ds(group * slots, slots), at : at + 512] = dot(
                pick, x_buf[group, :, at : at + 512]
            ).astype(BF16)
        by_row = jnp.broadcast_to(slot, (META, rows)).T
        spots = lax.broadcasted_iota(jnp.int32, (rows, META), 1).astype(F32)
        places[group] = (spots == by_row).astype(F32).astype(BF16)

    for at in range(0, units, tile):
        gate = dot(slot_rows[...], up_ref[:, at : at + tile])
        up = dot(slot_rows[...], up_ref[:, units + at : units + at + tile])
        hidden[:, at : at + tile] = (gate / (1.0 + jnp.exp(-gate)) * up).astype(BF16)
    load_down.wait()
    for at in range(0, width, tile):
        out = dot(hidden[...], down_buf[:, at : at + tile]).astype(BF16).astype(F32)
        result[:, at : at + tile] = (out * slot_gates[:, 0:1]).astype(BF16)
    for group in range(groups):
        for at in range(0, width, 512):
            x_buf[group, :, at : at + 512] = dot(
                places[group, :, :slots], result[pl.ds(group * slots, slots), at : at + 512]
            ).astype(BF16)
        for copy in stores(group):
            copy.start()
    for group in range(groups):
        for copy in stores(group):
            copy.wait()


def run_experts(arrays, sources, targets, out_rows, w_gate_up, w_down, top, tok_rows, capacity):
    groups = len(sources)
    rows = sum(count for _, _, count in sources[0])
    packed = arrays[0].shape[1]
    total = groups * rows
    width = packed - META
    units = w_down.shape[0]
    slots = rows // tok_rows * capacity
    assert slots % 16 == 0 and slots <= META and units % 256 == 0 and width % 512 == 0
    all_slots = groups * slots
    (w_gate_up,) = in_vmem(w_gate_up)
    held = 2 * units * width + 2 * total * (packed + META) + all_slots * (4 * width + 2 * units + 4 * META)
    return pl.pallas_call(
        functools.partial(expert_kernel, top, tok_rows, capacity, sources, targets),
        out_shape=[jax.ShapeDtypeStruct((count, width), BF16) for count in out_rows],
        in_specs=[ANY] * len(arrays) + [IN_VMEM, ANY],
        out_specs=[ANY] * len(out_rows),
        scratch_shapes=[
            pltpu.VMEM((groups, rows, packed), BF16),
            pltpu.VMEM(w_down.shape, BF16),
            pltpu.VMEM((all_slots, width), BF16),
            pltpu.VMEM((all_slots, META), F32),
            pltpu.VMEM((groups, rows, META), BF16),
            pltpu.VMEM((all_slots, units), BF16),
            pltpu.VMEM((all_slots, width), BF16),
            pltpu.SemaphoreType.DMA((groups, max(len(s) for s in sources))),
            pltpu.SemaphoreType.DMA(()),
            pltpu.SemaphoreType.DMA((groups, max(len(t) for t in targets))),
        ],
        compiler_params=pltpu.CompilerParams(vmem_limit_bytes=held + 8 * 2**20),
        cost_estimate=SHORT,
        name="experts",
    )(*arrays, w_gate_up, w_down)


def value_kernel(key_rows, blocks, small_blocks, *refs):
    inputs = 1 + max(b[0] for b in blocks)
    smalls = 1 + max(b[0] for b in small_blocks)
    x_hbm = refs[:inputs]
    small_hbm = refs[inputs : inputs + smalls]
    key_ref, value_ref, x_buf, weight, sems = refs[inputs + smalls :]
    width = x_buf.shape[1]
    weight_rows = width // len(small_blocks)
    copies = []
    for number, (operand, first, device) in enumerate(blocks):
        copies.append(
            pltpu.make_async_copy(
                x_hbm[operand].at[pl.ds(first, key_rows), pl.ds(0, width)],
                x_buf.at[pl.ds(device() * key_rows, key_rows)],
                sems.at[0, number],
            )
        )
    for number, (operand, first, device) in enumerate(small_blocks):
        place = device()
        copies.append(
            pltpu.make_async_copy(
                small_hbm[operand].at[pl.ds(first, key_rows)],
                key_ref.at[pl.ds(place * key_rows, key_rows)],
                sems.at[1, number],
            )
        )
        copies.append(
            pltpu.make_async_copy(
                small_hbm[operand].at[pl.ds(first + key_rows, weight_rows)],
                weight.at[pl.ds(place * weight_rows, weight_rows)],
                sems.at[2, number],
            )
        )
    for copy in copies:
        copy.start()
    for copy in copies:
        copy.wait()
    value_ref[...] = dot(x_buf[...], weight[...]).astype(BF16)


def make_values(arrays, blocks, smalls, small_blocks, key_rows, width, earlier):
    smalls = [after(smalls[0], *earlier), *smalls[1:]]
    kv_width = smalls[0].shape[1]
    total = key_rows * len(blocks)
    kv = jax.ShapeDtypeStruct((total, kv_width), BF16)
    return pl.pallas_call(
        functools.partial(value_kernel, key_rows, blocks, small_blocks),
        out_shape=[kv, kv],
        in_specs=[ANY] * (len(arrays) + len(smalls)),
        out_specs=[IN_VMEM] * 2,
        scratch_shapes=[
            pltpu.VMEM((total, width), BF16),
            pltpu.VMEM((width, kv_width), BF16),
            pltpu.SemaphoreType.DMA((3, len(blocks))),
        ],
        compiler_params=pltpu.CompilerParams(vmem_limit_bytes=VMEM_LIMIT),
        cost_estimate=SHORT,
        name="values",
    )(*arrays, *smalls)


def attention_kernel(chunk, q_ref, k_ref, v_ref, *refs):
    out_ref = refs[-1]
    q_rows, q_width = q_ref.shape
    heads = q_width // HEAD_DIMENSION
    together = 4
    q_start = lax.axis_index("seq") * q_rows
    factor = math.log2(math.e) / math.sqrt(HEAD_DIMENSION)
    steps = k_ref.shape[0] // chunk
    tall = together * q_rows

    def scored(rows, start):
        scores = lax.dot_general(
            rows, k_ref[pl.ds(start, chunk)], (((1,), (1,)), ((), ())), preferred_element_type=F32
        )
        q_at = q_start + lax.broadcasted_iota(jnp.int32, (q_rows, chunk), 0)
        k_at = start + lax.broadcasted_iota(jnp.int32, (q_rows, chunk), 1)
        bias = jnp.where(q_at >= k_at, 0.0, -1e30)[None]
        return (scores.reshape(together, q_rows, chunk) + bias).reshape(tall, chunk)

    for at in range(0, heads, together):
        rows = jnp.concatenate(
            [
                q_ref[:, h * HEAD_DIMENSION : (h + 1) * HEAD_DIMENSION]
                for h in range(at, at + together)
            ],
            axis=0,
        )

        def one(step, state):
            top_score, run_sum, run_acc = state
            start = pl.multiple_of(step * chunk, chunk)
            scores = scored(rows, start)
            best = jnp.maximum(jnp.max(scores, axis=1, keepdims=True), top_score)
            rescale = jnp.exp2((top_score - best) * factor)
            weights = jnp.exp2((scores - best) * factor)
            total = run_sum * rescale + jnp.sum(weights, axis=1, keepdims=True)
            added = dot(weights.astype(BF16), v_ref[pl.ds(start, chunk)])
            return (best, total, run_acc * rescale + added)

        if steps == 1:
            scores = scored(rows, 0)
            best = jnp.max(scores, axis=1, keepdims=True)
            weights = jnp.exp2((scores - best) * factor)
            total = jnp.sum(weights, axis=1, keepdims=True)
            added = dot(weights.astype(BF16), v_ref[...])
        else:
            best, total, added = lax.fori_loop(
                0,
                (q_start + q_rows + chunk - 1) // chunk,
                one,
                (
                    jnp.full((tall, 1), -1e30, F32),
                    jnp.zeros((tall, 1), F32),
                    jnp.zeros((tall, HEAD_DIMENSION), F32),
                ),
            )
        context = (added / total).astype(BF16)
        for h in range(together):
            out_ref[:, (at + h) * HEAD_DIMENSION : (at + h + 1) * HEAD_DIMENSION] = context[
                h * q_rows : (h + 1) * q_rows
            ]


def attend_part(queries, keys, values, part, parts, context=None):
    q_rows, q_width = queries.shape
    total = keys.shape[0]
    part_width = q_width // parts
    per_kv = parts // KEY_VALUE_HEADS
    chunk = math.gcd(total, 1024)
    before = () if context is None else (context,)
    return pl.pallas_call(
        functools.partial(attention_kernel, chunk),
        grid=(1,),
        out_shape=jax.ShapeDtypeStruct((q_rows, q_width), BF16),
        in_specs=[
            pl.BlockSpec((q_rows, part_width), lambda i: (0, part)),
            pl.BlockSpec((total, HEAD_DIMENSION), lambda i: (0, part // per_kv)),
            pl.BlockSpec((total, HEAD_DIMENSION), lambda i: (0, part // per_kv)),
            *[ANY for _ in before],
        ],
        out_specs=pl.BlockSpec((q_rows, part_width), lambda i: (0, part)),
        input_output_aliases={3: 0} if before else {},
        compiler_params=pltpu.CompilerParams(vmem_limit_bytes=VMEM_LIMIT),
        cost_estimate=SHORT,
        name="attention",
    )(queries, keys, values, *before)


def summed(*terms):
    return sum(term.astype(F32) for term in terms).astype(BF16)


def after(x, *others):
    return lax.optimization_barrier((x, *others))[0]


def on_line(acts, packed, small, queries, w_gate_up, w_down, top, capacity):
    rows, width = acts.shape
    line = [packed, forward(packed), None, backward(packed)]
    small_across = across(small)
    pair = jnp.concatenate([small, small_across], axis=0)
    line, crossed = [packed, forward(packed)], [across(after(packed, small_across))]
    line.append(None)
    line.append(backward(after(packed, line[1])))
    line[2] = forward(after(line[1], line[3]))
    crossed.append(across(line[1]))
    crossed.append(None)
    crossed.append(across(after(line[3], crossed[1])))
    crossed[2] = across(after(line[2], crossed[3]))
    arrays = [None] * LINE

    def complete(step, crossed_rows):
        arrays[step] = [
            line[step],
            crossed_rows,
            other_core(line[step]),
            other_core(crossed_rows),
        ]

    blocks = [
        (4 * step + core * 2 + y, 0, functools.partial(from_device, step, y, core))
        for step in range(LINE)
        for core in range(2)
        for y in range(2)
    ]
    pair = after(pair, line[2])
    pairs = [pair, forward(pair), None, None]
    pairs[3] = backward(after(pair, pairs[1]))
    for step in (0, 1, 3):
        complete(step, crossed[step])
    complete(2, after(crossed[2], pairs[1]))
    small_rows = small.shape[0]
    small_blocks = [
        (2 * step + core, y * small_rows, functools.partial(from_device, step, y, core))
        for step in range(LINE)
        for core in range(2)
        for y in range(2)
    ]

    mine, crossing = [None] * LINE, [None] * LINE

    def experts(first, second, before, beside):
        ready = arrays[first] + arrays[second]
        ready = [after(ready[0], *before), *ready[1:]]
        sources = [[(4 * group + i, 0, rows) for i in range(4)] for group in range(2)]
        targets = [[(group, 0, 2 * rows), (2 + group, 0, 2 * rows)] for group in range(2)]
        *keep, send_first, send_second = run_experts(
            ready, sources, targets, [2 * rows] * 4, w_gate_up, w_down, top, rows, capacity
        )
        came = other_core(after(send_first, *beside))
        mine[first] = (keep[0][:rows], came[:rows])
        crossing[first] = summed(keep[0][rows:], came[rows:])
        came = other_core(after(send_second, crossing[first]))
        mine[second] = (keep[1][:rows], came[:rows])
        crossing[second] = summed(keep[1][rows:], came[rows:])
        return send_first

    theirs = [None] * LINE
    experts(1, 0, [line[3]], [crossed[3]])
    theirs[1] = across(crossing[1])
    send = experts(2, 3, [], [theirs[1], pairs[3]])
    pairs[2] = forward(after(pairs[1], send))
    total = summed(*mine[1], after(theirs[1], send))
    moving = forward(total)
    smalls = []
    for step in range(LINE):
        smalls += [pairs[step], other_core(after(pairs[step], total))]
    theirs[2], theirs[3] = across(crossing[2]), across(crossing[3])
    total = summed(*mine[2], theirs[2], moving)
    moving = forward(total)
    theirs[0] = across(after(crossing[0], total))
    new_keys, values = make_values(
        sum(arrays, []), blocks, smalls, small_blocks, rows, width, [total]
    )
    total = summed(*mine[3], theirs[3], after(moving, values))
    moving = forward(total)
    queries = after(queries, total)
    context = None
    for part in range(4):
        context = attend_part(queries, new_keys, values, part, 4, context)
    layer_out = summed(acts, *mine[0], theirs[0], after(moving, context))
    return context, layer_out


def on_any(acts, packed, small, queries, w_gate_up, w_down, top, capacity):
    rows, width = acts.shape
    keys, value_weight = small[:rows], small[rows:]
    gathered = lax.all_gather(packed, "seq", axis=0, tiled=True)
    all_keys = lax.all_gather(keys, "seq", axis=0, tiled=True)
    weight = lax.all_gather(value_weight, "seq", axis=0, tiled=True)
    total = gathered.shape[0]
    part = total // GROUPS
    pieces = [[(0, group * part, part)] for group in range(GROUPS)]
    (partial,) = run_experts(
        [gathered], pieces, pieces, [total], w_gate_up, w_down, top, rows, capacity
    )
    values = dot(gathered[:, :width], weight).astype(BF16)
    context = None
    for part in range(KEY_VALUE_HEADS):
        context = attend_part(queries, all_keys, values, part, KEY_VALUE_HEADS, context)
    combined = lax.psum_scatter(partial, "seq", scatter_dimension=0, tiled=True)
    return context, summed(acts, combined)


def per_device(
    activations, queries, keys, norm_gain, value_weight, expert_ids, gate_weights, w_gate_up, w_down
):
    pos_rows, sequence_count, model_width = activations.shape
    assert sequence_count == 1 and w_down.shape[0] == 1
    top = expert_ids.shape[2]
    devices = lax.axis_size("seq")
    capacity = max(2, 3 * pos_rows * top // (2 * devices))
    acts = activations.reshape(pos_rows, model_width)
    packed, small, up_weights = pack(
        acts,
        norm_gain,
        expert_ids.transpose(1, 2, 0).reshape(top, pos_rows),
        gate_weights.transpose(1, 2, 0).reshape(top, pos_rows),
        keys.reshape(pos_rows, -1),
        value_weight,
        w_gate_up[0],
    )
    way = on_line if devices == 4 * LINE else on_any
    context, layer_out = way(
        acts,
        packed,
        small,
        queries.reshape(pos_rows, -1),
        up_weights,
        w_down[0],
        top,
        capacity,
    )
    return (context.reshape(queries.shape), layer_out.reshape(activations.shape))


def solution(mesh):
    placed = (
        P("seq", "grp", None),
        P("seq", "grp", None),
        P("seq", "grp", None),
        P(),
        P("seq", None),
        P("seq", "grp", None),
        P("seq", "grp", None),
        P("seq", None, None),
        P("seq", None, None),
    )
    return jax.shard_map(
        per_device,
        mesh=mesh,
        in_specs=placed,
        out_specs=(P("seq", "grp", None), P("seq", "grp", None)),
        check_vma=False,
    )
```

```python
import functools
import math

import jax
import jax.numpy as jnp
from jax import lax
from jax.experimental import pallas as pl
from jax.experimental.pallas import tpu as pltpu
from jax.sharding import PartitionSpec as P

QUERY_HEADS = 32
KEY_VALUE_HEADS = 2
HEAD_DIMENSION = 128
GROUPS = 4
META = 128
LINE = 4
VMEM_LIMIT = 24 * 2**20
F32 = jnp.float32
BF16 = jnp.bfloat16
ANY = pl.BlockSpec(memory_space=pl.ANY)
SHORT = pl.CostEstimate(flops=1, bytes_accessed=1, transcendentals=0)
IN_VMEM = pl.BlockSpec(memory_space=pltpu.VMEM)


def dot(a, b):
    return jnp.dot(a, b, preferred_element_type=F32)


RING = (0, 1, 3, 2)


def device_index(place, y, core):
    return (RING[place % LINE] * 2 + y) * 2 + core


def swaps(flip_y, flip_core):
    return [
        (device_index(p, y, c), device_index(p, y ^ flip_y, c ^ flip_core))
        for p in range(LINE)
        for y in range(2)
        for c in range(2)
    ]


def ring_steps(steps):
    return [
        (device_index(p, y, c), device_index(p + steps, y, c))
        for p in range(LINE)
        for y in range(2)
        for c in range(2)
    ]


def forward(x):
    return lax.ppermute(x, "seq", ring_steps(1))


def backward(x):
    return lax.ppermute(x, "seq", ring_steps(LINE - 1))


def across(x):
    return lax.ppermute(x, "seq", swaps(1, 0))


def other_core(x):
    return lax.ppermute(x, "seq", swaps(0, 1))


def from_device(steps, flip_y, flip_core):
    me = lax.axis_index("seq")
    core, y, line = me % 2, me // 2 % 2, me // 4
    place = sum(jnp.where(line == RING[p], p, 0) for p in range(LINE))
    place = (place + LINE - steps) % LINE
    line = sum(jnp.where(place == p, RING[p], 0) for p in range(LINE))
    y = 1 - y if flip_y else y
    core = 1 - core if flip_core else core
    return (line * 2 + y) * 2 + core


def pack_kernel(*refs):
    sources, targets = refs[:7], refs[10:17]
    out_ref, small_ref, up_ref = refs[7:10]
    meta_ref, sems = refs[17:]
    act_ref, gain_ref, ids_ref, gates_ref = targets[:4]
    copies = [
        pltpu.make_async_copy(source, target, sems.at[number])
        for number, (source, target) in enumerate(zip(sources, targets))
    ]
    for copy in copies:
        copy.start()
    meta_ref[...] = jnp.zeros_like(meta_ref)
    for copy in copies[:4]:
        copy.wait()
    width = act_ref.shape[1]
    rows = act_ref.shape[0]
    top = ids_ref.shape[0]
    features = act_ref[...].astype(F32)
    inverse = lax.rsqrt(jnp.mean(features * features, axis=-1, keepdims=True) + 1e-06)
    out_ref[:, :width] = (features * inverse * gain_ref[...]).astype(BF16)
    gates = gates_ref[...]
    high = gates.astype(BF16).astype(F32)
    rest = gates - high
    middle = rest.astype(BF16).astype(F32)
    meta_ref[0:top, 0:rows] = ids_ref[...].astype(F32)
    meta_ref[8 : 8 + top, 0:rows] = high
    meta_ref[16 : 16 + top, 0:rows] = middle
    meta_ref[24 : 24 + top, 0:rows] = rest - middle
    out_ref[:, width:] = meta_ref[...].T[:rows, :].astype(BF16)
    for copy in copies[4:]:
        copy.wait()


def in_vmem(*arrays):
    return [pltpu.with_memory_space_constraint(x, pltpu.VMEM) for x in arrays]


def pack(activations, norm_gain, ids, gates, keys, value_weight, w_gate_up):
    rows, width = activations.shape
    small_rows = rows + value_weight.shape[0]
    assert rows <= META and ids.shape[0] <= 8
    operands = (activations, norm_gain.reshape(1, width), ids, gates, keys, value_weight, w_gate_up)

    def kernel(*refs):
        small_ref, up_ref = refs[8:10]
        loaded = (*refs[10:14], small_ref.at[pl.ds(0, rows)], small_ref.at[pl.ds(rows, small_rows - rows)], up_ref)
        pack_kernel(*refs[:10], *loaded, *refs[14:])

    return pl.pallas_call(
        kernel,
        out_shape=[
            jax.ShapeDtypeStruct((rows, width + META), BF16),
            jax.ShapeDtypeStruct((small_rows, keys.shape[1]), BF16),
            pltpu.VMEM(w_gate_up.shape, BF16),
        ],
        in_specs=[ANY] * 7,
        out_specs=[IN_VMEM] * 3,
        scratch_shapes=[
            *(pltpu.VMEM(x.shape, x.dtype) for x in operands[:4]),
            pltpu.VMEM((META, META), F32),
            pltpu.SemaphoreType.DMA((7,)),
        ],
        compiler_params=pltpu.CompilerParams(vmem_limit_bytes=VMEM_LIMIT),
        cost_estimate=SHORT,
        name="normalize_and_pack",
    )(*(pltpu.with_memory_space_constraint(x, pltpu.HBM) for x in operands))


def expert_kernel(top, tok_rows, capacity, sources, targets, *refs):
    inputs = 1 + max(s[0] for group in sources for s in group)
    outputs = 1 + max(t[0] for group in targets for t in group)
    x_hbm = refs[:inputs]
    up_ref, down_hbm = refs[inputs : inputs + 2]
    out_hbm = refs[inputs + 2 : inputs + 2 + outputs]
    (
        x_buf,
        down_buf,
        slot_rows,
        slot_gates,
        places,
        hidden,
        result,
        x_sem,
        down_sem,
        out_sem,
    ) = refs[inputs + 2 + outputs :]
    groups, rows, packed = x_buf.shape
    width = packed - META
    slots = slot_rows.shape[0] // groups
    units = down_buf.shape[0]
    tile = 256
    me = lax.axis_index("seq").astype(F32)

    def loads(group):
        copies, at = [], 0
        for number, (operand, first, count) in enumerate(sources[group]):
            copies.append(
                pltpu.make_async_copy(
                    x_hbm[operand].at[pl.ds(first, count)],
                    x_buf.at[group, pl.ds(at, count)],
                    x_sem.at[group, number],
                )
            )
            at += count
        return copies

    def stores(group):
        copies, at = [], 0
        for number, (operand, first, count) in enumerate(targets[group]):
            copies.append(
                pltpu.make_async_copy(
                    x_buf.at[group, pl.ds(at, count), pl.ds(0, width)],
                    out_hbm[operand].at[pl.ds(first, count)],
                    out_sem.at[group, number],
                )
            )
            at += count
        return copies

    for group in range(groups):
        for copy in loads(group):
            copy.start()
    load_down = pltpu.make_async_copy(down_hbm, down_buf, down_sem)
    load_down.start()

    chunk = tok_rows * META // math.gcd(tok_rows, META)
    first = lax.broadcasted_iota(jnp.int32, (chunk, chunk), 0)
    second = lax.broadcasted_iota(jnp.int32, (chunk, chunk), 1)
    earlier = ((first < second) & (first // tok_rows == second // tok_rows)).astype(F32).astype(BF16)
    block = lax.broadcasted_iota(jnp.int32, (1, rows), 1) // tok_rows
    for group in range(groups):
        for copy in loads(group):
            copy.wait()
        meta = x_buf[group, :, width:].astype(F32).T
        gate = jnp.zeros((1, rows), F32)
        named = jnp.zeros((1, rows), F32)
        for k in range(top):
            match = meta[k : k + 1] == me
            value = meta[8 + k : 9 + k] + (meta[16 + k : 17 + k] + meta[24 + k : 25 + k])
            gate = jnp.where(match, value, gate)
            named = jnp.where(match, 1.0, named)
        marks = jnp.broadcast_to(named, (8, rows)).astype(BF16)
        rank = jnp.concatenate(
            [dot(marks[:, at : at + chunk], earlier) for at in range(0, rows, chunk)], axis=1
        )[0:1]
        slot = jnp.where(named > 0.0, (block * capacity).astype(F32) + rank, -1.0)
        spots = lax.broadcasted_iota(jnp.int32, (slots, rows), 0).astype(F32)
        chosen = spots == slot
        slot_gates[pl.ds(group * slots, slots)] = jnp.broadcast_to(
            jnp.sum(jnp.where(chosen, gate, 0.0), axis=1, keepdims=True), (slots, META)
        )
        pick = chosen.astype(F32).astype(BF16)
        for at in range(0, width, 512):
            slot_rows[pl.ds(group * slots, slots), at : at + 512] = dot(
                pick, x_buf[group, :, at : at + 512]
            ).astype(BF16)
        by_row = jnp.broadcast_to(slot, (META, rows)).T
        spots = lax.broadcasted_iota(jnp.int32, (rows, META), 1).astype(F32)
        places[group] = (spots == by_row).astype(F32).astype(BF16)

    for at in range(0, units, tile):
        gate = dot(slot_rows[...], up_ref[:, at : at + tile])
        up = dot(slot_rows[...], up_ref[:, units + at : units + at + tile])
        hidden[:, at : at + tile] = (gate / (1.0 + jnp.exp(-gate)) * up).astype(BF16)
    load_down.wait()
    for at in range(0, width, tile):
        out = dot(hidden[...], down_buf[:, at : at + tile]).astype(BF16).astype(F32)
        result[:, at : at + tile] = (out * slot_gates[:, 0:1]).astype(BF16)
    for group in range(groups):
        for at in range(0, width, 512):
            x_buf[group, :, at : at + 512] = dot(
                places[group, :, :slots], result[pl.ds(group * slots, slots), at : at + 512]
            ).astype(BF16)
        for copy in stores(group):
            copy.start()
    for group in range(groups):
        for copy in stores(group):
            copy.wait()


def run_experts(arrays, sources, targets, out_rows, w_gate_up, w_down, top, tok_rows, capacity):
    groups = len(sources)
    rows = sum(count for _, _, count in sources[0])
    packed = arrays[0].shape[1]
    total = groups * rows
    width = packed - META
    units = w_down.shape[0]
    slots = rows // tok_rows * capacity
    assert slots % 16 == 0 and slots <= META and units % 256 == 0 and width % 512 == 0
    all_slots = groups * slots
    (w_gate_up,) = in_vmem(w_gate_up)
    held = 2 * units * width + 2 * total * (packed + META) + all_slots * (4 * width + 2 * units + 4 * META)
    return pl.pallas_call(
        functools.partial(expert_kernel, top, tok_rows, capacity, sources, targets),
        out_shape=[jax.ShapeDtypeStruct((count, width), BF16) for count in out_rows],
        in_specs=[ANY] * len(arrays) + [IN_VMEM, ANY],
        out_specs=[ANY] * len(out_rows),
        scratch_shapes=[
            pltpu.VMEM((groups, rows, packed), BF16),
            pltpu.VMEM(w_down.shape, BF16),
            pltpu.VMEM((all_slots, width), BF16),
            pltpu.VMEM((all_slots, META), F32),
            pltpu.VMEM((groups, rows, META), BF16),
            pltpu.VMEM((all_slots, units), BF16),
            pltpu.VMEM((all_slots, width), BF16),
            pltpu.SemaphoreType.DMA((groups, max(len(s) for s in sources))),
            pltpu.SemaphoreType.DMA(()),
            pltpu.SemaphoreType.DMA((groups, max(len(t) for t in targets))),
        ],
        compiler_params=pltpu.CompilerParams(vmem_limit_bytes=held + 8 * 2**20),
        cost_estimate=SHORT,
        name="experts",
    )(*arrays, w_gate_up, w_down)


def value_kernel(key_rows, blocks, small_blocks, *refs):
    inputs = 1 + max(b[0] for b in blocks)
    smalls = 1 + max(b[0] for b in small_blocks)
    x_hbm = refs[:inputs]
    small_hbm = refs[inputs : inputs + smalls]
    key_ref, value_ref, x_buf, weight, sems = refs[inputs + smalls :]
    width = x_buf.shape[1]
    weight_rows = width // len(small_blocks)
    copies = []
    for number, (operand, first, device) in enumerate(blocks):
        copies.append(
            pltpu.make_async_copy(
                x_hbm[operand].at[pl.ds(first, key_rows), pl.ds(0, width)],
                x_buf.at[pl.ds(device() * key_rows, key_rows)],
                sems.at[0, number],
            )
        )
    for number, (operand, first, device) in enumerate(small_blocks):
        place = device()
        copies.append(
            pltpu.make_async_copy(
                small_hbm[operand].at[pl.ds(first, key_rows)],
                key_ref.at[pl.ds(place * key_rows, key_rows)],
                sems.at[1, number],
            )
        )
        copies.append(
            pltpu.make_async_copy(
                small_hbm[operand].at[pl.ds(first + key_rows, weight_rows)],
                weight.at[pl.ds(place * weight_rows, weight_rows)],
                sems.at[2, number],
            )
        )
    for copy in copies:
        copy.start()
    for copy in copies:
        copy.wait()
    value_ref[...] = dot(x_buf[...], weight[...]).astype(BF16)


def make_values(arrays, blocks, smalls, small_blocks, key_rows, width, earlier):
    smalls = [after(smalls[0], *earlier), *smalls[1:]]
    kv_width = smalls[0].shape[1]
    total = key_rows * len(blocks)
    kv = jax.ShapeDtypeStruct((total, kv_width), BF16)
    return pl.pallas_call(
        functools.partial(value_kernel, key_rows, blocks, small_blocks),
        out_shape=[kv, kv],
        in_specs=[ANY] * (len(arrays) + len(smalls)),
        out_specs=[IN_VMEM] * 2,
        scratch_shapes=[
            pltpu.VMEM((total, width), BF16),
            pltpu.VMEM((width, kv_width), BF16),
            pltpu.SemaphoreType.DMA((3, len(blocks))),
        ],
        compiler_params=pltpu.CompilerParams(vmem_limit_bytes=VMEM_LIMIT),
        cost_estimate=SHORT,
        name="values",
    )(*arrays, *smalls)


def attention_kernel(chunk, q_ref, k_ref, v_ref, *refs):
    out_ref = refs[-1]
    q_rows, q_width = q_ref.shape
    heads = q_width // HEAD_DIMENSION
    together = 4
    q_start = lax.axis_index("seq") * q_rows
    factor = math.log2(math.e) / math.sqrt(HEAD_DIMENSION)
    steps = k_ref.shape[0] // chunk
    tall = together * q_rows

    def scored(rows, start):
        scores = lax.dot_general(
            rows, k_ref[pl.ds(start, chunk)], (((1,), (1,)), ((), ())), preferred_element_type=F32
        )
        q_at = q_start + lax.broadcasted_iota(jnp.int32, (q_rows, chunk), 0)
        k_at = start + lax.broadcasted_iota(jnp.int32, (q_rows, chunk), 1)
        bias = jnp.where(q_at >= k_at, 0.0, -1e30)[None]
        return (scores.reshape(together, q_rows, chunk) + bias).reshape(tall, chunk)

    for at in range(0, heads, together):
        rows = jnp.concatenate(
            [
                q_ref[:, h * HEAD_DIMENSION : (h + 1) * HEAD_DIMENSION]
                for h in range(at, at + together)
            ],
            axis=0,
        )

        def one(step, state):
            top_score, run_sum, run_acc = state
            start = pl.multiple_of(step * chunk, chunk)
            scores = scored(rows, start)
            best = jnp.maximum(jnp.max(scores, axis=1, keepdims=True), top_score)
            rescale = jnp.exp2((top_score - best) * factor)
            weights = jnp.exp2((scores - best) * factor)
            total = run_sum * rescale + jnp.sum(weights, axis=1, keepdims=True)
            added = dot(weights.astype(BF16), v_ref[pl.ds(start, chunk)])
            return (best, total, run_acc * rescale + added)

        if steps == 1:
            scores = scored(rows, 0)
            best = jnp.max(scores, axis=1, keepdims=True)
            weights = jnp.exp2((scores - best) * factor)
            total = jnp.sum(weights, axis=1, keepdims=True)
            added = dot(weights.astype(BF16), v_ref[...])
        else:
            best, total, added = lax.fori_loop(
                0,
                (q_start + q_rows + chunk - 1) // chunk,
                one,
                (
                    jnp.full((tall, 1), -1e30, F32),
                    jnp.zeros((tall, 1), F32),
                    jnp.zeros((tall, HEAD_DIMENSION), F32),
                ),
            )
        context = (added / total).astype(BF16)
        for h in range(together):
            out_ref[:, (at + h) * HEAD_DIMENSION : (at + h + 1) * HEAD_DIMENSION] = context[
                h * q_rows : (h + 1) * q_rows
            ]


def attend_part(queries, keys, values, part, parts, context=None):
    q_rows, q_width = queries.shape
    total = keys.shape[0]
    part_width = q_width // parts
    per_kv = parts // KEY_VALUE_HEADS
    chunk = math.gcd(total, 1024)
    before = () if context is None else (context,)
    return pl.pallas_call(
        functools.partial(attention_kernel, chunk),
        grid=(1,),
        out_shape=jax.ShapeDtypeStruct((q_rows, q_width), BF16),
        in_specs=[
            pl.BlockSpec((q_rows, part_width), lambda i: (0, part)),
            pl.BlockSpec((total, HEAD_DIMENSION), lambda i: (0, part // per_kv)),
            pl.BlockSpec((total, HEAD_DIMENSION), lambda i: (0, part // per_kv)),
            *[ANY for _ in before],
        ],
        out_specs=pl.BlockSpec((q_rows, part_width), lambda i: (0, part)),
        input_output_aliases={3: 0} if before else {},
        compiler_params=pltpu.CompilerParams(vmem_limit_bytes=VMEM_LIMIT),
        cost_estimate=SHORT,
        name="attention",
    )(queries, keys, values, *before)


def summed(*terms):
    return sum(term.astype(F32) for term in terms).astype(BF16)


def after(x, *others):
    return lax.optimization_barrier((x, *others))[0]


def on_line(acts, packed, small, queries, w_gate_up, w_down, top, capacity):
    rows, width = acts.shape
    small_across = across(small)
    pair = jnp.concatenate([small, small_across], axis=0)
    line = [packed, forward(packed), None, backward(packed)]
    line[2] = forward(line[1])
    crossed = [across(after(packed, small_across)), *map(across, line[1:])]
    arrays = [
        [line[step], crossed[step], other_core(line[step]), other_core(crossed[step])]
        for step in range(LINE)
    ]
    blocks = [
        (4 * step + core * 2 + y, 0, functools.partial(from_device, step, y, core))
        for step in range(LINE)
        for core in range(2)
        for y in range(2)
    ]
    pair = after(pair, line[2])
    pairs = [pair, forward(pair), None, None]
    pairs[3] = backward(after(pair, pairs[1]))
    small_rows = small.shape[0]
    small_blocks = [
        (2 * step + core, y * small_rows, functools.partial(from_device, step, y, core))
        for step in range(LINE)
        for core in range(2)
        for y in range(2)
    ]

    def experts(first, second, before, beside):
        ready = arrays[first] + arrays[second]
        ready = [after(ready[0], *before), *ready[1:]]
        sources = [[(4 * group + i, 0, rows) for i in range(4)] for group in range(2)]
        targets = [[(group, 0, 2 * rows), (2 + group, 0, 2 * rows)] for group in range(2)]
        *keep, send_first, send_second = run_experts(
            ready, sources, targets, [2 * rows] * 4, w_gate_up, w_down, top, rows, capacity
        )
        came_first = other_core(after(send_first, *beside))
        crossing = summed(keep[0][rows:], came_first[rows:])
        came_second = other_core(after(send_second, crossing))
        return keep, (came_first, came_second), send_first

    beside = [crossed[3], crossed[2], pairs[1], arrays[3][2], arrays[2][2]]
    keep, came, send = experts(1, 0, [line[2]], beside)
    near = [(keep[i][:rows], came[i][:rows]) for i in range(2)]
    crossing = [summed(keep[i][rows:], came[i][rows:]) for i in range(2)]
    theirs_near = across(crossing[0])
    keep, came, send = experts(2, 3, [crossing[0]], [theirs_near, pairs[3]])
    pairs[2] = forward(after(pairs[1], send))
    total = summed(*near[0], after(theirs_near, send))
    moving = forward(total)
    far = [summed(keep[i][rows:], came[i][rows:]) for i in range(2)]
    theirs = across(far[0])
    smalls = []
    for step in range(LINE):
        smalls += [pairs[step], other_core(after(pairs[step], far[0]))]
    total = summed(keep[0][:rows], came[0][:rows], theirs, moving)
    moving = forward(total)
    new_keys, values = make_values(
        sum(arrays, []), blocks, smalls, small_blocks, rows, width, [total]
    )
    theirs = across(after(far[1], theirs))
    total = summed(keep[1][:rows], came[1][:rows], theirs, after(moving, values))
    moving = forward(total)
    theirs = across(after(crossing[1], theirs))
    queries = after(queries, total)
    context = None
    for number in range(4):
        context = attend_part(queries, new_keys, values, number, 4, context)
    layer_out = summed(acts, *near[1], theirs, after(moving, context))
    return context, layer_out


def on_any(acts, packed, small, queries, w_gate_up, w_down, top, capacity):
    rows, width = acts.shape
    keys, value_weight = small[:rows], small[rows:]
    gathered = lax.all_gather(packed, "seq", axis=0, tiled=True)
    all_keys = lax.all_gather(keys, "seq", axis=0, tiled=True)
    weight = lax.all_gather(value_weight, "seq", axis=0, tiled=True)
    total = gathered.shape[0]
    part = total // GROUPS
    pieces = [[(0, group * part, part)] for group in range(GROUPS)]
    (partial,) = run_experts(
        [gathered], pieces, pieces, [total], w_gate_up, w_down, top, rows, capacity
    )
    values = dot(gathered[:, :width], weight).astype(BF16)
    context = None
    for part in range(KEY_VALUE_HEADS):
        context = attend_part(queries, all_keys, values, part, KEY_VALUE_HEADS, context)
    combined = lax.psum_scatter(partial, "seq", scatter_dimension=0, tiled=True)
    return context, summed(acts, combined)


def per_device(
    activations, queries, keys, norm_gain, value_weight, expert_ids, gate_weights, w_gate_up, w_down
):
    pos_rows, sequence_count, model_width = activations.shape
    assert sequence_count == 1 and w_down.shape[0] == 1
    top = expert_ids.shape[2]
    devices = lax.axis_size("seq")
    capacity = max(2, 3 * pos_rows * top // (2 * devices))
    acts = activations.reshape(pos_rows, model_width)
    packed, small, up_weights = pack(
        acts,
        norm_gain,
        expert_ids.transpose(1, 2, 0).reshape(top, pos_rows),
        gate_weights.transpose(1, 2, 0).reshape(top, pos_rows),
        keys.reshape(pos_rows, -1),
        value_weight,
        w_gate_up[0],
    )
    way = on_line if devices == 4 * LINE else on_any
    context, layer_out = way(
        acts,
        packed,
        small,
        queries.reshape(pos_rows, -1),
        up_weights,
        w_down[0],
        top,
        capacity,
    )
    return (context.reshape(queries.shape), layer_out.reshape(activations.shape))


def solution(mesh):
    placed = (
        P("seq", "grp", None),
        P("seq", "grp", None),
        P("seq", "grp", None),
        P(),
        P("seq", None),
        P("seq", "grp", None),
        P("seq", "grp", None),
        P("seq", None, None),
        P("seq", None, None),
    )
    return jax.shard_map(
        per_device,
        mesh=mesh,
        in_specs=placed,
        out_specs=(P("seq", "grp", None), P("seq", "grp", None)),
        check_vma=False,
    )
```

```python
import functools
import math

import jax
import jax.numpy as jnp
from jax import lax
from jax.experimental import pallas as pl
from jax.experimental.pallas import tpu as pltpu
from jax.sharding import PartitionSpec as P

QUERY_HEADS = 32
KEY_VALUE_HEADS = 2
HEAD_DIMENSION = 128
GROUPS = 4
META = 128
LINE = 4
VMEM_LIMIT = 24 * 2**20
F32 = jnp.float32
BF16 = jnp.bfloat16
ANY = pl.BlockSpec(memory_space=pl.ANY)
SHORT = pl.CostEstimate(flops=1, bytes_accessed=1, transcendentals=0)
IN_VMEM = pl.BlockSpec(memory_space=pltpu.VMEM)


def dot(a, b):
    return jnp.dot(a, b, preferred_element_type=F32)


RING = (0, 1, 3, 2)


def device_index(place, y, core):
    return (RING[place % LINE] * 2 + y) * 2 + core


def swaps(flip_y, flip_core):
    return [
        (device_index(p, y, c), device_index(p, y ^ flip_y, c ^ flip_core))
        for p in range(LINE)
        for y in range(2)
        for c in range(2)
    ]


def ring_steps(steps):
    return [
        (device_index(p, y, c), device_index(p + steps, y, c))
        for p in range(LINE)
        for y in range(2)
        for c in range(2)
    ]


def forward(x):
    return lax.ppermute(x, "seq", ring_steps(1))


def backward(x):
    return lax.ppermute(x, "seq", ring_steps(LINE - 1))


def across(x):
    return lax.ppermute(x, "seq", swaps(1, 0))


def other_core(x):
    return lax.ppermute(x, "seq", swaps(0, 1))


def from_device(steps, flip_y, flip_core):
    me = lax.axis_index("seq")
    core, y, line = me % 2, me // 2 % 2, me // 4
    place = sum(jnp.where(line == RING[p], p, 0) for p in range(LINE))
    place = (place + LINE - steps) % LINE
    line = sum(jnp.where(place == p, RING[p], 0) for p in range(LINE))
    y = 1 - y if flip_y else y
    core = 1 - core if flip_core else core
    return (line * 2 + y) * 2 + core


def pack_kernel(act_hbm, gain_hbm, ids_hbm, gates_hbm, up_hbm, *refs):
    *extra, out_ref, up_ref, act_ref, gain_ref, ids_ref, gates_ref, meta_ref, sems = refs
    rows, width = act_ref.shape
    top = ids_ref.shape[0]
    pairs = [
        (act_hbm, act_ref),
        (gain_hbm, gain_ref),
        (ids_hbm, ids_ref),
        (gates_hbm, gates_ref),
        (up_hbm, up_ref),
    ]
    at = width + META
    for source in extra:
        for first in range(0, source.shape[0], rows):
            pairs.append(
                (source.at[pl.ds(first, rows)], out_ref.at[:, pl.ds(at, source.shape[1])])
            )
            at += source.shape[1]
    copies = [
        pltpu.make_async_copy(source, target, sems.at[number])
        for number, (source, target) in enumerate(pairs)
    ]
    for copy in copies:
        copy.start()
    meta_ref[...] = jnp.zeros_like(meta_ref)
    for copy in copies[:4]:
        copy.wait()
    features = act_ref[...].astype(F32)
    inverse = lax.rsqrt(jnp.mean(features * features, axis=-1, keepdims=True) + 1e-06)
    out_ref[:, :width] = (features * inverse * gain_ref[...]).astype(BF16)
    gates = gates_ref[...]
    high = gates.astype(BF16).astype(F32)
    rest = gates - high
    middle = rest.astype(BF16).astype(F32)
    meta_ref[0:top, 0:rows] = ids_ref[...].astype(F32)
    meta_ref[8 : 8 + top, 0:rows] = high
    meta_ref[16 : 16 + top, 0:rows] = middle
    meta_ref[24 : 24 + top, 0:rows] = rest - middle
    out_ref[:, width : width + META] = meta_ref[...].T[:rows, :].astype(BF16)
    for copy in copies[4:]:
        copy.wait()


def pack(activations, norm_gain, ids, gates, w_gate_up, *extra):
    rows, width = activations.shape
    assert rows <= META and ids.shape[0] <= 8
    operands = (activations, norm_gain.reshape(1, width), ids, gates, w_gate_up, *extra)
    columns = width + META + sum(x.shape[0] // rows * x.shape[1] for x in extra)
    return pl.pallas_call(
        pack_kernel,
        out_shape=[
            jax.ShapeDtypeStruct((rows, columns), BF16),
            pltpu.VMEM(w_gate_up.shape, BF16),
        ],
        in_specs=[ANY] * len(operands),
        out_specs=[IN_VMEM] * 2,
        scratch_shapes=[
            *(pltpu.VMEM(x.shape, x.dtype) for x in operands[:4]),
            pltpu.VMEM((META, META), F32),
            pltpu.SemaphoreType.DMA((5 + sum(x.shape[0] // rows for x in extra),)),
        ],
        compiler_params=pltpu.CompilerParams(vmem_limit_bytes=VMEM_LIMIT),
        cost_estimate=SHORT,
        name="normalize_and_pack",
    )(*(pltpu.with_memory_space_constraint(x, pltpu.HBM) for x in operands))


def in_vmem(*arrays):
    return [pltpu.with_memory_space_constraint(x, pltpu.VMEM) for x in arrays]


def expert_kernel(top, tok_rows, capacity, sources, targets, *refs):
    inputs = 1 + max(s[0] for group in sources for s in group)
    outputs = 1 + max(t[0] for group in targets for t in group)
    x_hbm = refs[:inputs]
    up_ref, down_hbm = refs[inputs : inputs + 2]
    out_hbm = refs[inputs + 2 : inputs + 2 + outputs]
    (
        x_buf,
        down_buf,
        slot_rows,
        slot_gates,
        places,
        hidden,
        result,
        x_sem,
        down_sem,
        out_sem,
    ) = refs[inputs + 2 + outputs :]
    groups, rows, packed = x_buf.shape
    width = packed - META
    slots = slot_rows.shape[0] // groups
    units = down_buf.shape[0]
    tile = 256
    me = lax.axis_index("seq").astype(F32)

    def loads(group):
        copies, at = [], 0
        for number, (operand, first, count) in enumerate(sources[group]):
            copies.append(
                pltpu.make_async_copy(
                    x_hbm[operand].at[pl.ds(first, count), pl.ds(0, packed)],
                    x_buf.at[group, pl.ds(at, count)],
                    x_sem.at[group, number],
                )
            )
            at += count
        return copies

    def stores(group):
        copies, at = [], 0
        for number, (operand, first, count) in enumerate(targets[group]):
            copies.append(
                pltpu.make_async_copy(
                    x_buf.at[group, pl.ds(at, count), pl.ds(0, width)],
                    out_hbm[operand].at[pl.ds(first, count)],
                    out_sem.at[group, number],
                )
            )
            at += count
        return copies

    for group in range(groups):
        for copy in loads(group):
            copy.start()
    load_down = pltpu.make_async_copy(down_hbm, down_buf, down_sem)
    load_down.start()

    chunk = tok_rows * META // math.gcd(tok_rows, META)
    first = lax.broadcasted_iota(jnp.int32, (chunk, chunk), 0)
    second = lax.broadcasted_iota(jnp.int32, (chunk, chunk), 1)
    earlier = ((first < second) & (first // tok_rows == second // tok_rows)).astype(F32).astype(BF16)
    block = lax.broadcasted_iota(jnp.int32, (1, rows), 1) // tok_rows
    for group in range(groups):
        for copy in loads(group):
            copy.wait()
        meta = x_buf[group, :, width:].astype(F32).T
        gate = jnp.zeros((1, rows), F32)
        named = jnp.zeros((1, rows), F32)
        for k in range(top):
            match = meta[k : k + 1] == me
            value = meta[8 + k : 9 + k] + (meta[16 + k : 17 + k] + meta[24 + k : 25 + k])
            gate = jnp.where(match, value, gate)
            named = jnp.where(match, 1.0, named)
        marks = jnp.broadcast_to(named, (8, rows)).astype(BF16)
        rank = jnp.concatenate(
            [dot(marks[:, at : at + chunk], earlier) for at in range(0, rows, chunk)], axis=1
        )[0:1]
        slot = jnp.where(named > 0.0, (block * capacity).astype(F32) + rank, -1.0)
        spots = lax.broadcasted_iota(jnp.int32, (slots, rows), 0).astype(F32)
        chosen = spots == slot
        slot_gates[pl.ds(group * slots, slots)] = jnp.broadcast_to(
            jnp.sum(jnp.where(chosen, gate, 0.0), axis=1, keepdims=True), (slots, META)
        )
        pick = chosen.astype(F32).astype(BF16)
        for at in range(0, width, 512):
            slot_rows[pl.ds(group * slots, slots), at : at + 512] = dot(
                pick, x_buf[group, :, at : at + 512]
            ).astype(BF16)
        by_row = jnp.broadcast_to(slot, (META, rows)).T
        spots = lax.broadcasted_iota(jnp.int32, (rows, META), 1).astype(F32)
        places[group] = (spots == by_row).astype(F32).astype(BF16)

    for at in range(0, units, tile):
        gate = dot(slot_rows[...], up_ref[:, at : at + tile])
        up = dot(slot_rows[...], up_ref[:, units + at : units + at + tile])
        hidden[:, at : at + tile] = (gate / (1.0 + jnp.exp(-gate)) * up).astype(BF16)
    load_down.wait()
    for at in range(0, width, tile):
        out = dot(hidden[...], down_buf[:, at : at + tile]).astype(BF16).astype(F32)
        result[:, at : at + tile] = (out * slot_gates[:, 0:1]).astype(BF16)
    for group in range(groups):
        for at in range(0, width, 512):
            x_buf[group, :, at : at + 512] = dot(
                places[group, :, :slots], result[pl.ds(group * slots, slots), at : at + 512]
            ).astype(BF16)
        for copy in stores(group):
            copy.start()
    for group in range(groups):
        for copy in stores(group):
            copy.wait()


def run_experts(arrays, sources, targets, out_rows, w_gate_up, w_down, top, tok_rows, capacity):
    groups = len(sources)
    rows = sum(count for _, _, count in sources[0])
    total = groups * rows
    units, width = w_down.shape
    packed = width + META
    slots = rows // tok_rows * capacity
    assert slots % 16 == 0 and slots <= META and units % 256 == 0 and width % 512 == 0
    all_slots = groups * slots
    (w_gate_up,) = in_vmem(w_gate_up)
    held = 2 * units * width + 2 * total * (packed + META) + all_slots * (4 * width + 2 * units + 4 * META)
    return pl.pallas_call(
        functools.partial(expert_kernel, top, tok_rows, capacity, sources, targets),
        out_shape=[jax.ShapeDtypeStruct((count, width), BF16) for count in out_rows],
        in_specs=[ANY] * len(arrays) + [IN_VMEM, ANY],
        out_specs=[ANY] * len(out_rows),
        scratch_shapes=[
            pltpu.VMEM((groups, rows, packed), BF16),
            pltpu.VMEM(w_down.shape, BF16),
            pltpu.VMEM((all_slots, width), BF16),
            pltpu.VMEM((all_slots, META), F32),
            pltpu.VMEM((groups, rows, META), BF16),
            pltpu.VMEM((all_slots, units), BF16),
            pltpu.VMEM((all_slots, width), BF16),
            pltpu.SemaphoreType.DMA((groups, max(len(s) for s in sources))),
            pltpu.SemaphoreType.DMA(()),
            pltpu.SemaphoreType.DMA((groups, max(len(t) for t in targets))),
        ],
        compiler_params=pltpu.CompilerParams(vmem_limit_bytes=held + 8 * 2**20),
        cost_estimate=SHORT,
        name="experts",
    )(*arrays, w_gate_up, w_down)


def value_kernel(kv_width, devices, *refs):
    x_hbm = refs[: len(devices)]
    key_ref, value_ref, x_buf, weight, sems = refs[len(devices) :]
    rows = x_hbm[0].shape[0]
    width = x_buf.shape[1]
    weight_rows = width // len(devices)
    copies = []
    for number, device in enumerate(devices):
        place = device()
        block = x_hbm[number]
        pairs = [
            (block.at[:, pl.ds(0, width)], x_buf.at[pl.ds(place * rows, rows)]),
            (block.at[:, pl.ds(width + META, kv_width)], key_ref.at[pl.ds(place * rows, rows)]),
        ]
        for part in range(weight_rows // rows):
            pairs.append(
                (
                    block.at[:, pl.ds(width + META + (1 + part) * kv_width, kv_width)],
                    weight.at[pl.ds(place * weight_rows + part * rows, rows)],
                )
            )
        for kind, (source, target) in enumerate(pairs):
            copies.append(pltpu.make_async_copy(source, target, sems.at[kind, number]))
    for copy in copies:
        copy.start()
    for copy in copies:
        copy.wait()
    value_ref[...] = dot(x_buf[...], weight[...]).astype(BF16)


def make_values(arrays, devices, width, kv_width):
    rows = arrays[0].shape[0]
    total = rows * len(devices)
    kinds = 2 + width // total
    kv = jax.ShapeDtypeStruct((total, kv_width), BF16)
    return pl.pallas_call(
        functools.partial(value_kernel, kv_width, devices),
        out_shape=[kv, kv],
        in_specs=[ANY] * len(arrays),
        out_specs=[IN_VMEM] * 2,
        scratch_shapes=[
            pltpu.VMEM((total, width), BF16),
            pltpu.VMEM((width, kv_width), BF16),
            pltpu.SemaphoreType.DMA((kinds, len(devices))),
        ],
        compiler_params=pltpu.CompilerParams(vmem_limit_bytes=VMEM_LIMIT),
        cost_estimate=SHORT,
        name="values",
    )(*arrays)


def attention_kernel(chunk, q_ref, k_ref, v_ref, *refs):
    out_ref = refs[-1]
    q_rows, q_width = q_ref.shape
    heads = q_width // HEAD_DIMENSION
    together = 4
    q_start = lax.axis_index("seq") * q_rows
    factor = math.log2(math.e) / math.sqrt(HEAD_DIMENSION)
    steps = k_ref.shape[0] // chunk
    tall = together * q_rows

    def scored(rows, start):
        scores = lax.dot_general(
            rows, k_ref[pl.ds(start, chunk)], (((1,), (1,)), ((), ())), preferred_element_type=F32
        )
        q_at = q_start + lax.broadcasted_iota(jnp.int32, (q_rows, chunk), 0)
        k_at = start + lax.broadcasted_iota(jnp.int32, (q_rows, chunk), 1)
        bias = jnp.where(q_at >= k_at, 0.0, -1e30)[None]
        return (scores.reshape(together, q_rows, chunk) + bias).reshape(tall, chunk)

    for at in range(0, heads, together):
        rows = jnp.concatenate(
            [
                q_ref[:, h * HEAD_DIMENSION : (h + 1) * HEAD_DIMENSION]
                for h in range(at, at + together)
            ],
            axis=0,
        )

        def one(step, state):
            top_score, run_sum, run_acc = state
            start = pl.multiple_of(step * chunk, chunk)
            scores = scored(rows, start)
            best = jnp.maximum(jnp.max(scores, axis=1, keepdims=True), top_score)
            rescale = jnp.exp2((top_score - best) * factor)
            weights = jnp.exp2((scores - best) * factor)
            total = run_sum * rescale + jnp.sum(weights, axis=1, keepdims=True)
            added = dot(weights.astype(BF16), v_ref[pl.ds(start, chunk)])
            return (best, total, run_acc * rescale + added)

        if steps == 1:
            scores = scored(rows, 0)
            best = jnp.max(scores, axis=1, keepdims=True)
            weights = jnp.exp2((scores - best) * factor)
            total = jnp.sum(weights, axis=1, keepdims=True)
            added = dot(weights.astype(BF16), v_ref[...])
        else:
            best, total, added = lax.fori_loop(
                0,
                (q_start + q_rows + chunk - 1) // chunk,
                one,
                (
                    jnp.full((tall, 1), -1e30, F32),
                    jnp.zeros((tall, 1), F32),
                    jnp.zeros((tall, HEAD_DIMENSION), F32),
                ),
            )
        context = (added / total).astype(BF16)
        for h in range(together):
            out_ref[:, (at + h) * HEAD_DIMENSION : (at + h + 1) * HEAD_DIMENSION] = context[
                h * q_rows : (h + 1) * q_rows
            ]


def attend_part(queries, keys, values, part, parts, context=None):
    q_rows, q_width = queries.shape
    total = keys.shape[0]
    part_width = q_width // parts
    per_kv = parts // KEY_VALUE_HEADS
    chunk = math.gcd(total, 1024)
    before = () if context is None else (context,)
    return pl.pallas_call(
        functools.partial(attention_kernel, chunk),
        grid=(1,),
        out_shape=jax.ShapeDtypeStruct((q_rows, q_width), BF16),
        in_specs=[
            pl.BlockSpec((q_rows, part_width), lambda i: (0, part)),
            pl.BlockSpec((total, HEAD_DIMENSION), lambda i: (0, part // per_kv)),
            pl.BlockSpec((total, HEAD_DIMENSION), lambda i: (0, part // per_kv)),
            *[ANY for _ in before],
        ],
        out_specs=pl.BlockSpec((q_rows, part_width), lambda i: (0, part)),
        input_output_aliases={3: 0} if before else {},
        compiler_params=pltpu.CompilerParams(vmem_limit_bytes=VMEM_LIMIT),
        cost_estimate=SHORT,
        name="attention",
    )(queries, keys, values, *before)


def summed(*terms):
    return sum(term.astype(F32) for term in terms).astype(BF16)


def after(x, *others):
    return lax.optimization_barrier((x, *others))[0]


def on_line(acts, packed, kv_width, queries, w_gate_up, w_down, top, capacity):
    rows, width = acts.shape
    line = [packed, forward(packed), None, None]
    line[2] = forward(line[1])
    line[3] = backward(after(packed, line[1]))
    crossed = [across(x) for x in line]
    arrays = [
        [line[step], crossed[step], other_core(line[step]), other_core(crossed[step])]
        for step in range(LINE)
    ]
    devices = [
        functools.partial(from_device, step, y, core)
        for step in range(LINE)
        for core in range(2)
        for y in range(2)
    ]

    def experts(first, second, before, beside):
        ready = arrays[first] + arrays[second]
        ready = [after(ready[0], *before), *ready[1:]]
        sources = [[(4 * group + i, 0, rows) for i in range(4)] for group in range(2)]
        targets = [[(group, 0, 2 * rows), (2 + group, 0, 2 * rows)] for group in range(2)]
        *keep, send_first, send_second = run_experts(
            ready, sources, targets, [2 * rows] * 4, w_gate_up, w_down, top, rows, capacity
        )
        came_first = other_core(after(send_first, *beside))
        crossing = summed(keep[0][rows:], came_first[rows:])
        came_second = other_core(after(send_second, crossing))
        return keep, (came_first, came_second), send_first

    beside = [crossed[3], crossed[2], arrays[3][2], arrays[2][2]]
    keep, came, send = experts(1, 0, [line[2]], beside)
    near = [(keep[i][:rows], came[i][:rows]) for i in range(2)]
    crossing = [summed(keep[i][rows:], came[i][rows:]) for i in range(2)]
    theirs_near = across(crossing[0])
    keep, came, _ = experts(2, 3, [crossing[0]], [theirs_near])
    far = [summed(keep[i][rows:], came[i][rows:]) for i in range(2)]
    theirs = across(far[0])
    total = summed(*near[0], after(theirs_near, far[0]))
    moving = forward(total)
    total = summed(keep[0][:rows], came[0][:rows], theirs, moving)
    moving = forward(total)
    blocks = sum(arrays, [])
    blocks[0] = after(blocks[0], total)
    new_keys, values = make_values(blocks, devices, width, kv_width)
    theirs = across(after(far[1], theirs))
    total = summed(keep[1][:rows], came[1][:rows], theirs, after(moving, values))
    moving = forward(total)
    theirs = across(after(crossing[1], theirs))
    queries = after(queries, total)
    context = None
    for number in range(4):
        context = attend_part(queries, new_keys, values, number, 4, context)
    layer_out = summed(acts, *near[1], theirs, after(moving, context))
    return context, layer_out


def on_any(
    acts, packed, keys, value_weight, queries, w_gate_up, w_down, top, capacity
):
    rows, width = acts.shape
    gathered = lax.all_gather(packed, "seq", axis=0, tiled=True)
    all_keys = lax.all_gather(keys, "seq", axis=0, tiled=True)
    weight = lax.all_gather(value_weight, "seq", axis=0, tiled=True)
    total = gathered.shape[0]
    part = total // GROUPS
    pieces = [[(0, group * part, part)] for group in range(GROUPS)]
    (partial,) = run_experts(
        [gathered], pieces, pieces, [total], w_gate_up, w_down, top, rows, capacity
    )
    values = dot(gathered[:, :width], weight).astype(BF16)
    context = None
    for part in range(KEY_VALUE_HEADS):
        context = attend_part(queries, all_keys, values, part, KEY_VALUE_HEADS, context)
    combined = lax.psum_scatter(partial, "seq", scatter_dimension=0, tiled=True)
    return context, summed(acts, combined)


def per_device(
    activations, queries, keys, norm_gain, value_weight, expert_ids, gate_weights, w_gate_up, w_down
):
    pos_rows, sequence_count, model_width = activations.shape
    assert sequence_count == 1 and w_down.shape[0] == 1
    top = expert_ids.shape[2]
    devices = lax.axis_size("seq")
    capacity = max(2, 3 * pos_rows * top // (2 * devices))
    acts = activations.reshape(pos_rows, model_width)
    keys = keys.reshape(pos_rows, -1)
    line = devices == 4 * LINE and value_weight.shape[0] % pos_rows == 0
    packed, up_weights = pack(
        acts,
        norm_gain,
        expert_ids.transpose(1, 2, 0).reshape(top, pos_rows),
        gate_weights.transpose(1, 2, 0).reshape(top, pos_rows),
        w_gate_up[0],
        *((keys, value_weight) if line else ()),
    )
    rest = (queries.reshape(pos_rows, -1), up_weights, w_down[0], top, capacity)
    if line:
        context, layer_out = on_line(acts, packed, keys.shape[1], *rest)
    else:
        context, layer_out = on_any(acts, packed, keys, value_weight, *rest)
    return (context.reshape(queries.shape), layer_out.reshape(activations.shape))


def solution(mesh):
    placed = (
        P("seq", "grp", None),
        P("seq", "grp", None),
        P("seq", "grp", None),
        P(),
        P("seq", None),
        P("seq", "grp", None),
        P("seq", "grp", None),
        P("seq", None, None),
        P("seq", None, None),
    )
    return jax.shard_map(
        per_device,
        mesh=mesh,
        in_specs=placed,
        out_specs=(P("seq", "grp", None), P("seq", "grp", None)),
        check_vma=False,
    )
```

```python
import functools
import math

import jax
import jax.numpy as jnp
from jax import lax
from jax.experimental import pallas as pl
from jax.experimental.pallas import tpu as pltpu
from jax.sharding import PartitionSpec as P

QUERY_HEADS = 32
KEY_VALUE_HEADS = 2
HEAD_DIMENSION = 128
GROUPS = 4
META = 128
LINE = 4
VMEM_LIMIT = 24 * 2**20
F32 = jnp.float32
BF16 = jnp.bfloat16
ANY = pl.BlockSpec(memory_space=pl.ANY)
SHORT = pl.CostEstimate(flops=1, bytes_accessed=1, transcendentals=0)
IN_VMEM = pl.BlockSpec(memory_space=pltpu.VMEM)


def dot(a, b):
    return jnp.dot(a, b, preferred_element_type=F32)


RING = (0, 1, 3, 2)


def device_index(place, y, core):
    return (RING[place % LINE] * 2 + y) * 2 + core


def swaps(flip_y, flip_core):
    return [
        (device_index(p, y, c), device_index(p, y ^ flip_y, c ^ flip_core))
        for p in range(LINE)
        for y in range(2)
        for c in range(2)
    ]


def ring_steps(steps):
    return [
        (device_index(p, y, c), device_index(p + steps, y, c))
        for p in range(LINE)
        for y in range(2)
        for c in range(2)
    ]


def forward(x):
    return lax.ppermute(x, "seq", ring_steps(1))


def backward(x):
    return lax.ppermute(x, "seq", ring_steps(LINE - 1))


def across(x):
    return lax.ppermute(x, "seq", swaps(1, 0))


def other_core(x):
    return lax.ppermute(x, "seq", swaps(0, 1))


def from_device(steps, flip_y, flip_core):
    me = lax.axis_index("seq")
    core, y, line = me % 2, me // 2 % 2, me // 4
    place = sum(jnp.where(line == RING[p], p, 0) for p in range(LINE))
    place = (place + LINE - steps) % LINE
    line = sum(jnp.where(place == p, RING[p], 0) for p in range(LINE))
    y = 1 - y if flip_y else y
    core = 1 - core if flip_core else core
    return (line * 2 + y) * 2 + core


def pack_kernel(
    act_ref, gain_ref, ids_ref, gates_ref, key_ref, weight_ref, out_ref, small_ref, meta_ref
):
    width = act_ref.shape[1]
    rows = act_ref.shape[0]
    top = ids_ref.shape[0]
    features = act_ref[...].astype(F32)
    inverse = lax.rsqrt(jnp.mean(features * features, axis=-1, keepdims=True) + 1e-06)
    out_ref[:, :width] = (features * inverse * gain_ref[...]).astype(BF16)
    gates = gates_ref[...]
    high = gates.astype(BF16).astype(F32)
    rest = gates - high
    middle = rest.astype(BF16).astype(F32)
    meta_ref[...] = jnp.zeros_like(meta_ref)
    meta_ref[0:top, 0:rows] = ids_ref[...].astype(F32)
    meta_ref[8 : 8 + top, 0:rows] = high
    meta_ref[16 : 16 + top, 0:rows] = middle
    meta_ref[24 : 24 + top, 0:rows] = rest - middle
    out_ref[:, width:] = meta_ref[...].T[:rows, :].astype(BF16)
    small_ref[:rows] = key_ref[...]
    small_ref[rows:] = weight_ref[...]


def pack(activations, norm_gain, ids, gates, keys, value_weight):
    rows, width = activations.shape
    small_rows = rows + value_weight.shape[0]
    assert rows <= META and ids.shape[0] <= 8
    return pl.pallas_call(
        pack_kernel,
        out_shape=[
            jax.ShapeDtypeStruct((rows, width + META), BF16),
            jax.ShapeDtypeStruct((small_rows, keys.shape[1]), BF16),
        ],
        scratch_shapes=[pltpu.VMEM((META, META), F32)],
        cost_estimate=SHORT,
        name="normalize_and_pack",
    )(activations, norm_gain.reshape(1, width), ids, gates, keys, value_weight)


def hold_kernel(small_ref, up_ref, down_ref, out_ref):
    out_ref[...] = small_ref[...]


def hold(small, weights):
    return pl.pallas_call(
        hold_kernel,
        out_shape=jax.ShapeDtypeStruct(small.shape, small.dtype),
        in_specs=[IN_VMEM] * 3,
        out_specs=IN_VMEM,
        compiler_params=pltpu.CompilerParams(vmem_limit_bytes=4 * 2**20),
        cost_estimate=SHORT,
        name="hold_weights",
    )(small, *weights)


def in_vmem(*arrays):
    return [pltpu.with_memory_space_constraint(x, pltpu.VMEM) for x in arrays]


def expert_kernel(top, tok_rows, capacity, sources, targets, *refs):
    inputs = 1 + max(s[0] for group in sources for s in group)
    outputs = 1 + max(t[0] for group in targets for t in group)
    x_hbm = refs[:inputs]
    up_ref, down_ref = refs[inputs : inputs + 2]
    out_hbm = refs[inputs + 2 : inputs + 2 + outputs]
    (
        x_buf,
        slot_rows,
        slot_gates,
        places,
        hidden,
        result,
        x_sem,
        out_sem,
    ) = refs[inputs + 2 + outputs :]
    groups, rows, packed = x_buf.shape
    width = packed - META
    slots = slot_rows.shape[0] // groups
    units = down_ref.shape[0]
    tile = 256
    me = lax.axis_index("seq").astype(F32)

    def loads(group):
        copies, at = [], 0
        for number, (operand, first, count) in enumerate(sources[group]):
            copies.append(
                pltpu.make_async_copy(
                    x_hbm[operand].at[pl.ds(first, count)],
                    x_buf.at[group, pl.ds(at, count)],
                    x_sem.at[group, number],
                )
            )
            at += count
        return copies

    def stores(group):
        copies, at = [], 0
        for number, (operand, first, count) in enumerate(targets[group]):
            copies.append(
                pltpu.make_async_copy(
                    x_buf.at[group, pl.ds(at, count), pl.ds(0, width)],
                    out_hbm[operand].at[pl.ds(first, count)],
                    out_sem.at[group, number],
                )
            )
            at += count
        return copies

    for group in range(groups):
        for copy in loads(group):
            copy.start()

    chunk = tok_rows * META // math.gcd(tok_rows, META)
    first = lax.broadcasted_iota(jnp.int32, (chunk, chunk), 0)
    second = lax.broadcasted_iota(jnp.int32, (chunk, chunk), 1)
    earlier = ((first < second) & (first // tok_rows == second // tok_rows)).astype(F32).astype(BF16)
    block = lax.broadcasted_iota(jnp.int32, (1, rows), 1) // tok_rows
    for group in range(groups):
        for copy in loads(group):
            copy.wait()
        meta = x_buf[group, :, width:].astype(F32).T
        gate = jnp.zeros((1, rows), F32)
        named = jnp.zeros((1, rows), F32)
        for k in range(top):
            match = meta[k : k + 1] == me
            value = meta[8 + k : 9 + k] + (meta[16 + k : 17 + k] + meta[24 + k : 25 + k])
            gate = jnp.where(match, value, gate)
            named = jnp.where(match, 1.0, named)
        marks = jnp.broadcast_to(named, (8, rows)).astype(BF16)
        rank = jnp.concatenate(
            [dot(marks[:, at : at + chunk], earlier) for at in range(0, rows, chunk)], axis=1
        )[0:1]
        slot = jnp.where(named > 0.0, (block * capacity).astype(F32) + rank, -1.0)
        spots = lax.broadcasted_iota(jnp.int32, (slots, rows), 0).astype(F32)
        chosen = spots == slot
        slot_gates[pl.ds(group * slots, slots)] = jnp.broadcast_to(
            jnp.sum(jnp.where(chosen, gate, 0.0), axis=1, keepdims=True), (slots, META)
        )
        pick = chosen.astype(F32).astype(BF16)
        for at in range(0, width, 512):
            slot_rows[pl.ds(group * slots, slots), at : at + 512] = dot(
                pick, x_buf[group, :, at : at + 512]
            ).astype(BF16)
        by_row = jnp.broadcast_to(slot, (META, rows)).T
        spots = lax.broadcasted_iota(jnp.int32, (rows, META), 1).astype(F32)
        places[group] = (spots == by_row).astype(F32).astype(BF16)

    for at in range(0, units, tile):
        gate = dot(slot_rows[...], up_ref[:, at : at + tile])
        up = dot(slot_rows[...], up_ref[:, units + at : units + at + tile])
        hidden[:, at : at + tile] = (gate / (1.0 + jnp.exp(-gate)) * up).astype(BF16)
    for at in range(0, width, tile):
        out = dot(hidden[...], down_ref[:, at : at + tile]).astype(BF16).astype(F32)
        result[:, at : at + tile] = (out * slot_gates[:, 0:1]).astype(BF16)
    for group in range(groups):
        for at in range(0, width, 512):
            x_buf[group, :, at : at + 512] = dot(
                places[group, :, :slots], result[pl.ds(group * slots, slots), at : at + 512]
            ).astype(BF16)
        for copy in stores(group):
            copy.start()
    for group in range(groups):
        for copy in stores(group):
            copy.wait()


def run_experts(arrays, sources, targets, out_rows, w_gate_up, w_down, top, tok_rows, capacity):
    groups = len(sources)
    rows = sum(count for _, _, count in sources[0])
    packed = arrays[0].shape[1]
    total = groups * rows
    width = packed - META
    units = w_down.shape[0]
    slots = rows // tok_rows * capacity
    assert slots % 16 == 0 and slots <= META and units % 256 == 0 and width % 512 == 0
    all_slots = groups * slots
    weights = in_vmem(w_gate_up, w_down)
    held = 2 * total * (packed + META) + all_slots * (4 * width + 2 * units + 4 * META)
    return pl.pallas_call(
        functools.partial(expert_kernel, top, tok_rows, capacity, sources, targets),
        out_shape=[jax.ShapeDtypeStruct((count, width), BF16) for count in out_rows],
        in_specs=[ANY] * len(arrays) + [IN_VMEM] * 2,
        out_specs=[ANY] * len(out_rows),
        scratch_shapes=[
            pltpu.VMEM((groups, rows, packed), BF16),
            pltpu.VMEM((all_slots, width), BF16),
            pltpu.VMEM((all_slots, META), F32),
            pltpu.VMEM((groups, rows, META), BF16),
            pltpu.VMEM((all_slots, units), BF16),
            pltpu.VMEM((all_slots, width), BF16),
            pltpu.SemaphoreType.DMA((groups, max(len(s) for s in sources))),
            pltpu.SemaphoreType.DMA((groups, max(len(t) for t in targets))),
        ],
        compiler_params=pltpu.CompilerParams(vmem_limit_bytes=held + 8 * 2**20),
        cost_estimate=SHORT,
        name="experts",
    )(*arrays, *weights)


def value_kernel(key_rows, blocks, small_blocks, *refs):
    inputs = 1 + max(b[0] for b in blocks)
    smalls = 1 + max(b[0] for b in small_blocks)
    x_hbm = refs[:inputs]
    small_hbm = refs[inputs : inputs + smalls]
    key_ref, value_ref, x_buf, weight, sems = refs[inputs + smalls :]
    width = x_buf.shape[1]
    weight_rows = width // len(small_blocks)
    copies = []
    for number, (operand, first, device) in enumerate(blocks):
        copies.append(
            pltpu.make_async_copy(
                x_hbm[operand].at[pl.ds(first, key_rows), pl.ds(0, width)],
                x_buf.at[pl.ds(device() * key_rows, key_rows)],
                sems.at[0, number],
            )
        )
    for number, (operand, first, device) in enumerate(small_blocks):
        place = device()
        copies.append(
            pltpu.make_async_copy(
                small_hbm[operand].at[pl.ds(first, key_rows)],
                key_ref.at[pl.ds(place * key_rows, key_rows)],
                sems.at[1, number],
            )
        )
        copies.append(
            pltpu.make_async_copy(
                small_hbm[operand].at[pl.ds(first + key_rows, weight_rows)],
                weight.at[pl.ds(place * weight_rows, weight_rows)],
                sems.at[2, number],
            )
        )
    for copy in copies:
        copy.start()
    for copy in copies:
        copy.wait()
    value_ref[...] = dot(x_buf[...], weight[...]).astype(BF16)


def make_values(arrays, blocks, smalls, small_blocks, key_rows, width, earlier):
    smalls = [after(smalls[0], *earlier), *smalls[1:]]
    kv_width = smalls[0].shape[1]
    total = key_rows * len(blocks)
    kv = jax.ShapeDtypeStruct((total, kv_width), BF16)
    return pl.pallas_call(
        functools.partial(value_kernel, key_rows, blocks, small_blocks),
        out_shape=[kv, kv],
        in_specs=[ANY] * (len(arrays) + len(smalls)),
        out_specs=[IN_VMEM] * 2,
        scratch_shapes=[
            pltpu.VMEM((total, width), BF16),
            pltpu.VMEM((width, kv_width), BF16),
            pltpu.SemaphoreType.DMA((3, len(blocks))),
        ],
        compiler_params=pltpu.CompilerParams(vmem_limit_bytes=VMEM_LIMIT),
        cost_estimate=SHORT,
        name="values",
    )(*arrays, *smalls)


def attention_kernel(chunk, q_ref, k_ref, v_ref, *refs):
    out_ref = refs[-1]
    q_rows, q_width = q_ref.shape
    heads = q_width // HEAD_DIMENSION
    together = 4
    q_start = lax.axis_index("seq") * q_rows
    factor = math.log2(math.e) / math.sqrt(HEAD_DIMENSION)
    steps = k_ref.shape[0] // chunk
    tall = together * q_rows

    def scored(rows, start):
        scores = lax.dot_general(
            rows, k_ref[pl.ds(start, chunk)], (((1,), (1,)), ((), ())), preferred_element_type=F32
        )
        q_at = q_start + lax.broadcasted_iota(jnp.int32, (q_rows, chunk), 0)
        k_at = start + lax.broadcasted_iota(jnp.int32, (q_rows, chunk), 1)
        bias = jnp.where(q_at >= k_at, 0.0, -1e30)[None]
        return (scores.reshape(together, q_rows, chunk) + bias).reshape(tall, chunk)

    for at in range(0, heads, together):
        rows = jnp.concatenate(
            [
                q_ref[:, h * HEAD_DIMENSION : (h + 1) * HEAD_DIMENSION]
                for h in range(at, at + together)
            ],
            axis=0,
        )

        def one(step, state):
            top_score, run_sum, run_acc = state
            start = pl.multiple_of(step * chunk, chunk)
            scores = scored(rows, start)
            best = jnp.maximum(jnp.max(scores, axis=1, keepdims=True), top_score)
            rescale = jnp.exp2((top_score - best) * factor)
            weights = jnp.exp2((scores - best) * factor)
            total = run_sum * rescale + jnp.sum(weights, axis=1, keepdims=True)
            added = dot(weights.astype(BF16), v_ref[pl.ds(start, chunk)])
            return (best, total, run_acc * rescale + added)

        if steps == 1:
            scores = scored(rows, 0)
            best = jnp.max(scores, axis=1, keepdims=True)
            weights = jnp.exp2((scores - best) * factor)
            total = jnp.sum(weights, axis=1, keepdims=True)
            added = dot(weights.astype(BF16), v_ref[...])
        else:
            best, total, added = lax.fori_loop(
                0,
                (q_start + q_rows + chunk - 1) // chunk,
                one,
                (
                    jnp.full((tall, 1), -1e30, F32),
                    jnp.zeros((tall, 1), F32),
                    jnp.zeros((tall, HEAD_DIMENSION), F32),
                ),
            )
        context = (added / total).astype(BF16)
        for h in range(together):
            out_ref[:, (at + h) * HEAD_DIMENSION : (at + h + 1) * HEAD_DIMENSION] = context[
                h * q_rows : (h + 1) * q_rows
            ]


def attend_part(queries, keys, values, part, parts, context=None):
    q_rows, q_width = queries.shape
    total = keys.shape[0]
    part_width = q_width // parts
    per_kv = parts // KEY_VALUE_HEADS
    chunk = math.gcd(total, 1024)
    before = () if context is None else (context,)
    return pl.pallas_call(
        functools.partial(attention_kernel, chunk),
        grid=(1,),
        out_shape=jax.ShapeDtypeStruct((q_rows, q_width), BF16),
        in_specs=[
            pl.BlockSpec((q_rows, part_width), lambda i: (0, part)),
            pl.BlockSpec((total, HEAD_DIMENSION), lambda i: (0, part // per_kv)),
            pl.BlockSpec((total, HEAD_DIMENSION), lambda i: (0, part // per_kv)),
            *[ANY for _ in before],
        ],
        out_specs=pl.BlockSpec((q_rows, part_width), lambda i: (0, part)),
        input_output_aliases={3: 0} if before else {},
        compiler_params=pltpu.CompilerParams(vmem_limit_bytes=VMEM_LIMIT),
        cost_estimate=SHORT,
        name="attention",
    )(queries, keys, values, *before)


def summed(*terms):
    return sum(term.astype(F32) for term in terms).astype(BF16)


def after(x, *others):
    return lax.optimization_barrier((x, *others))[0]


def on_line(acts, packed, small, queries, w_gate_up, w_down, top, capacity):
    rows, width = acts.shape
    line = [packed, forward(packed), None, None]
    line[3] = backward(after(packed, line[1]))
    crossed = [across(packed), across(line[1]), None, across(line[3])]
    to_core = other_core(packed)
    small = hold(after(small, to_core), in_vmem(w_gate_up, w_down))
    pair = jnp.concatenate([small, across(small)], axis=0)
    line[2] = forward(after(line[1], pair, crossed[0]))
    crossed[2] = across(line[2])
    arrays = [
        [
            line[step],
            crossed[step],
            other_core(line[step]) if step else to_core,
            other_core(crossed[step]),
        ]
        for step in range(LINE)
    ]
    blocks = [
        (4 * step + core * 2 + y, 0, functools.partial(from_device, step, y, core))
        for step in range(LINE)
        for core in range(2)
        for y in range(2)
    ]
    pair = after(pair, line[3])
    pairs = [pair, forward(pair), None, backward(pair)]
    pairs[2] = forward(pairs[1])
    small_rows = small.shape[0]
    small_blocks = [
        (2 * step + core, y * small_rows, functools.partial(from_device, step, y, core))
        for step in range(LINE)
        for core in range(2)
        for y in range(2)
    ]

    keep, mine, crossing = [None] * LINE, [None] * LINE, [None] * LINE

    def experts(first, second, before, beside):
        ready = arrays[first] + arrays[second]
        ready = [after(ready[0], *before), *ready[1:]]
        sources = [[(4 * group + i, 0, rows) for i in range(4)] for group in range(2)]
        targets = [[(group, 0, 2 * rows), (2, group * 2 * rows, 2 * rows)] for group in range(2)]
        keep[first], keep[second], send = run_experts(
            ready,
            sources,
            targets,
            [2 * rows, 2 * rows, 4 * rows],
            w_gate_up,
            w_down,
            top,
            rows,
            capacity,
        )
        came = other_core(after(send, *beside))
        for at, step in ((0, first), (2 * rows, second)):
            mine[step] = (keep[step][:rows], came[at : at + rows])
            crossing[step] = summed(keep[step][rows:], came[at + rows : at + 2 * rows])
        return send

    theirs = [None] * LINE
    ready = [line[2], crossed[3], arrays[3][2], arrays[2][2]]
    experts(1, 0, ready, [crossed[2], pairs[1]])
    theirs[1] = across(crossing[1])
    send = experts(2, 3, [crossing[0], crossing[1]], [theirs[1], pairs[2], pairs[3]])
    total = summed(*mine[1], after(theirs[1], send))
    moving = forward(total)
    smalls = []
    for step in range(LINE):
        smalls += [pairs[step], other_core(after(pairs[step], total))]
    theirs[2], theirs[3] = across(crossing[2]), across(crossing[3])
    new_keys, values = make_values(
        sum(arrays, []), blocks, smalls, small_blocks, rows, width, crossing[2:]
    )
    total = summed(*mine[2], theirs[2], after(moving, values))
    moving = forward(total)
    theirs[0] = across(after(crossing[0], total))
    context = attend_part(after(queries, total), new_keys, values, 0, 4)
    context = attend_part(queries, new_keys, values, 1, 4, context)
    total = summed(*mine[3], theirs[3], after(moving, context))
    moving = forward(total)
    context = attend_part(after(queries, total), new_keys, values, 2, 4, context)
    context = attend_part(queries, new_keys, values, 3, 4, context)
    layer_out = summed(acts, *mine[0], theirs[0], after(moving, context))
    return context, layer_out


def on_any(acts, packed, small, queries, w_gate_up, w_down, top, capacity):
    rows, width = acts.shape
    keys, value_weight = small[:rows], small[rows:]
    gathered = lax.all_gather(packed, "seq", axis=0, tiled=True)
    all_keys = lax.all_gather(keys, "seq", axis=0, tiled=True)
    weight = lax.all_gather(value_weight, "seq", axis=0, tiled=True)
    total = gathered.shape[0]
    part = total // GROUPS
    pieces = [[(0, group * part, part)] for group in range(GROUPS)]
    (partial,) = run_experts(
        [gathered], pieces, pieces, [total], w_gate_up, w_down, top, rows, capacity
    )
    values = dot(gathered[:, :width], weight).astype(BF16)
    context = None
    for part in range(KEY_VALUE_HEADS):
        context = attend_part(queries, all_keys, values, part, KEY_VALUE_HEADS, context)
    combined = lax.psum_scatter(partial, "seq", scatter_dimension=0, tiled=True)
    return context, summed(acts, combined)


def per_device(
    activations, queries, keys, norm_gain, value_weight, expert_ids, gate_weights, w_gate_up, w_down
):
    pos_rows, sequence_count, model_width = activations.shape
    assert sequence_count == 1 and w_down.shape[0] == 1
    top = expert_ids.shape[2]
    devices = lax.axis_size("seq")
    capacity = max(2, 3 * pos_rows * top // (2 * devices))
    acts = activations.reshape(pos_rows, model_width)
    packed, small = pack(
        acts,
        norm_gain,
        expert_ids.transpose(1, 2, 0).reshape(top, pos_rows),
        gate_weights.transpose(1, 2, 0).reshape(top, pos_rows),
        keys.reshape(pos_rows, -1),
        value_weight,
    )
    way = on_line if devices == 4 * LINE else on_any
    context, layer_out = way(
        acts,
        packed,
        small,
        queries.reshape(pos_rows, -1),
        w_gate_up[0],
        w_down[0],
        top,
        capacity,
    )
    return (context.reshape(queries.shape), layer_out.reshape(activations.shape))


def solution(mesh):
    placed = (
        P("seq", "grp", None),
        P("seq", "grp", None),
        P("seq", "grp", None),
        P(),
        P("seq", None),
        P("seq", "grp", None),
        P("seq", "grp", None),
        P("seq", None, None),
        P("seq", None, None),
    )
    return jax.shard_map(
        per_device,
        mesh=mesh,
        in_specs=placed,
        out_specs=(P("seq", "grp", None), P("seq", "grp", None)),
        check_vma=False,
    )
```

```python
import functools
import math

import jax
import jax.numpy as jnp
from jax import lax
from jax.experimental import pallas as pl
from jax.experimental.pallas import tpu as pltpu
from jax.sharding import PartitionSpec as P

QUERY_HEADS = 32
KEY_VALUE_HEADS = 2
HEAD_DIMENSION = 128
GROUPS = 4
META = 128
LINE = 4
VMEM_LIMIT = 24 * 2**20
F32 = jnp.float32
BF16 = jnp.bfloat16
ANY = pl.BlockSpec(memory_space=pl.ANY)
SHORT = pl.CostEstimate(flops=1, bytes_accessed=1, transcendentals=0)
IN_VMEM = pl.BlockSpec(memory_space=pltpu.VMEM)


def dot(a, b):
    return jnp.dot(a, b, preferred_element_type=F32)


RING = (0, 1, 3, 2)


def device_index(place, y, core):
    return (RING[place % LINE] * 2 + y) * 2 + core


def swaps(flip_y, flip_core):
    return [
        (device_index(p, y, c), device_index(p, y ^ flip_y, c ^ flip_core))
        for p in range(LINE)
        for y in range(2)
        for c in range(2)
    ]


def ring_steps(steps):
    return [
        (device_index(p, y, c), device_index(p + steps, y, c))
        for p in range(LINE)
        for y in range(2)
        for c in range(2)
    ]


def forward(x):
    return lax.ppermute(x, "seq", ring_steps(1))


def backward(x):
    return lax.ppermute(x, "seq", ring_steps(LINE - 1))


def across(x):
    return lax.ppermute(x, "seq", swaps(1, 0))


def other_core(x):
    return lax.ppermute(x, "seq", swaps(0, 1))


def from_device(steps, flip_y, flip_core):
    me = lax.axis_index("seq")
    core, y, line = me % 2, me // 2 % 2, me // 4
    place = sum(jnp.where(line == RING[p], p, 0) for p in range(LINE))
    place = (place + LINE - steps) % LINE
    line = sum(jnp.where(place == p, RING[p], 0) for p in range(LINE))
    y = 1 - y if flip_y else y
    core = 1 - core if flip_core else core
    return (line * 2 + y) * 2 + core


def pack_kernel(
    act_ref, gain_ref, ids_ref, gates_ref, key_ref, weight_ref, out_ref, small_ref, meta_ref
):
    width = act_ref.shape[1]
    rows = act_ref.shape[0]
    top = ids_ref.shape[0]
    features = act_ref[...].astype(F32)
    inverse = lax.rsqrt(jnp.mean(features * features, axis=-1, keepdims=True) + 1e-06)
    out_ref[:, :width] = (features * inverse * gain_ref[...]).astype(BF16)
    gates = gates_ref[...]
    high = gates.astype(BF16).astype(F32)
    rest = gates - high
    middle = rest.astype(BF16).astype(F32)
    meta_ref[...] = jnp.zeros_like(meta_ref)
    meta_ref[0:top, 0:rows] = ids_ref[...].astype(F32)
    meta_ref[8 : 8 + top, 0:rows] = high
    meta_ref[16 : 16 + top, 0:rows] = middle
    meta_ref[24 : 24 + top, 0:rows] = rest - middle
    out_ref[:, width:] = meta_ref[...].T[:rows, :].astype(BF16)
    small_ref[:rows] = key_ref[...]
    small_ref[rows:] = weight_ref[...]


def pack(activations, norm_gain, ids, gates, keys, value_weight):
    rows, width = activations.shape
    small_rows = rows + value_weight.shape[0]
    assert rows <= META and ids.shape[0] <= 8
    return pl.pallas_call(
        pack_kernel,
        out_shape=[
            jax.ShapeDtypeStruct((rows, width + META), BF16),
            jax.ShapeDtypeStruct((small_rows, keys.shape[1]), BF16),
        ],
        scratch_shapes=[pltpu.VMEM((META, META), F32)],
        cost_estimate=SHORT,
        name="normalize_and_pack",
    )(activations, norm_gain.reshape(1, width), ids, gates, keys, value_weight)


def hold_kernel(small_ref, up_ref, down_ref, out_ref):
    out_ref[...] = small_ref[...]


def hold(small, weights):
    return pl.pallas_call(
        hold_kernel,
        out_shape=jax.ShapeDtypeStruct(small.shape, small.dtype),
        in_specs=[IN_VMEM] * 3,
        out_specs=IN_VMEM,
        compiler_params=pltpu.CompilerParams(vmem_limit_bytes=4 * 2**20),
        cost_estimate=SHORT,
        name="hold_weights",
    )(small, *weights)


def in_vmem(*arrays):
    return [pltpu.with_memory_space_constraint(x, pltpu.VMEM) for x in arrays]


def expert_kernel(top, tok_rows, capacity, direct, sources, targets, *refs):
    inputs = 1 + max(s[0] for group in sources for s in group)
    outputs = 1 + max(t[0] for group in targets for t in group)
    x_hbm = refs[:inputs]
    up_ref, down_ref = refs[inputs : inputs + 2]
    out_hbm = refs[inputs + 2 : inputs + 2 + outputs]
    slot_rows, slot_gates, places, hidden, result, *rest = refs[inputs + 2 + outputs :]
    groups, rows, _ = places.shape
    units, width = down_ref.shape
    packed = width + META
    slots = slot_rows.shape[0] // groups
    tile = 256
    me = lax.axis_index("seq").astype(F32)
    if direct:

        def read(group, columns):
            return jnp.concatenate(
                [x_hbm[operand][:, columns] for operand, _, _ in sources[group]], axis=0
            )

        def write(group, columns, value):
            at = 0
            for operand, first, count in targets[group]:
                out_hbm[operand][first : first + count, columns] = value[at : at + count]
                at += count

    else:
        x_buf, x_sem, out_sem = rest

        def read(group, columns):
            return x_buf[group, :, columns]

        def write(group, columns, value):
            x_buf[group, :, columns] = value

    def loads(group):
        copies, at = [], 0
        for number, (operand, first, count) in enumerate([] if direct else sources[group]):
            copies.append(
                pltpu.make_async_copy(
                    x_hbm[operand].at[pl.ds(first, count)],
                    x_buf.at[group, pl.ds(at, count)],
                    x_sem.at[group, number],
                )
            )
            at += count
        return copies

    def stores(group):
        copies, at = [], 0
        for number, (operand, first, count) in enumerate([] if direct else targets[group]):
            copies.append(
                pltpu.make_async_copy(
                    x_buf.at[group, pl.ds(at, count), pl.ds(0, width)],
                    out_hbm[operand].at[pl.ds(first, count)],
                    out_sem.at[group, number],
                )
            )
            at += count
        return copies

    for group in range(groups):
        for copy in loads(group):
            copy.start()

    chunk = tok_rows * META // math.gcd(tok_rows, META)
    first = lax.broadcasted_iota(jnp.int32, (chunk, chunk), 0)
    second = lax.broadcasted_iota(jnp.int32, (chunk, chunk), 1)
    earlier = ((first < second) & (first // tok_rows == second // tok_rows)).astype(F32).astype(BF16)
    block = lax.broadcasted_iota(jnp.int32, (1, rows), 1) // tok_rows
    for group in range(groups):
        for copy in loads(group):
            copy.wait()
        meta = read(group, slice(width, packed)).astype(F32).T
        gate = jnp.zeros((1, rows), F32)
        named = jnp.zeros((1, rows), F32)
        for k in range(top):
            match = meta[k : k + 1] == me
            value = meta[8 + k : 9 + k] + (meta[16 + k : 17 + k] + meta[24 + k : 25 + k])
            gate = jnp.where(match, value, gate)
            named = jnp.where(match, 1.0, named)
        marks = jnp.broadcast_to(named, (8, rows)).astype(BF16)
        rank = jnp.concatenate(
            [dot(marks[:, at : at + chunk], earlier) for at in range(0, rows, chunk)], axis=1
        )[0:1]
        slot = jnp.where(named > 0.0, (block * capacity).astype(F32) + rank, -1.0)
        spots = lax.broadcasted_iota(jnp.int32, (slots, rows), 0).astype(F32)
        chosen = spots == slot
        slot_gates[pl.ds(group * slots, slots)] = jnp.broadcast_to(
            jnp.sum(jnp.where(chosen, gate, 0.0), axis=1, keepdims=True), (slots, META)
        )
        pick = chosen.astype(F32).astype(BF16)
        for at in range(0, width, 512):
            slot_rows[pl.ds(group * slots, slots), at : at + 512] = dot(
                pick, read(group, slice(at, at + 512))
            ).astype(BF16)
        by_row = jnp.broadcast_to(slot, (META, rows)).T
        spots = lax.broadcasted_iota(jnp.int32, (rows, META), 1).astype(F32)
        places[group] = (spots == by_row).astype(F32).astype(BF16)

    for at in range(0, units, tile):
        gate = dot(slot_rows[...], up_ref[:, at : at + tile])
        up = dot(slot_rows[...], up_ref[:, units + at : units + at + tile])
        hidden[:, at : at + tile] = (gate / (1.0 + jnp.exp(-gate)) * up).astype(BF16)
    for at in range(0, width, tile):
        out = dot(hidden[...], down_ref[:, at : at + tile]).astype(BF16).astype(F32)
        result[:, at : at + tile] = (out * slot_gates[:, 0:1]).astype(BF16)
    for group in range(groups):
        for at in range(0, width, 512):
            placed = dot(
                places[group, :, :slots], result[pl.ds(group * slots, slots), at : at + 512]
            )
            write(group, slice(at, at + 512), placed.astype(BF16))
        for copy in stores(group):
            copy.start()
    for group in range(groups):
        for copy in stores(group):
            copy.wait()


def run_experts(arrays, sources, targets, out_rows, w_gate_up, w_down, top, tok_rows, capacity):
    direct = len(arrays) > 1
    groups = len(sources)
    rows = sum(count for _, _, count in sources[0])
    total = groups * rows
    units, width = w_down.shape
    packed = width + META
    slots = rows // tok_rows * capacity
    assert slots % 16 == 0 and slots <= META and units % 256 == 0 and width % 512 == 0
    all_slots = groups * slots
    held = 2 * total * (packed + META) + all_slots * (4 * width + 2 * units + 4 * META)
    scratch = [
        pltpu.VMEM((all_slots, width), BF16),
        pltpu.VMEM((all_slots, META), F32),
        pltpu.VMEM((groups, rows, META), BF16),
        pltpu.VMEM((all_slots, units), BF16),
        pltpu.VMEM((all_slots, width), BF16),
    ]
    if not direct:
        scratch += [
            pltpu.VMEM((groups, rows, packed), BF16),
            pltpu.SemaphoreType.DMA((groups, max(len(s) for s in sources))),
            pltpu.SemaphoreType.DMA((groups, max(len(t) for t in targets))),
        ]
    shape = pltpu.VMEM if direct else jax.ShapeDtypeStruct
    place = IN_VMEM if direct else ANY
    return pl.pallas_call(
        functools.partial(expert_kernel, top, tok_rows, capacity, direct, sources, targets),
        out_shape=[shape((count, width), BF16) for count in out_rows],
        in_specs=[place] * len(arrays) + [IN_VMEM] * 2,
        out_specs=[place] * len(out_rows),
        scratch_shapes=scratch,
        compiler_params=pltpu.CompilerParams(vmem_limit_bytes=held + 8 * 2**20),
        cost_estimate=SHORT,
        name="experts",
    )(*(in_vmem(*arrays) if direct else arrays), *in_vmem(w_gate_up, w_down))


def value_kernel(key_rows, blocks, small_blocks, *refs):
    inputs = 1 + max(b[0] for b in blocks)
    smalls = 1 + max(b[0] for b in small_blocks)
    x_hbm = refs[:inputs]
    small_hbm = refs[inputs : inputs + smalls]
    key_ref, value_ref, x_buf, weight, sems = refs[inputs + smalls :]
    width = x_buf.shape[1]
    weight_rows = width // len(small_blocks)
    copies = []
    for number, (operand, first, device) in enumerate(blocks):
        copies.append(
            pltpu.make_async_copy(
                x_hbm[operand].at[pl.ds(first, key_rows), pl.ds(0, width)],
                x_buf.at[pl.ds(device() * key_rows, key_rows)],
                sems.at[0, number],
            )
        )
    for number, (operand, first, device) in enumerate(small_blocks):
        place = device()
        copies.append(
            pltpu.make_async_copy(
                small_hbm[operand].at[pl.ds(first, key_rows)],
                key_ref.at[pl.ds(place * key_rows, key_rows)],
                sems.at[1, number],
            )
        )
        copies.append(
            pltpu.make_async_copy(
                small_hbm[operand].at[pl.ds(first + key_rows, weight_rows)],
                weight.at[pl.ds(place * weight_rows, weight_rows)],
                sems.at[2, number],
            )
        )
    for copy in copies:
        copy.start()
    for copy in copies:
        copy.wait()
    value_ref[...] = dot(x_buf[...], weight[...]).astype(BF16)


def make_values(arrays, blocks, smalls, small_blocks, key_rows, width, earlier):
    smalls = [after(smalls[0], *earlier), *smalls[1:]]
    kv_width = smalls[0].shape[1]
    total = key_rows * len(blocks)
    kv = jax.ShapeDtypeStruct((total, kv_width), BF16)
    return pl.pallas_call(
        functools.partial(value_kernel, key_rows, blocks, small_blocks),
        out_shape=[kv, kv],
        in_specs=[ANY] * (len(arrays) + len(smalls)),
        out_specs=[IN_VMEM] * 2,
        scratch_shapes=[
            pltpu.VMEM((total, width), BF16),
            pltpu.VMEM((width, kv_width), BF16),
            pltpu.SemaphoreType.DMA((3, len(blocks))),
        ],
        compiler_params=pltpu.CompilerParams(vmem_limit_bytes=VMEM_LIMIT),
        cost_estimate=SHORT,
        name="values",
    )(*arrays, *smalls)


def attention_kernel(chunk, q_ref, k_ref, v_ref, *refs):
    out_ref = refs[-1]
    q_rows, q_width = q_ref.shape
    heads = q_width // HEAD_DIMENSION
    together = 4
    q_start = lax.axis_index("seq") * q_rows
    factor = math.log2(math.e) / math.sqrt(HEAD_DIMENSION)
    steps = k_ref.shape[0] // chunk
    tall = together * q_rows

    def scored(rows, start):
        scores = lax.dot_general(
            rows, k_ref[pl.ds(start, chunk)], (((1,), (1,)), ((), ())), preferred_element_type=F32
        )
        q_at = q_start + lax.broadcasted_iota(jnp.int32, (q_rows, chunk), 0)
        k_at = start + lax.broadcasted_iota(jnp.int32, (q_rows, chunk), 1)
        bias = jnp.where(q_at >= k_at, 0.0, -1e30)[None]
        return (scores.reshape(together, q_rows, chunk) + bias).reshape(tall, chunk)

    for at in range(0, heads, together):
        rows = jnp.concatenate(
            [
                q_ref[:, h * HEAD_DIMENSION : (h + 1) * HEAD_DIMENSION]
                for h in range(at, at + together)
            ],
            axis=0,
        )

        def one(step, state):
            top_score, run_sum, run_acc = state
            start = pl.multiple_of(step * chunk, chunk)
            scores = scored(rows, start)
            best = jnp.maximum(jnp.max(scores, axis=1, keepdims=True), top_score)
            rescale = jnp.exp2((top_score - best) * factor)
            weights = jnp.exp2((scores - best) * factor)
            total = run_sum * rescale + jnp.sum(weights, axis=1, keepdims=True)
            added = dot(weights.astype(BF16), v_ref[pl.ds(start, chunk)])
            return (best, total, run_acc * rescale + added)

        if steps == 1:
            scores = scored(rows, 0)
            best = jnp.max(scores, axis=1, keepdims=True)
            weights = jnp.exp2((scores - best) * factor)
            total = jnp.sum(weights, axis=1, keepdims=True)
            added = dot(weights.astype(BF16), v_ref[...])
        else:
            best, total, added = lax.fori_loop(
                0,
                (q_start + q_rows + chunk - 1) // chunk,
                one,
                (
                    jnp.full((tall, 1), -1e30, F32),
                    jnp.zeros((tall, 1), F32),
                    jnp.zeros((tall, HEAD_DIMENSION), F32),
                ),
            )
        context = (added / total).astype(BF16)
        for h in range(together):
            out_ref[:, (at + h) * HEAD_DIMENSION : (at + h + 1) * HEAD_DIMENSION] = context[
                h * q_rows : (h + 1) * q_rows
            ]


def attend_part(queries, keys, values, part, parts, context=None):
    q_rows, q_width = queries.shape
    total = keys.shape[0]
    part_width = q_width // parts
    per_kv = parts // KEY_VALUE_HEADS
    chunk = math.gcd(total, 1024)
    before = () if context is None else (context,)
    return pl.pallas_call(
        functools.partial(attention_kernel, chunk),
        grid=(1,),
        out_shape=jax.ShapeDtypeStruct((q_rows, q_width), BF16),
        in_specs=[
            pl.BlockSpec((q_rows, part_width), lambda i: (0, part)),
            pl.BlockSpec((total, HEAD_DIMENSION), lambda i: (0, part // per_kv)),
            pl.BlockSpec((total, HEAD_DIMENSION), lambda i: (0, part // per_kv)),
            *[ANY for _ in before],
        ],
        out_specs=pl.BlockSpec((q_rows, part_width), lambda i: (0, part)),
        input_output_aliases={3: 0} if before else {},
        compiler_params=pltpu.CompilerParams(vmem_limit_bytes=VMEM_LIMIT),
        cost_estimate=SHORT,
        name="attention",
    )(queries, keys, values, *before)


def summed(*terms):
    return sum(term.astype(F32) for term in terms).astype(BF16)


def after(x, *others):
    return lax.optimization_barrier((x, *others))[0]


def on_line(acts, packed, small, queries, w_gate_up, w_down, top, capacity):
    rows, width = acts.shape
    line = [packed, forward(packed), None, backward(packed)]
    crossed = [across(packed), across(line[1]), None, across(line[3])]
    to_core = other_core(packed)
    small = hold(after(small, to_core), in_vmem(w_gate_up, w_down))
    pair = jnp.concatenate([small, across(small)], axis=0)
    line[2] = forward(after(line[1], pair, crossed[0]))
    crossed[2] = across(line[2])
    arrays = [
        [
            line[step],
            crossed[step],
            other_core(line[step]) if step else to_core,
            other_core(crossed[step]),
        ]
        for step in range(LINE)
    ]
    blocks = [
        (4 * step + core * 2 + y, 0, functools.partial(from_device, step, y, core))
        for step in range(LINE)
        for core in range(2)
        for y in range(2)
    ]
    pair = after(pair, line[3])
    pairs = [pair, forward(pair), None, backward(pair)]
    pairs[2] = forward(pairs[1])
    small_rows = small.shape[0]
    small_blocks = [
        (2 * step + core, y * small_rows, functools.partial(from_device, step, y, core))
        for step in range(LINE)
        for core in range(2)
        for y in range(2)
    ]

    keep, mine, crossing = [None] * LINE, [None] * LINE, [None] * LINE

    def experts(first, second, before, beside):
        ready = arrays[first] + arrays[second]
        ready = [after(ready[0], *before), *ready[1:]]
        sources = [[(4 * group + i, 0, rows) for i in range(4)] for group in range(2)]
        targets = [[(group, 0, 2 * rows), (2, group * 2 * rows, 2 * rows)] for group in range(2)]
        keep[first], keep[second], send = run_experts(
            ready,
            sources,
            targets,
            [2 * rows, 2 * rows, 4 * rows],
            w_gate_up,
            w_down,
            top,
            rows,
            capacity,
        )
        came = other_core(after(send, *beside))
        for at, step in ((0, first), (2 * rows, second)):
            mine[step] = (keep[step][:rows], came[at : at + rows])
            crossing[step] = summed(keep[step][rows:], came[at + rows : at + 2 * rows])
        return send

    theirs = [None] * LINE
    experts(1, 0, [line[2], crossed[3]], [crossed[2], pairs[1], pairs[3]])
    theirs[1] = across(crossing[1])
    send = experts(2, 3, [crossing[0], crossing[1]], [theirs[1], pairs[2]])
    total = summed(*mine[1], after(theirs[1], send))
    moving = forward(total)
    smalls = []
    for step in range(LINE):
        smalls += [pairs[step], other_core(after(pairs[step], total))]
    theirs[2], theirs[3] = across(crossing[2]), across(crossing[3])
    new_keys, values = make_values(
        sum(arrays, []), blocks, smalls, small_blocks, rows, width, crossing[2:]
    )
    total = summed(*mine[2], theirs[2], after(moving, values))
    moving = forward(total)
    theirs[0] = across(after(crossing[0], total))
    context = attend_part(after(queries, total), new_keys, values, 0, 4)
    context = attend_part(queries, new_keys, values, 1, 4, context)
    total = summed(*mine[3], theirs[3], after(moving, context))
    moving = forward(total)
    context = attend_part(after(queries, total), new_keys, values, 2, 4, context)
    context = attend_part(queries, new_keys, values, 3, 4, context)
    layer_out = summed(acts, *mine[0], theirs[0], after(moving, context))
    return context, layer_out


def on_any(acts, packed, small, queries, w_gate_up, w_down, top, capacity):
    rows, width = acts.shape
    keys, value_weight = small[:rows], small[rows:]
    gathered = lax.all_gather(packed, "seq", axis=0, tiled=True)
    all_keys = lax.all_gather(keys, "seq", axis=0, tiled=True)
    weight = lax.all_gather(value_weight, "seq", axis=0, tiled=True)
    total = gathered.shape[0]
    part = total // GROUPS
    pieces = [[(0, group * part, part)] for group in range(GROUPS)]
    (partial,) = run_experts(
        [gathered], pieces, pieces, [total], w_gate_up, w_down, top, rows, capacity
    )
    values = dot(gathered[:, :width], weight).astype(BF16)
    context = None
    for part in range(KEY_VALUE_HEADS):
        context = attend_part(queries, all_keys, values, part, KEY_VALUE_HEADS, context)
    combined = lax.psum_scatter(partial, "seq", scatter_dimension=0, tiled=True)
    return context, summed(acts, combined)


def per_device(
    activations, queries, keys, norm_gain, value_weight, expert_ids, gate_weights, w_gate_up, w_down
):
    pos_rows, sequence_count, model_width = activations.shape
    assert sequence_count == 1 and w_down.shape[0] == 1
    top = expert_ids.shape[2]
    devices = lax.axis_size("seq")
    capacity = max(2, 3 * pos_rows * top // (2 * devices))
    acts = activations.reshape(pos_rows, model_width)
    packed, small = pack(
        acts,
        norm_gain,
        expert_ids.transpose(1, 2, 0).reshape(top, pos_rows),
        gate_weights.transpose(1, 2, 0).reshape(top, pos_rows),
        keys.reshape(pos_rows, -1),
        value_weight,
    )
    way = on_line if devices == 4 * LINE else on_any
    context, layer_out = way(
        acts,
        packed,
        small,
        queries.reshape(pos_rows, -1),
        w_gate_up[0],
        w_down[0],
        top,
        capacity,
    )
    return (context.reshape(queries.shape), layer_out.reshape(activations.shape))


def solution(mesh):
    placed = (
        P("seq", "grp", None),
        P("seq", "grp", None),
        P("seq", "grp", None),
        P(),
        P("seq", None),
        P("seq", "grp", None),
        P("seq", "grp", None),
        P("seq", None, None),
        P("seq", None, None),
    )
    return jax.shard_map(
        per_device,
        mesh=mesh,
        in_specs=placed,
        out_specs=(P("seq", "grp", None), P("seq", "grp", None)),
        check_vma=False,
    )
```

```python
import functools
import math

import jax
import jax.numpy as jnp
from jax import lax
from jax.experimental import pallas as pl
from jax.experimental.pallas import tpu as pltpu
from jax.sharding import PartitionSpec as P

QUERY_HEADS = 32
KEY_VALUE_HEADS = 2
HEAD_DIMENSION = 128
GROUPS = 4
META = 128
LINE = 4
VMEM_LIMIT = 24 * 2**20
F32 = jnp.float32
BF16 = jnp.bfloat16
ANY = pl.BlockSpec(memory_space=pl.ANY)
SHORT = pl.CostEstimate(flops=1, bytes_accessed=1, transcendentals=0)
IN_VMEM = pl.BlockSpec(memory_space=pltpu.VMEM)


def dot(a, b):
    return jnp.dot(a, b, preferred_element_type=F32)


RING = (0, 1, 3, 2)


def device_index(place, y, core):
    return (RING[place % LINE] * 2 + y) * 2 + core


def swaps(flip_y, flip_core):
    return [
        (device_index(p, y, c), device_index(p, y ^ flip_y, c ^ flip_core))
        for p in range(LINE)
        for y in range(2)
        for c in range(2)
    ]


def ring_steps(steps):
    return [
        (device_index(p, y, c), device_index(p + steps, y, c))
        for p in range(LINE)
        for y in range(2)
        for c in range(2)
    ]


def forward(x):
    return lax.ppermute(x, "seq", ring_steps(1))


def backward(x):
    return lax.ppermute(x, "seq", ring_steps(LINE - 1))


def across(x):
    return lax.ppermute(x, "seq", swaps(1, 0))


def other_core(x):
    return lax.ppermute(x, "seq", swaps(0, 1))


def from_device(steps, flip_y, flip_core):
    me = lax.axis_index("seq")
    core, y, line = me % 2, me // 2 % 2, me // 4
    place = sum(jnp.where(line == RING[p], p, 0) for p in range(LINE))
    place = (place + LINE - steps) % LINE
    line = sum(jnp.where(place == p, RING[p], 0) for p in range(LINE))
    y = 1 - y if flip_y else y
    core = 1 - core if flip_core else core
    return (line * 2 + y) * 2 + core


def pack_kernel(
    act_ref, gain_ref, ids_ref, gates_ref, key_ref, weight_ref, out_ref, small_ref, meta_ref
):
    width = act_ref.shape[1]
    rows = act_ref.shape[0]
    top = ids_ref.shape[0]
    features = act_ref[...].astype(F32)
    inverse = lax.rsqrt(jnp.mean(features * features, axis=-1, keepdims=True) + 1e-06)
    out_ref[:, :width] = (features * inverse * gain_ref[...]).astype(BF16)
    gates = gates_ref[...]
    high = gates.astype(BF16).astype(F32)
    rest = gates - high
    middle = rest.astype(BF16).astype(F32)
    meta_ref[...] = jnp.zeros_like(meta_ref)
    meta_ref[0:top, 0:rows] = ids_ref[...].astype(F32)
    meta_ref[8 : 8 + top, 0:rows] = high
    meta_ref[16 : 16 + top, 0:rows] = middle
    meta_ref[24 : 24 + top, 0:rows] = rest - middle
    out_ref[:, width:] = meta_ref[...].T[:rows, :].astype(BF16)
    small_ref[:rows] = key_ref[...]
    share = small_ref.shape[0] - rows
    first = 0
    if share < weight_ref.shape[0]:
        first = pl.multiple_of(lax.axis_index("grp") * share, share)
    small_ref[rows:] = weight_ref[pl.ds(first, share)]


def pack(activations, norm_gain, ids, gates, keys, value_weight, planes):
    rows, width = activations.shape
    small_rows = rows + value_weight.shape[0] // planes
    assert rows <= META and ids.shape[0] <= 8
    return pl.pallas_call(
        pack_kernel,
        out_shape=[
            jax.ShapeDtypeStruct((rows, width + META), BF16),
            jax.ShapeDtypeStruct((small_rows, keys.shape[1]), BF16),
        ],
        scratch_shapes=[pltpu.VMEM((META, META), F32)],
        cost_estimate=SHORT,
        name="normalize_and_pack",
    )(activations, norm_gain.reshape(1, width), ids, gates, keys, value_weight)


def hold_kernel(small_ref, up_ref, down_ref, out_ref):
    out_ref[...] = small_ref[...]


def hold(small, weights):
    return pl.pallas_call(
        hold_kernel,
        out_shape=jax.ShapeDtypeStruct(small.shape, small.dtype),
        in_specs=[IN_VMEM] * 3,
        out_specs=IN_VMEM,
        compiler_params=pltpu.CompilerParams(vmem_limit_bytes=4 * 2**20),
        cost_estimate=SHORT,
        name="hold_weights",
    )(small, *weights)


def in_vmem(*arrays):
    return [pltpu.with_memory_space_constraint(x, pltpu.VMEM) for x in arrays]


def expert_kernel(top, tok_rows, capacity, direct, sources, targets, *refs):
    inputs = 1 + max(s[0] for group in sources for s in group)
    outputs = 1 + max(t[0] for group in targets for t in group)
    x_hbm = refs[:inputs]
    up_ref, down_ref = refs[inputs : inputs + 2]
    out_hbm = refs[inputs + 2 : inputs + 2 + outputs]
    slot_rows, slot_gates, places, hidden, result, *rest = refs[inputs + 2 + outputs :]
    groups, rows, _ = places.shape
    units, width = down_ref.shape
    packed = width + META
    slots = slot_rows.shape[0] // groups
    tile = 256
    me = lax.axis_index("seq").astype(F32)
    if direct:

        def read(group, columns):
            return jnp.concatenate(
                [x_hbm[operand][:, columns] for operand, _, _ in sources[group]], axis=0
            )

        def write(group, columns, value):
            at = 0
            for operand, first, count in targets[group]:
                out_hbm[operand][first : first + count, columns] = value[at : at + count]
                at += count

    else:
        x_buf, x_sem, out_sem = rest

        def read(group, columns):
            return x_buf[group, :, columns]

        def write(group, columns, value):
            x_buf[group, :, columns] = value

    def loads(group):
        copies, at = [], 0
        for number, (operand, first, count) in enumerate([] if direct else sources[group]):
            copies.append(
                pltpu.make_async_copy(
                    x_hbm[operand].at[pl.ds(first, count)],
                    x_buf.at[group, pl.ds(at, count)],
                    x_sem.at[group, number],
                )
            )
            at += count
        return copies

    def stores(group):
        copies, at = [], 0
        for number, (operand, first, count) in enumerate([] if direct else targets[group]):
            copies.append(
                pltpu.make_async_copy(
                    x_buf.at[group, pl.ds(at, count), pl.ds(0, width)],
                    out_hbm[operand].at[pl.ds(first, count)],
                    out_sem.at[group, number],
                )
            )
            at += count
        return copies

    for group in range(groups):
        for copy in loads(group):
            copy.start()

    chunk = tok_rows * META // math.gcd(tok_rows, META)
    first = lax.broadcasted_iota(jnp.int32, (chunk, chunk), 0)
    second = lax.broadcasted_iota(jnp.int32, (chunk, chunk), 1)
    earlier = ((first < second) & (first // tok_rows == second // tok_rows)).astype(F32).astype(BF16)
    block = lax.broadcasted_iota(jnp.int32, (1, rows), 1) // tok_rows
    for group in range(groups):
        for copy in loads(group):
            copy.wait()
        meta = read(group, slice(width, packed)).astype(F32).T
        gate = jnp.zeros((1, rows), F32)
        named = jnp.zeros((1, rows), F32)
        for k in range(top):
            match = meta[k : k + 1] == me
            value = meta[8 + k : 9 + k] + (meta[16 + k : 17 + k] + meta[24 + k : 25 + k])
            gate = jnp.where(match, value, gate)
            named = jnp.where(match, 1.0, named)
        marks = jnp.broadcast_to(named, (8, rows)).astype(BF16)
        rank = jnp.concatenate(
            [dot(marks[:, at : at + chunk], earlier) for at in range(0, rows, chunk)], axis=1
        )[0:1]
        slot = jnp.where(named > 0.0, (block * capacity).astype(F32) + rank, -1.0)
        spots = lax.broadcasted_iota(jnp.int32, (slots, rows), 0).astype(F32)
        chosen = spots == slot
        slot_gates[pl.ds(group * slots, slots)] = jnp.broadcast_to(
            jnp.sum(jnp.where(chosen, gate, 0.0), axis=1, keepdims=True), (slots, META)
        )
        pick = chosen.astype(F32).astype(BF16)
        for at in range(0, width, 512):
            slot_rows[pl.ds(group * slots, slots), at : at + 512] = dot(
                pick, read(group, slice(at, at + 512))
            ).astype(BF16)
        by_row = jnp.broadcast_to(slot, (META, rows)).T
        spots = lax.broadcasted_iota(jnp.int32, (rows, META), 1).astype(F32)
        places[group] = (spots == by_row).astype(F32).astype(BF16)

    for at in range(0, units, tile):
        gate = dot(slot_rows[...], up_ref[:, at : at + tile])
        up = dot(slot_rows[...], up_ref[:, units + at : units + at + tile])
        hidden[:, at : at + tile] = (gate / (1.0 + jnp.exp(-gate)) * up).astype(BF16)
    for at in range(0, width, tile):
        out = dot(hidden[...], down_ref[:, at : at + tile]).astype(BF16).astype(F32)
        result[:, at : at + tile] = (out * slot_gates[:, 0:1]).astype(BF16)
    for group in range(groups):
        for at in range(0, width, 512):
            placed = dot(
                places[group, :, :slots], result[pl.ds(group * slots, slots), at : at + 512]
            )
            write(group, slice(at, at + 512), placed.astype(BF16))
        for copy in stores(group):
            copy.start()
    for group in range(groups):
        for copy in stores(group):
            copy.wait()


def run_experts(arrays, sources, targets, out_rows, w_gate_up, w_down, top, tok_rows, capacity):
    direct = len(arrays) > 1
    groups = len(sources)
    rows = sum(count for _, _, count in sources[0])
    total = groups * rows
    units, width = w_down.shape
    packed = width + META
    slots = rows // tok_rows * capacity
    assert slots % 16 == 0 and slots <= META and units % 256 == 0 and width % 512 == 0
    all_slots = groups * slots
    held = 2 * total * (packed + META) + all_slots * (4 * width + 2 * units + 4 * META)
    scratch = [
        pltpu.VMEM((all_slots, width), BF16),
        pltpu.VMEM((all_slots, META), F32),
        pltpu.VMEM((groups, rows, META), BF16),
        pltpu.VMEM((all_slots, units), BF16),
        pltpu.VMEM((all_slots, width), BF16),
    ]
    if not direct:
        scratch += [
            pltpu.VMEM((groups, rows, packed), BF16),
            pltpu.SemaphoreType.DMA((groups, max(len(s) for s in sources))),
            pltpu.SemaphoreType.DMA((groups, max(len(t) for t in targets))),
        ]
    shape = pltpu.VMEM if direct else jax.ShapeDtypeStruct
    place = IN_VMEM if direct else ANY
    return pl.pallas_call(
        functools.partial(expert_kernel, top, tok_rows, capacity, direct, sources, targets),
        out_shape=[shape((count, width), BF16) for count in out_rows],
        in_specs=[place] * len(arrays) + [IN_VMEM] * 2,
        out_specs=[place] * len(out_rows),
        scratch_shapes=scratch,
        compiler_params=pltpu.CompilerParams(vmem_limit_bytes=held + 8 * 2**20),
        cost_estimate=SHORT,
        name="experts",
    )(*(in_vmem(*arrays) if direct else arrays), *in_vmem(w_gate_up, w_down))


def value_kernel(key_rows, blocks, *refs):
    count = len(blocks)
    x_hbm, smalls = refs[:count], refs[count : count + 4]
    key_ref, value_ref, x_buf, weight, sems = refs[count + 4 :]
    width = x_buf.shape[1]
    share = width // count // 2
    plane = lax.axis_index("grp")
    copies = []
    for number, (operand, at, device) in enumerate(blocks):
        place = device()
        own, other = smalls[number * 2 // count * 2 : number * 2 // count * 2 + 2]
        below = at * (key_rows + share)
        pairs = [
            (x_hbm[operand].at[:, pl.ds(0, width)], x_buf.at[pl.ds(place * key_rows, key_rows)]),
            (own.at[pl.ds(below, key_rows)], key_ref.at[pl.ds(place * key_rows, key_rows)]),
            (
                own.at[pl.ds(below + key_rows, share)],
                weight.at[pl.ds((2 * place + plane) * share, share)],
            ),
            (
                other.at[pl.ds(at * share, share)],
                weight.at[pl.ds((2 * place + 1 - plane) * share, share)],
            ),
        ]
        for kind, (source, target) in enumerate(pairs):
            copies.append(pltpu.make_async_copy(source, target, sems.at[kind, number]))
    for copy in copies:
        copy.start()
    for copy in copies:
        copy.wait()
    value_ref[...] = dot(x_buf[...], weight[...]).astype(BF16)


def make_values(arrays, blocks, smalls, key_rows, width):
    kv_width = smalls[0].shape[1]
    total = key_rows * len(blocks)
    kv = jax.ShapeDtypeStruct((total, kv_width), BF16)
    return pl.pallas_call(
        functools.partial(value_kernel, key_rows, blocks),
        out_shape=[kv, kv],
        in_specs=[ANY] * (len(arrays) + len(smalls)),
        out_specs=[IN_VMEM] * 2,
        scratch_shapes=[
            pltpu.VMEM((total, width), BF16),
            pltpu.VMEM((width, kv_width), BF16),
            pltpu.SemaphoreType.DMA((4, len(blocks))),
        ],
        compiler_params=pltpu.CompilerParams(vmem_limit_bytes=VMEM_LIMIT),
        cost_estimate=SHORT,
        name="values",
    )(*arrays, *smalls)


def attention_kernel(chunk, q_ref, k_ref, v_ref, *refs):
    out_ref = refs[-1]
    q_rows, q_width = q_ref.shape
    heads = q_width // HEAD_DIMENSION
    together = 4
    q_start = lax.axis_index("seq") * q_rows
    factor = math.log2(math.e) / math.sqrt(HEAD_DIMENSION)
    steps = k_ref.shape[0] // chunk
    tall = together * q_rows

    def scored(rows, start):
        scores = lax.dot_general(
            rows, k_ref[pl.ds(start, chunk)], (((1,), (1,)), ((), ())), preferred_element_type=F32
        )
        q_at = q_start + lax.broadcasted_iota(jnp.int32, (q_rows, chunk), 0)
        k_at = start + lax.broadcasted_iota(jnp.int32, (q_rows, chunk), 1)
        bias = jnp.where(q_at >= k_at, 0.0, -1e30)[None]
        return (scores.reshape(together, q_rows, chunk) + bias).reshape(tall, chunk)

    for at in range(0, heads, together):
        rows = jnp.concatenate(
            [
                q_ref[:, h * HEAD_DIMENSION : (h + 1) * HEAD_DIMENSION]
                for h in range(at, at + together)
            ],
            axis=0,
        )

        def one(step, state):
            top_score, run_sum, run_acc = state
            start = pl.multiple_of(step * chunk, chunk)
            scores = scored(rows, start)
            best = jnp.maximum(jnp.max(scores, axis=1, keepdims=True), top_score)
            rescale = jnp.exp2((top_score - best) * factor)
            weights = jnp.exp2((scores - best) * factor)
            total = run_sum * rescale + jnp.sum(weights, axis=1, keepdims=True)
            added = dot(weights.astype(BF16), v_ref[pl.ds(start, chunk)])
            return (best, total, run_acc * rescale + added)

        if steps == 1:
            scores = scored(rows, 0)
            best = jnp.max(scores, axis=1, keepdims=True)
            weights = jnp.exp2((scores - best) * factor)
            total = jnp.sum(weights, axis=1, keepdims=True)
            added = dot(weights.astype(BF16), v_ref[...])
        else:
            best, total, added = lax.fori_loop(
                0,
                (q_start + q_rows + chunk - 1) // chunk,
                one,
                (
                    jnp.full((tall, 1), -1e30, F32),
                    jnp.zeros((tall, 1), F32),
                    jnp.zeros((tall, HEAD_DIMENSION), F32),
                ),
            )
        context = (added / total).astype(BF16)
        for h in range(together):
            out_ref[:, (at + h) * HEAD_DIMENSION : (at + h + 1) * HEAD_DIMENSION] = context[
                h * q_rows : (h + 1) * q_rows
            ]


def attend_part(queries, keys, values, part, parts, context=None):
    q_rows, q_width = queries.shape
    total = keys.shape[0]
    part_width = q_width // parts
    per_kv = parts // KEY_VALUE_HEADS
    chunk = math.gcd(total, 1024)
    before = () if context is None else (context,)
    return pl.pallas_call(
        functools.partial(attention_kernel, chunk),
        grid=(1,),
        out_shape=jax.ShapeDtypeStruct((q_rows, q_width), BF16),
        in_specs=[
            pl.BlockSpec((q_rows, part_width), lambda i: (0, part)),
            pl.BlockSpec((total, HEAD_DIMENSION), lambda i: (0, part // per_kv)),
            pl.BlockSpec((total, HEAD_DIMENSION), lambda i: (0, part // per_kv)),
            *[ANY for _ in before],
        ],
        out_specs=pl.BlockSpec((q_rows, part_width), lambda i: (0, part)),
        input_output_aliases={3: 0} if before else {},
        compiler_params=pltpu.CompilerParams(vmem_limit_bytes=VMEM_LIMIT),
        cost_estimate=SHORT,
        name="attention",
    )(queries, keys, values, *before)


def summed(*terms):
    return sum(term.astype(F32) for term in terms).astype(BF16)


def after(x, *others):
    return lax.optimization_barrier((x, *others))[0]


def on_line(acts, packed, small, queries, w_gate_up, w_down, top, capacity):
    rows, width = acts.shape
    line = [packed, forward(packed), None, backward(packed)]
    crossed = [across(packed), across(line[1]), None, across(line[3])]
    to_core = other_core(packed)
    small = hold(after(small, to_core), in_vmem(w_gate_up, w_down))
    pair = jnp.concatenate([small, across(small)], axis=0)
    line[2] = forward(after(line[1], pair, crossed[0]))
    crossed[2] = across(line[2])
    arrays = [
        [
            line[step],
            crossed[step],
            other_core(line[step]) if step else to_core,
            other_core(crossed[step]),
        ]
        for step in range(LINE)
    ]
    blocks = [
        (4 * step + core * 2 + y, 2 * step + y, functools.partial(from_device, step, y, core))
        for core in range(2)
        for step in range(LINE)
        for y in range(2)
    ]
    pair = after(pair, line[3])
    pairs = [pair, forward(pair), None, backward(pair)]
    pairs[2] = forward(pairs[1])
    keep, mine, crossing = [None] * LINE, [None] * LINE, [None] * LINE

    def experts(first, second, before, beside):
        ready = arrays[first] + arrays[second]
        ready = [after(ready[0], *before), *ready[1:]]
        sources = [[(4 * group + i, 0, rows) for i in range(4)] for group in range(2)]
        targets = [[(group, 0, 2 * rows), (2, group * 2 * rows, 2 * rows)] for group in range(2)]
        keep[first], keep[second], send = run_experts(
            ready,
            sources,
            targets,
            [2 * rows, 2 * rows, 4 * rows],
            w_gate_up,
            w_down,
            top,
            rows,
            capacity,
        )
        came = other_core(after(send, *beside))
        for at, step in ((0, first), (2 * rows, second)):
            mine[step] = (keep[step][:rows], came[at : at + rows])
            crossing[step] = summed(keep[step][rows:], came[at + rows : at + 2 * rows])
        return send

    theirs = [None] * LINE
    experts(1, 0, [line[2], crossed[3]], [crossed[2], pairs[1], pairs[3]])
    theirs[1] = across(crossing[1])
    send = experts(2, 3, [crossing[0], crossing[1]], [theirs[1], pairs[2]])
    total = summed(*mine[1], after(theirs[1], send))
    moving = forward(total)
    theirs[2], theirs[3] = across(crossing[2]), across(crossing[3])
    own = jnp.concatenate(after(tuple(pairs), *crossing[2:], total), axis=0)
    shares = own.reshape(2 * LINE, small.shape[0], -1)[:, rows:]
    other = lax.ppermute(shares.reshape(-1, own.shape[1]), "grp", [(0, 1), (1, 0)])
    total = summed(*mine[2], theirs[2], moving)
    moving = forward(total)
    theirs[0] = across(after(crossing[0], total))
    other = after(other, total)
    smalls = [own, other, other_core(own), other_core(other)]
    new_keys, values = make_values(sum(arrays, []), blocks, smalls, rows, width)
    total = summed(*mine[3], theirs[3], after(moving, values))
    moving = forward(total)
    queries = after(queries, total)
    context = None
    for part in range(4):
        context = attend_part(queries, new_keys, values, part, 4, context)
    layer_out = summed(acts, *mine[0], theirs[0], after(moving, context))
    return context, layer_out


def on_any(acts, packed, small, queries, w_gate_up, w_down, top, capacity):
    rows, width = acts.shape
    keys, value_weight = small[:rows], small[rows:]
    gathered = lax.all_gather(packed, "seq", axis=0, tiled=True)
    all_keys = lax.all_gather(keys, "seq", axis=0, tiled=True)
    weight = lax.all_gather(value_weight, "seq", axis=0, tiled=True)
    total = gathered.shape[0]
    part = total // GROUPS
    pieces = [[(0, group * part, part)] for group in range(GROUPS)]
    (partial,) = run_experts(
        [gathered], pieces, pieces, [total], w_gate_up, w_down, top, rows, capacity
    )
    values = dot(gathered[:, :width], weight).astype(BF16)
    context = None
    for part in range(KEY_VALUE_HEADS):
        context = attend_part(queries, all_keys, values, part, KEY_VALUE_HEADS, context)
    combined = lax.psum_scatter(partial, "seq", scatter_dimension=0, tiled=True)
    return context, summed(acts, combined)


def per_device(
    activations, queries, keys, norm_gain, value_weight, expert_ids, gate_weights, w_gate_up, w_down
):
    pos_rows, sequence_count, model_width = activations.shape
    assert sequence_count == 1 and w_down.shape[0] == 1
    top = expert_ids.shape[2]
    devices = lax.axis_size("seq")
    capacity = max(2, 3 * pos_rows * top // (2 * devices))
    acts = activations.reshape(pos_rows, model_width)
    halves = 2 * devices * pos_rows == model_width and value_weight.shape[0] % (2 * pos_rows) == 0
    line = devices == 4 * LINE and lax.axis_size("grp") == 2 and halves
    packed, small = pack(
        acts,
        norm_gain,
        expert_ids.transpose(1, 2, 0).reshape(top, pos_rows),
        gate_weights.transpose(1, 2, 0).reshape(top, pos_rows),
        keys.reshape(pos_rows, -1),
        value_weight,
        2 if line else 1,
    )
    way = on_line if line else on_any
    context, layer_out = way(
        acts,
        packed,
        small,
        queries.reshape(pos_rows, -1),
        w_gate_up[0],
        w_down[0],
        top,
        capacity,
    )
    return (context.reshape(queries.shape), layer_out.reshape(activations.shape))


def solution(mesh):
    placed = (
        P("seq", "grp", None),
        P("seq", "grp", None),
        P("seq", "grp", None),
        P(),
        P("seq", None),
        P("seq", "grp", None),
        P("seq", "grp", None),
        P("seq", None, None),
        P("seq", None, None),
    )
    return jax.shard_map(
        per_device,
        mesh=mesh,
        in_specs=placed,
        out_specs=(P("seq", "grp", None), P("seq", "grp", None)),
        check_vma=False,
    )
```

```python
import functools
import math

import jax
import jax.numpy as jnp
from jax import lax
from jax.experimental import pallas as pl
from jax.experimental.pallas import tpu as pltpu
from jax.sharding import PartitionSpec as P

QUERY_HEADS = 32
KEY_VALUE_HEADS = 2
HEAD_DIMENSION = 128
GROUPS = 4
META = 128
LINE = 4
VMEM_LIMIT = 24 * 2**20
F32 = jnp.float32
BF16 = jnp.bfloat16
ANY = pl.BlockSpec(memory_space=pl.ANY)
SHORT = pl.CostEstimate(flops=1, bytes_accessed=1, transcendentals=0)
IN_VMEM = pl.BlockSpec(memory_space=pltpu.VMEM)


def dot(a, b):
    return jnp.dot(a, b, preferred_element_type=F32)


RING = (0, 1, 3, 2)


def device_index(place, y, core):
    return (RING[place % LINE] * 2 + y) * 2 + core


def swaps(flip_y, flip_core):
    return [
        (device_index(p, y, c), device_index(p, y ^ flip_y, c ^ flip_core))
        for p in range(LINE)
        for y in range(2)
        for c in range(2)
    ]


def ring_steps(steps):
    return [
        (device_index(p, y, c), device_index(p + steps, y, c))
        for p in range(LINE)
        for y in range(2)
        for c in range(2)
    ]


def forward(x):
    return lax.ppermute(x, "seq", ring_steps(1))


def backward(x):
    return lax.ppermute(x, "seq", ring_steps(LINE - 1))


def across(x):
    return lax.ppermute(x, "seq", swaps(1, 0))


def other_core(x):
    return lax.ppermute(x, "seq", swaps(0, 1))


def from_device(steps, flip_y, flip_core):
    me = lax.axis_index("seq")
    core, y, line = me % 2, me // 2 % 2, me // 4
    place = sum(jnp.where(line == RING[p], p, 0) for p in range(LINE))
    place = (place + LINE - steps) % LINE
    line = sum(jnp.where(place == p, RING[p], 0) for p in range(LINE))
    y = 1 - y if flip_y else y
    core = 1 - core if flip_core else core
    return (line * 2 + y) * 2 + core


def pack_kernel(
    act_ref, gain_ref, ids_ref, gates_ref, key_ref, weight_ref, out_ref, small_ref, meta_ref
):
    width = act_ref.shape[1]
    rows = act_ref.shape[0]
    top = ids_ref.shape[0]
    features = act_ref[...].astype(F32)
    inverse = lax.rsqrt(jnp.mean(features * features, axis=-1, keepdims=True) + 1e-06)
    out_ref[:, :width] = (features * inverse * gain_ref[...]).astype(BF16)
    gates = gates_ref[...]
    high = gates.astype(BF16).astype(F32)
    rest = gates - high
    middle = rest.astype(BF16).astype(F32)
    meta_ref[...] = jnp.zeros_like(meta_ref)
    meta_ref[0:top, 0:rows] = ids_ref[...].astype(F32)
    meta_ref[8 : 8 + top, 0:rows] = high
    meta_ref[16 : 16 + top, 0:rows] = middle
    meta_ref[24 : 24 + top, 0:rows] = rest - middle
    out_ref[:, width:] = meta_ref[...].T[:rows, :].astype(BF16)
    small_ref[:rows] = key_ref[...]
    share = small_ref.shape[0] - rows
    first = 0
    if share < weight_ref.shape[0]:
        first = pl.multiple_of(lax.axis_index("grp") * share, share)
    small_ref[rows:] = weight_ref[pl.ds(first, share)]


def pack(activations, norm_gain, ids, gates, keys, value_weight, planes):
    rows, width = activations.shape
    small_rows = rows + value_weight.shape[0] // planes
    assert rows <= META and ids.shape[0] <= 8
    return pl.pallas_call(
        pack_kernel,
        out_shape=[
            jax.ShapeDtypeStruct((rows, width + META), BF16),
            jax.ShapeDtypeStruct((small_rows, keys.shape[1]), BF16),
        ],
        scratch_shapes=[pltpu.VMEM((META, META), F32)],
        cost_estimate=SHORT,
        name="normalize_and_pack",
    )(activations, norm_gain.reshape(1, width), ids, gates, keys, value_weight)


def hold_kernel(small_ref, up_ref, down_ref, out_ref):
    out_ref[...] = small_ref[...]


def hold(small, weights):
    return pl.pallas_call(
        hold_kernel,
        out_shape=jax.ShapeDtypeStruct(small.shape, small.dtype),
        in_specs=[IN_VMEM] * 3,
        out_specs=IN_VMEM,
        compiler_params=pltpu.CompilerParams(vmem_limit_bytes=4 * 2**20),
        cost_estimate=SHORT,
        name="hold_weights",
    )(small, *weights)


def in_vmem(*arrays):
    return [pltpu.with_memory_space_constraint(x, pltpu.VMEM) for x in arrays]


def expert_kernel(top, tok_rows, capacity, direct, sources, targets, *refs):
    inputs = 1 + max(s[0] for group in sources for s in group)
    outputs = 1 + max(t[0] for group in targets for t in group)
    x_hbm = refs[:inputs]
    up_ref, down_ref = refs[inputs : inputs + 2]
    out_hbm = refs[inputs + 2 : inputs + 2 + outputs]
    slot_rows, slot_gates, places, hidden, result, *rest = refs[inputs + 2 + outputs :]
    groups, rows, _ = places.shape
    units, width = down_ref.shape
    packed = width + META
    slots = slot_rows.shape[0] // groups
    tile = 256
    me = lax.axis_index("seq").astype(F32)
    if direct:

        def read(group, columns):
            return jnp.concatenate(
                [x_hbm[operand][:, columns] for operand, _, _ in sources[group]], axis=0
            )

        def write(group, columns, value):
            at = 0
            for operand, first, count in targets[group]:
                out_hbm[operand][first : first + count, columns] = value[at : at + count]
                at += count

    else:
        x_buf, x_sem, out_sem = rest

        def read(group, columns):
            return x_buf[group, :, columns]

        def write(group, columns, value):
            x_buf[group, :, columns] = value

    def loads(group):
        copies, at = [], 0
        for number, (operand, first, count) in enumerate([] if direct else sources[group]):
            copies.append(
                pltpu.make_async_copy(
                    x_hbm[operand].at[pl.ds(first, count)],
                    x_buf.at[group, pl.ds(at, count)],
                    x_sem.at[group, number],
                )
            )
            at += count
        return copies

    def stores(group):
        copies, at = [], 0
        for number, (operand, first, count) in enumerate([] if direct else targets[group]):
            copies.append(
                pltpu.make_async_copy(
                    x_buf.at[group, pl.ds(at, count), pl.ds(0, width)],
                    out_hbm[operand].at[pl.ds(first, count)],
                    out_sem.at[group, number],
                )
            )
            at += count
        return copies

    for group in range(groups):
        for copy in loads(group):
            copy.start()

    chunk = tok_rows * META // math.gcd(tok_rows, META)
    first = lax.broadcasted_iota(jnp.int32, (chunk, chunk), 0)
    second = lax.broadcasted_iota(jnp.int32, (chunk, chunk), 1)
    earlier = ((first < second) & (first // tok_rows == second // tok_rows)).astype(F32).astype(BF16)
    block = lax.broadcasted_iota(jnp.int32, (1, rows), 1) // tok_rows
    for group in range(groups):
        for copy in loads(group):
            copy.wait()
        meta = read(group, slice(width, packed)).astype(F32).T
        gate = jnp.zeros((1, rows), F32)
        named = jnp.zeros((1, rows), F32)
        for k in range(top):
            match = meta[k : k + 1] == me
            value = meta[8 + k : 9 + k] + (meta[16 + k : 17 + k] + meta[24 + k : 25 + k])
            gate = jnp.where(match, value, gate)
            named = jnp.where(match, 1.0, named)
        marks = jnp.broadcast_to(named, (8, rows)).astype(BF16)
        rank = jnp.concatenate(
            [dot(marks[:, at : at + chunk], earlier) for at in range(0, rows, chunk)], axis=1
        )[0:1]
        slot = jnp.where(named > 0.0, (block * capacity).astype(F32) + rank, -1.0)
        spots = lax.broadcasted_iota(jnp.int32, (slots, rows), 0).astype(F32)
        chosen = spots == slot
        slot_gates[pl.ds(group * slots, slots)] = jnp.broadcast_to(
            jnp.sum(jnp.where(chosen, gate, 0.0), axis=1, keepdims=True), (slots, META)
        )
        pick = chosen.astype(F32).astype(BF16)
        for at in range(0, width, 512):
            slot_rows[pl.ds(group * slots, slots), at : at + 512] = dot(
                pick, read(group, slice(at, at + 512))
            ).astype(BF16)
        by_row = jnp.broadcast_to(slot, (META, rows)).T
        spots = lax.broadcasted_iota(jnp.int32, (rows, META), 1).astype(F32)
        places[group] = (spots == by_row).astype(F32).astype(BF16)

    for at in range(0, units, tile):
        gate = dot(slot_rows[...], up_ref[:, at : at + tile])
        up = dot(slot_rows[...], up_ref[:, units + at : units + at + tile])
        hidden[:, at : at + tile] = (gate / (1.0 + jnp.exp(-gate)) * up).astype(BF16)
    for at in range(0, width, tile):
        out = dot(hidden[...], down_ref[:, at : at + tile]).astype(BF16).astype(F32)
        result[:, at : at + tile] = (out * slot_gates[:, 0:1]).astype(BF16)
    for group in range(groups):
        for at in range(0, width, 512):
            placed = dot(
                places[group, :, :slots], result[pl.ds(group * slots, slots), at : at + 512]
            )
            write(group, slice(at, at + 512), placed.astype(BF16))
        for copy in stores(group):
            copy.start()
    for group in range(groups):
        for copy in stores(group):
            copy.wait()


def run_experts(arrays, sources, targets, out_rows, w_gate_up, w_down, top, tok_rows, capacity):
    direct = len(arrays) > 1
    groups = len(sources)
    rows = sum(count for _, _, count in sources[0])
    total = groups * rows
    units, width = w_down.shape
    packed = width + META
    slots = rows // tok_rows * capacity
    assert slots % 16 == 0 and slots <= META and units % 256 == 0 and width % 512 == 0
    all_slots = groups * slots
    held = 2 * total * (packed + META) + all_slots * (4 * width + 2 * units + 4 * META)
    scratch = [
        pltpu.VMEM((all_slots, width), BF16),
        pltpu.VMEM((all_slots, META), F32),
        pltpu.VMEM((groups, rows, META), BF16),
        pltpu.VMEM((all_slots, units), BF16),
        pltpu.VMEM((all_slots, width), BF16),
    ]
    if not direct:
        scratch += [
            pltpu.VMEM((groups, rows, packed), BF16),
            pltpu.SemaphoreType.DMA((groups, max(len(s) for s in sources))),
            pltpu.SemaphoreType.DMA((groups, max(len(t) for t in targets))),
        ]
    shape = pltpu.VMEM if direct else jax.ShapeDtypeStruct
    place = IN_VMEM if direct else ANY
    return pl.pallas_call(
        functools.partial(expert_kernel, top, tok_rows, capacity, direct, sources, targets),
        out_shape=[shape((count, width), BF16) for count in out_rows],
        in_specs=[place] * len(arrays) + [IN_VMEM] * 2,
        out_specs=[place] * len(out_rows),
        scratch_shapes=scratch,
        compiler_params=pltpu.CompilerParams(vmem_limit_bytes=held + 8 * 2**20),
        cost_estimate=SHORT,
        name="experts",
    )(*(in_vmem(*arrays) if direct else arrays), *in_vmem(w_gate_up, w_down))


def value_kernel(key_rows, blocks, *refs):
    count = len(blocks)
    x_hbm, smalls = refs[:count], refs[count : count + 4]
    key_ref, value_ref, x_buf, weight, sems = refs[count + 4 :]
    width = x_buf.shape[1]
    share = width // count // 2
    plane = lax.axis_index("grp")
    copies = []
    for number, (operand, at, device) in enumerate(blocks):
        place = device()
        own, other = smalls[number * 2 // count * 2 : number * 2 // count * 2 + 2]
        below = at * (key_rows + share)
        pairs = [
            (x_hbm[operand].at[:, pl.ds(0, width)], x_buf.at[pl.ds(place * key_rows, key_rows)]),
            (own.at[pl.ds(below, key_rows)], key_ref.at[pl.ds(place * key_rows, key_rows)]),
            (
                own.at[pl.ds(below + key_rows, share)],
                weight.at[pl.ds((2 * place + plane) * share, share)],
            ),
            (
                other.at[pl.ds(at * share, share)],
                weight.at[pl.ds((2 * place + 1 - plane) * share, share)],
            ),
        ]
        for kind, (source, target) in enumerate(pairs):
            copies.append(pltpu.make_async_copy(source, target, sems.at[kind, number]))
    for copy in copies:
        copy.start()
    for copy in copies:
        copy.wait()
    value_ref[...] = dot(x_buf[...], weight[...]).astype(BF16)


def make_values(arrays, blocks, smalls, key_rows, width):
    kv_width = smalls[0].shape[1]
    total = key_rows * len(blocks)
    kv = jax.ShapeDtypeStruct((total, kv_width), BF16)
    return pl.pallas_call(
        functools.partial(value_kernel, key_rows, blocks),
        out_shape=[kv, kv],
        in_specs=[ANY] * (len(arrays) + len(smalls)),
        out_specs=[IN_VMEM] * 2,
        scratch_shapes=[
            pltpu.VMEM((total, width), BF16),
            pltpu.VMEM((width, kv_width), BF16),
            pltpu.SemaphoreType.DMA((4, len(blocks))),
        ],
        compiler_params=pltpu.CompilerParams(vmem_limit_bytes=VMEM_LIMIT),
        cost_estimate=SHORT,
        name="values",
    )(*arrays, *smalls)


def attention_kernel(chunk, q_ref, k_ref, v_ref, *refs):
    out_ref = refs[-1]
    q_rows, q_width = q_ref.shape
    heads = q_width // HEAD_DIMENSION
    together = 4
    q_start = lax.axis_index("seq") * q_rows
    factor = math.log2(math.e) / math.sqrt(HEAD_DIMENSION)
    steps = k_ref.shape[0] // chunk
    tall = together * q_rows

    def scored(rows, start):
        scores = lax.dot_general(
            rows, k_ref[pl.ds(start, chunk)], (((1,), (1,)), ((), ())), preferred_element_type=F32
        )
        q_at = q_start + lax.broadcasted_iota(jnp.int32, (q_rows, chunk), 0)
        k_at = start + lax.broadcasted_iota(jnp.int32, (q_rows, chunk), 1)
        bias = jnp.where(q_at >= k_at, 0.0, -1e30)[None]
        return (scores.reshape(together, q_rows, chunk) + bias).reshape(tall, chunk)

    for at in range(0, heads, together):
        rows = jnp.concatenate(
            [
                q_ref[:, h * HEAD_DIMENSION : (h + 1) * HEAD_DIMENSION]
                for h in range(at, at + together)
            ],
            axis=0,
        )

        def one(step, state):
            top_score, run_sum, run_acc = state
            start = pl.multiple_of(step * chunk, chunk)
            scores = scored(rows, start)
            best = jnp.maximum(jnp.max(scores, axis=1, keepdims=True), top_score)
            rescale = jnp.exp2((top_score - best) * factor)
            weights = jnp.exp2((scores - best) * factor)
            total = run_sum * rescale + jnp.sum(weights, axis=1, keepdims=True)
            added = dot(weights.astype(BF16), v_ref[pl.ds(start, chunk)])
            return (best, total, run_acc * rescale + added)

        if steps == 1:
            scores = scored(rows, 0)
            best = jnp.max(scores, axis=1, keepdims=True)
            weights = jnp.exp2((scores - best) * factor)
            total = jnp.sum(weights, axis=1, keepdims=True)
            added = dot(weights.astype(BF16), v_ref[...])
        else:
            best, total, added = lax.fori_loop(
                0,
                (q_start + q_rows + chunk - 1) // chunk,
                one,
                (
                    jnp.full((tall, 1), -1e30, F32),
                    jnp.zeros((tall, 1), F32),
                    jnp.zeros((tall, HEAD_DIMENSION), F32),
                ),
            )
        context = (added / total).astype(BF16)
        for h in range(together):
            out_ref[:, (at + h) * HEAD_DIMENSION : (at + h + 1) * HEAD_DIMENSION] = context[
                h * q_rows : (h + 1) * q_rows
            ]


def attend_part(queries, keys, values, part, parts, context=None):
    q_rows, q_width = queries.shape
    total = keys.shape[0]
    part_width = q_width // parts
    per_kv = parts // KEY_VALUE_HEADS
    chunk = math.gcd(total, 1024)
    before = () if context is None else (context,)
    return pl.pallas_call(
        functools.partial(attention_kernel, chunk),
        grid=(1,),
        out_shape=jax.ShapeDtypeStruct((q_rows, q_width), BF16),
        in_specs=[
            pl.BlockSpec((q_rows, part_width), lambda i: (0, part)),
            pl.BlockSpec((total, HEAD_DIMENSION), lambda i: (0, part // per_kv)),
            pl.BlockSpec((total, HEAD_DIMENSION), lambda i: (0, part // per_kv)),
            *[ANY for _ in before],
        ],
        out_specs=pl.BlockSpec((q_rows, part_width), lambda i: (0, part)),
        input_output_aliases={3: 0} if before else {},
        compiler_params=pltpu.CompilerParams(vmem_limit_bytes=VMEM_LIMIT),
        cost_estimate=SHORT,
        name="attention",
    )(queries, keys, values, *before)


def summed(*terms):
    return sum(term.astype(F32) for term in terms).astype(BF16)


def after(x, *others):
    return lax.optimization_barrier((x, *others))[0]


def on_line(acts, packed, small, queries, w_gate_up, w_down, top, capacity):
    rows, width = acts.shape
    line = [packed, forward(packed), None, backward(packed)]
    crossed = [across(packed), across(line[1]), None, across(line[3])]
    to_core = other_core(packed)
    small = hold(after(small, to_core), in_vmem(w_gate_up, w_down))
    pair = jnp.concatenate([small, across(small)], axis=0)
    line[2] = forward(after(line[1], pair, crossed[0]))
    crossed[2] = across(line[2])
    arrays = [
        [
            line[step],
            crossed[step],
            other_core(line[step]) if step else to_core,
            other_core(crossed[step]),
        ]
        for step in range(LINE)
    ]
    blocks = [
        (4 * step + core * 2 + y, 2 * step + y, functools.partial(from_device, step, y, core))
        for core in range(2)
        for step in range(LINE)
        for y in range(2)
    ]
    pair = after(pair, line[3])
    pairs = [pair, forward(pair), None, backward(pair)]
    pairs[2] = forward(pairs[1])
    keep, mine, crossing = [None] * LINE, [None] * LINE, [None] * LINE

    def experts(first, second, before, beside):
        ready = arrays[first] + arrays[second]
        ready = [after(ready[0], *before), *ready[1:]]
        sources = [[(4 * group + i, 0, rows) for i in range(4)] for group in range(2)]
        targets = [[(group, 0, 2 * rows), (2, group * 2 * rows, 2 * rows)] for group in range(2)]
        keep[first], keep[second], send = run_experts(
            ready,
            sources,
            targets,
            [2 * rows, 2 * rows, 4 * rows],
            w_gate_up,
            w_down,
            top,
            rows,
            capacity,
        )
        came = other_core(after(send, *beside))
        for at, step in ((0, first), (2 * rows, second)):
            mine[step] = (keep[step][:rows], came[at : at + rows])
            crossing[step] = summed(keep[step][rows:], came[at + rows : at + 2 * rows])
        return send

    theirs = [None] * LINE
    experts(1, 0, [line[2], crossed[3]], [crossed[2], pairs[1], pairs[3]])
    theirs[1] = across(crossing[1])
    send = experts(2, 3, [crossing[0], crossing[1]], [theirs[1], pairs[2]])
    total = summed(*mine[1], after(theirs[1], send))
    moving = forward(total)
    theirs[2], theirs[3] = across(crossing[2]), across(crossing[3])
    own = jnp.concatenate(pairs, axis=0)
    shares = own.reshape(2 * LINE, small.shape[0], -1)[:, rows:]
    other = lax.ppermute(shares.reshape(-1, own.shape[1]), "grp", [(0, 1), (1, 0)])
    total = summed(*mine[2], theirs[2], moving)
    moving = forward(total)
    theirs[0] = across(after(crossing[0], total))
    smalls = [own, other, other_core(own), other_core(after(other, crossing[3]))]
    smalls[0] = after(own, total)
    new_keys, values = make_values(sum(arrays, []), blocks, smalls, rows, width)
    context = attend_part(queries, new_keys, values, 0, 4)
    total = summed(*mine[3], theirs[3], after(moving, context))
    moving = forward(total)
    queries = after(queries, total)
    for part in range(1, 4):
        context = attend_part(queries, new_keys, values, part, 4, context)
    layer_out = summed(acts, *mine[0], theirs[0], after(moving, context))
    return context, layer_out


def on_any(acts, packed, small, queries, w_gate_up, w_down, top, capacity):
    rows, width = acts.shape
    keys, value_weight = small[:rows], small[rows:]
    gathered = lax.all_gather(packed, "seq", axis=0, tiled=True)
    all_keys = lax.all_gather(keys, "seq", axis=0, tiled=True)
    weight = lax.all_gather(value_weight, "seq", axis=0, tiled=True)
    total = gathered.shape[0]
    part = total // GROUPS
    pieces = [[(0, group * part, part)] for group in range(GROUPS)]
    (partial,) = run_experts(
        [gathered], pieces, pieces, [total], w_gate_up, w_down, top, rows, capacity
    )
    values = dot(gathered[:, :width], weight).astype(BF16)
    context = None
    for part in range(KEY_VALUE_HEADS):
        context = attend_part(queries, all_keys, values, part, KEY_VALUE_HEADS, context)
    combined = lax.psum_scatter(partial, "seq", scatter_dimension=0, tiled=True)
    return context, summed(acts, combined)


def per_device(
    activations, queries, keys, norm_gain, value_weight, expert_ids, gate_weights, w_gate_up, w_down
):
    pos_rows, sequence_count, model_width = activations.shape
    assert sequence_count == 1 and w_down.shape[0] == 1
    top = expert_ids.shape[2]
    devices = lax.axis_size("seq")
    capacity = max(2, 3 * pos_rows * top // (2 * devices))
    acts = activations.reshape(pos_rows, model_width)
    halves = 2 * devices * pos_rows == model_width and value_weight.shape[0] % (2 * pos_rows) == 0
    line = devices == 4 * LINE and lax.axis_size("grp") == 2 and halves
    packed, small = pack(
        acts,
        norm_gain,
        expert_ids.transpose(1, 2, 0).reshape(top, pos_rows),
        gate_weights.transpose(1, 2, 0).reshape(top, pos_rows),
        keys.reshape(pos_rows, -1),
        value_weight,
        2 if line else 1,
    )
    way = on_line if line else on_any
    context, layer_out = way(
        acts,
        packed,
        small,
        queries.reshape(pos_rows, -1),
        w_gate_up[0],
        w_down[0],
        top,
        capacity,
    )
    return (context.reshape(queries.shape), layer_out.reshape(activations.shape))


def solution(mesh):
    placed = (
        P("seq", "grp", None),
        P("seq", "grp", None),
        P("seq", "grp", None),
        P(),
        P("seq", None),
        P("seq", "grp", None),
        P("seq", "grp", None),
        P("seq", None, None),
        P("seq", None, None),
    )
    return jax.shard_map(
        per_device,
        mesh=mesh,
        in_specs=placed,
        out_specs=(P("seq", "grp", None), P("seq", "grp", None)),
        check_vma=False,
    )
```

```python
import functools
import math

import jax
import jax.numpy as jnp
from jax import lax
from jax.experimental import pallas as pl
from jax.experimental.pallas import tpu as pltpu
from jax.sharding import PartitionSpec as P

QUERY_HEADS = 32
KEY_VALUE_HEADS = 2
HEAD_DIMENSION = 128
GROUPS = 4
META = 128
LINE = 4
VMEM_LIMIT = 24 * 2**20
F32 = jnp.float32
BF16 = jnp.bfloat16
ANY = pl.BlockSpec(memory_space=pl.ANY)
SHORT = pl.CostEstimate(flops=1, bytes_accessed=1, transcendentals=0)
IN_VMEM = pl.BlockSpec(memory_space=pltpu.VMEM)


def dot(a, b):
    return jnp.dot(a, b, preferred_element_type=F32)


RING = (0, 1, 3, 2)


def device_index(place, y, core):
    return (RING[place % LINE] * 2 + y) * 2 + core


def swaps(flip_y, flip_core):
    return [
        (device_index(p, y, c), device_index(p, y ^ flip_y, c ^ flip_core))
        for p in range(LINE)
        for y in range(2)
        for c in range(2)
    ]


def ring_steps(steps):
    return [
        (device_index(p, y, c), device_index(p + steps, y, c))
        for p in range(LINE)
        for y in range(2)
        for c in range(2)
    ]


def forward(x):
    return lax.ppermute(x, "seq", ring_steps(1))


def backward(x):
    return lax.ppermute(x, "seq", ring_steps(LINE - 1))


def across(x):
    return lax.ppermute(x, "seq", swaps(1, 0))


def other_core(x):
    return lax.ppermute(x, "seq", swaps(0, 1))


def from_device(steps, flip_y, flip_core):
    me = lax.axis_index("seq")
    core, y, line = me % 2, me // 2 % 2, me // 4
    place = sum(jnp.where(line == RING[p], p, 0) for p in range(LINE))
    place = (place + LINE - steps) % LINE
    line = sum(jnp.where(place == p, RING[p], 0) for p in range(LINE))
    y = 1 - y if flip_y else y
    core = 1 - core if flip_core else core
    return (line * 2 + y) * 2 + core


def pack_kernel(
    act_ref, gain_ref, ids_ref, gates_ref, key_ref, weight_ref, out_ref, small_ref, meta_ref
):
    width = act_ref.shape[1]
    rows = act_ref.shape[0]
    top = ids_ref.shape[0]
    features = act_ref[...].astype(F32)
    inverse = lax.rsqrt(jnp.mean(features * features, axis=-1, keepdims=True) + 1e-06)
    out_ref[:, :width] = (features * inverse * gain_ref[...]).astype(BF16)
    gates = gates_ref[...]
    high = gates.astype(BF16).astype(F32)
    rest = gates - high
    middle = rest.astype(BF16).astype(F32)
    meta_ref[...] = jnp.zeros_like(meta_ref)
    meta_ref[0:top, 0:rows] = ids_ref[...].astype(F32)
    meta_ref[8 : 8 + top, 0:rows] = high
    meta_ref[16 : 16 + top, 0:rows] = middle
    meta_ref[24 : 24 + top, 0:rows] = rest - middle
    out_ref[:, width:] = meta_ref[...].T[:rows, :].astype(BF16)
    small_ref[:rows] = key_ref[...]
    share = small_ref.shape[0] - rows
    first = 0
    if share < weight_ref.shape[0]:
        first = pl.multiple_of(lax.axis_index("grp") * share, share)
    small_ref[rows:] = weight_ref[pl.ds(first, share)]


def pack(activations, norm_gain, ids, gates, keys, value_weight, planes):
    rows, width = activations.shape
    small_rows = rows + value_weight.shape[0] // planes
    assert rows <= META and ids.shape[0] <= 8
    return pl.pallas_call(
        pack_kernel,
        out_shape=[
            jax.ShapeDtypeStruct((rows, width + META), BF16),
            jax.ShapeDtypeStruct((small_rows, keys.shape[1]), BF16),
        ],
        scratch_shapes=[pltpu.VMEM((META, META), F32)],
        cost_estimate=SHORT,
        name="normalize_and_pack",
    )(activations, norm_gain.reshape(1, width), ids, gates, keys, value_weight)


def hold_kernel(small_ref, up_ref, down_ref, out_ref):
    out_ref[...] = small_ref[...]


def hold(small, weights):
    return pl.pallas_call(
        hold_kernel,
        out_shape=jax.ShapeDtypeStruct(small.shape, small.dtype),
        in_specs=[IN_VMEM] * 3,
        out_specs=IN_VMEM,
        compiler_params=pltpu.CompilerParams(vmem_limit_bytes=4 * 2**20),
        cost_estimate=SHORT,
        name="hold_weights",
    )(small, *weights)


def in_vmem(*arrays):
    return [pltpu.with_memory_space_constraint(x, pltpu.VMEM) for x in arrays]


def expert_kernel(top, tok_rows, capacity, direct, sources, targets, *refs):
    inputs = 1 + max(s[0] for group in sources for s in group)
    outputs = 1 + max(t[0] for group in targets for t in group)
    x_hbm = refs[:inputs]
    up_ref, down_ref = refs[inputs : inputs + 2]
    out_hbm = refs[inputs + 2 : inputs + 2 + outputs]
    slot_rows, slot_gates, places, hidden, result, *rest = refs[inputs + 2 + outputs :]
    groups, rows, _ = places.shape
    units, width = down_ref.shape
    packed = width + META
    slots = slot_rows.shape[0] // groups
    tile = 256
    me = lax.axis_index("seq").astype(F32)
    if direct:

        def read(group, columns):
            return jnp.concatenate(
                [x_hbm[operand][:, columns] for operand, _, _ in sources[group]], axis=0
            )

        def write(group, columns, value):
            at = 0
            for operand, first, count in targets[group]:
                out_hbm[operand][first : first + count, columns] = value[at : at + count]
                at += count

    else:
        x_buf, x_sem, out_sem = rest

        def read(group, columns):
            return x_buf[group, :, columns]

        def write(group, columns, value):
            x_buf[group, :, columns] = value

    def loads(group):
        copies, at = [], 0
        for number, (operand, first, count) in enumerate([] if direct else sources[group]):
            copies.append(
                pltpu.make_async_copy(
                    x_hbm[operand].at[pl.ds(first, count)],
                    x_buf.at[group, pl.ds(at, count)],
                    x_sem.at[group, number],
                )
            )
            at += count
        return copies

    def stores(group):
        copies, at = [], 0
        for number, (operand, first, count) in enumerate([] if direct else targets[group]):
            copies.append(
                pltpu.make_async_copy(
                    x_buf.at[group, pl.ds(at, count), pl.ds(0, width)],
                    out_hbm[operand].at[pl.ds(first, count)],
                    out_sem.at[group, number],
                )
            )
            at += count
        return copies

    for group in range(groups):
        for copy in loads(group):
            copy.start()

    chunk = tok_rows * META // math.gcd(tok_rows, META)
    first = lax.broadcasted_iota(jnp.int32, (chunk, chunk), 0)
    second = lax.broadcasted_iota(jnp.int32, (chunk, chunk), 1)
    earlier = ((first < second) & (first // tok_rows == second // tok_rows)).astype(F32).astype(BF16)
    block = lax.broadcasted_iota(jnp.int32, (1, rows), 1) // tok_rows
    for group in range(groups):
        for copy in loads(group):
            copy.wait()
        meta = read(group, slice(width, packed)).astype(F32).T
        gate = jnp.zeros((1, rows), F32)
        named = jnp.zeros((1, rows), F32)
        for k in range(top):
            match = meta[k : k + 1] == me
            value = meta[8 + k : 9 + k] + (meta[16 + k : 17 + k] + meta[24 + k : 25 + k])
            gate = jnp.where(match, value, gate)
            named = jnp.where(match, 1.0, named)
        marks = jnp.broadcast_to(named, (8, rows)).astype(BF16)
        rank = jnp.concatenate(
            [dot(marks[:, at : at + chunk], earlier) for at in range(0, rows, chunk)], axis=1
        )[0:1]
        slot = jnp.where(named > 0.0, (block * capacity).astype(F32) + rank, -1.0)
        spots = lax.broadcasted_iota(jnp.int32, (slots, rows), 0).astype(F32)
        chosen = spots == slot
        slot_gates[pl.ds(group * slots, slots)] = jnp.broadcast_to(
            jnp.sum(jnp.where(chosen, gate, 0.0), axis=1, keepdims=True), (slots, META)
        )
        pick = chosen.astype(F32).astype(BF16)
        for at in range(0, width, 512):
            slot_rows[pl.ds(group * slots, slots), at : at + 512] = dot(
                pick, read(group, slice(at, at + 512))
            ).astype(BF16)
        by_row = jnp.broadcast_to(slot, (META, rows)).T
        spots = lax.broadcasted_iota(jnp.int32, (rows, META), 1).astype(F32)
        places[group] = (spots == by_row).astype(F32).astype(BF16)

    for at in range(0, units, tile):
        gate = dot(slot_rows[...], up_ref[:, at : at + tile])
        up = dot(slot_rows[...], up_ref[:, units + at : units + at + tile])
        hidden[:, at : at + tile] = (gate / (1.0 + jnp.exp(-gate)) * up).astype(BF16)
    for at in range(0, width, tile):
        out = dot(hidden[...], down_ref[:, at : at + tile]).astype(BF16).astype(F32)
        result[:, at : at + tile] = (out * slot_gates[:, 0:1]).astype(BF16)
    for group in range(groups):
        for at in range(0, width, 512):
            placed = dot(
                places[group, :, :slots], result[pl.ds(group * slots, slots), at : at + 512]
            )
            write(group, slice(at, at + 512), placed.astype(BF16))
        for copy in stores(group):
            copy.start()
    for group in range(groups):
        for copy in stores(group):
            copy.wait()


def run_experts(arrays, sources, targets, out_rows, w_gate_up, w_down, top, tok_rows, capacity):
    direct = len(arrays) > 1
    groups = len(sources)
    rows = sum(count for _, _, count in sources[0])
    total = groups * rows
    units, width = w_down.shape
    packed = width + META
    slots = rows // tok_rows * capacity
    assert slots % 16 == 0 and slots <= META and units % 256 == 0 and width % 512 == 0
    all_slots = groups * slots
    held = 2 * total * (packed + META) + all_slots * (4 * width + 2 * units + 4 * META)
    scratch = [
        pltpu.VMEM((all_slots, width), BF16),
        pltpu.VMEM((all_slots, META), F32),
        pltpu.VMEM((groups, rows, META), BF16),
        pltpu.VMEM((all_slots, units), BF16),
        pltpu.VMEM((all_slots, width), BF16),
    ]
    if not direct:
        scratch += [
            pltpu.VMEM((groups, rows, packed), BF16),
            pltpu.SemaphoreType.DMA((groups, max(len(s) for s in sources))),
            pltpu.SemaphoreType.DMA((groups, max(len(t) for t in targets))),
        ]
    shape = pltpu.VMEM if direct else jax.ShapeDtypeStruct
    place = IN_VMEM if direct else ANY
    return pl.pallas_call(
        functools.partial(expert_kernel, top, tok_rows, capacity, direct, sources, targets),
        out_shape=[shape((count, width), BF16) for count in out_rows],
        in_specs=[place] * len(arrays) + [IN_VMEM] * 2,
        out_specs=[place] * len(out_rows),
        scratch_shapes=scratch,
        compiler_params=pltpu.CompilerParams(vmem_limit_bytes=held + 8 * 2**20),
        cost_estimate=SHORT,
        name="experts",
    )(*(in_vmem(*arrays) if direct else arrays), *in_vmem(w_gate_up, w_down))


def value_kernel(key_rows, blocks, *refs):
    count = len(blocks)
    x_refs, smalls = refs[:count], refs[count : count + 6]
    key_ref, value_ref, weight = refs[count + 6 :]
    width = weight.shape[0]
    share = width // count // 2
    plane = lax.axis_index("grp")
    places = [device() for _, _, _, device in blocks]

    def below(number, size):
        return pl.ds(pl.multiple_of(number * size, size), size)

    for (_, at, core, _), place in zip(blocks, places):
        own, near, far = smalls[3 * core : 3 * core + 3]
        other, there = (near, at) if at * share < near.shape[0] else (far, at - near.shape[0] // share)
        first = at * (key_rows + share)
        key_ref[below(place, key_rows)] = own[first : first + key_rows]
        weight[below(2 * place + plane, share)] = own[first + key_rows : first + key_rows + share]
        weight[below(2 * place + 1 - plane, share)] = other[there * share : (there + 1) * share]
    for start in range(0, count, 4):
        rows = [x_refs[operand][:, :width] for operand, _, _, _ in blocks[start : start + 4]]
        values = dot(jnp.concatenate(rows, axis=0), weight[...]).astype(BF16)
        for number in range(4):
            value_ref[below(places[start + number], key_rows)] = values[
                number * key_rows : (number + 1) * key_rows
            ]


def make_values(arrays, blocks, smalls, key_rows, width):
    kv_width = smalls[0].shape[1]
    kv = jax.ShapeDtypeStruct((key_rows * len(blocks), kv_width), BF16)
    return pl.pallas_call(
        functools.partial(value_kernel, key_rows, blocks),
        out_shape=[kv, kv],
        in_specs=[IN_VMEM] * (len(arrays) + len(smalls)),
        out_specs=[IN_VMEM] * 2,
        scratch_shapes=[pltpu.VMEM((width, kv_width), BF16)],
        compiler_params=pltpu.CompilerParams(vmem_limit_bytes=VMEM_LIMIT),
        cost_estimate=SHORT,
        name="values",
    )(*in_vmem(*arrays, *smalls))


def attention_kernel(chunk, q_ref, k_ref, v_ref, *refs):
    out_ref = refs[-1]
    q_rows, q_width = q_ref.shape
    heads = q_width // HEAD_DIMENSION
    together = 4
    q_start = lax.axis_index("seq") * q_rows
    factor = math.log2(math.e) / math.sqrt(HEAD_DIMENSION)
    steps = k_ref.shape[0] // chunk
    tall = together * q_rows

    def scored(rows, start):
        scores = lax.dot_general(
            rows, k_ref[pl.ds(start, chunk)], (((1,), (1,)), ((), ())), preferred_element_type=F32
        )
        q_at = q_start + lax.broadcasted_iota(jnp.int32, (q_rows, chunk), 0)
        k_at = start + lax.broadcasted_iota(jnp.int32, (q_rows, chunk), 1)
        bias = jnp.where(q_at >= k_at, 0.0, -1e30)[None]
        return (scores.reshape(together, q_rows, chunk) + bias).reshape(tall, chunk)

    for at in range(0, heads, together):
        rows = jnp.concatenate(
            [
                q_ref[:, h * HEAD_DIMENSION : (h + 1) * HEAD_DIMENSION]
                for h in range(at, at + together)
            ],
            axis=0,
        )

        def one(step, state):
            top_score, run_sum, run_acc = state
            start = pl.multiple_of(step * chunk, chunk)
            scores = scored(rows, start)
            best = jnp.maximum(jnp.max(scores, axis=1, keepdims=True), top_score)
            rescale = jnp.exp2((top_score - best) * factor)
            weights = jnp.exp2((scores - best) * factor)
            total = run_sum * rescale + jnp.sum(weights, axis=1, keepdims=True)
            added = dot(weights.astype(BF16), v_ref[pl.ds(start, chunk)])
            return (best, total, run_acc * rescale + added)

        if steps == 1:
            scores = scored(rows, 0)
            best = jnp.max(scores, axis=1, keepdims=True)
            weights = jnp.exp2((scores - best) * factor)
            total = jnp.sum(weights, axis=1, keepdims=True)
            added = dot(weights.astype(BF16), v_ref[...])
        else:
            best, total, added = lax.fori_loop(
                0,
                (q_start + q_rows + chunk - 1) // chunk,
                one,
                (
                    jnp.full((tall, 1), -1e30, F32),
                    jnp.zeros((tall, 1), F32),
                    jnp.zeros((tall, HEAD_DIMENSION), F32),
                ),
            )
        context = (added / total).astype(BF16)
        for h in range(together):
            out_ref[:, (at + h) * HEAD_DIMENSION : (at + h + 1) * HEAD_DIMENSION] = context[
                h * q_rows : (h + 1) * q_rows
            ]


def attend_part(queries, keys, values, part, parts, context=None):
    q_rows, q_width = queries.shape
    total = keys.shape[0]
    part_width = q_width // parts
    per_kv = parts // KEY_VALUE_HEADS
    chunk = math.gcd(total, 1024)
    before = () if context is None else (context,)
    return pl.pallas_call(
        functools.partial(attention_kernel, chunk),
        grid=(1,),
        out_shape=jax.ShapeDtypeStruct((q_rows, q_width), BF16),
        in_specs=[
            pl.BlockSpec((q_rows, part_width), lambda i: (0, part)),
            pl.BlockSpec((total, HEAD_DIMENSION), lambda i: (0, part // per_kv)),
            pl.BlockSpec((total, HEAD_DIMENSION), lambda i: (0, part // per_kv)),
            *[ANY for _ in before],
        ],
        out_specs=pl.BlockSpec((q_rows, part_width), lambda i: (0, part)),
        input_output_aliases={3: 0} if before else {},
        compiler_params=pltpu.CompilerParams(vmem_limit_bytes=VMEM_LIMIT),
        cost_estimate=SHORT,
        name="attention",
    )(queries, keys, values, *before)


def summed(*terms):
    return sum(term.astype(F32) for term in terms).astype(BF16)


def after(x, *others):
    return lax.optimization_barrier((x, *others))[0]


def on_line(acts, packed, small, queries, w_gate_up, w_down, top, capacity):
    rows, width = acts.shape
    line = [packed, forward(packed), None, backward(packed)]
    crossed = [across(packed), across(line[1]), None, across(line[3])]
    to_core = other_core(packed)
    small = hold(after(small, to_core), in_vmem(w_gate_up, w_down))
    pair = jnp.concatenate([small, across(small)], axis=0)
    line[2] = forward(after(line[1], pair, crossed[0]))
    crossed[2] = across(line[2])
    arrays = [
        [
            line[step],
            crossed[step],
            other_core(line[step]) if step else to_core,
            other_core(crossed[step]),
        ]
        for step in range(LINE)
    ]
    order = (0, 1, 3, 2)
    blocks = [
        (4 * step + core * 2 + y, 2 * at + y, core, functools.partial(from_device, step, y, core))
        for core in range(2)
        for at, step in enumerate(order)
        for y in range(2)
    ]

    def swap_planes(pieces):
        both = jnp.concatenate(pieces, axis=0)
        shares = both.reshape(-1, small.shape[0], both.shape[1])[:, rows:]
        return lax.ppermute(shares.reshape(-1, both.shape[1]), "grp", [(0, 1), (1, 0)])

    pair = after(pair, line[3])
    pairs = [pair, forward(pair), None, backward(pair)]
    pairs[2] = forward(pairs[1])
    keep, mine, crossing = [None] * LINE, [None] * LINE, [None] * LINE

    def experts(first, second, before, beside):
        ready = arrays[first] + arrays[second]
        ready = [after(ready[0], *before), *ready[1:]]
        sources = [[(4 * group + i, 0, rows) for i in range(4)] for group in range(2)]
        targets = [[(group, 0, 2 * rows), (2, group * 2 * rows, 2 * rows)] for group in range(2)]
        keep[first], keep[second], send = run_experts(
            ready,
            sources,
            targets,
            [2 * rows, 2 * rows, 4 * rows],
            w_gate_up,
            w_down,
            top,
            rows,
            capacity,
        )
        came = other_core(after(send, *beside))
        for at, step in ((0, first), (2 * rows, second)):
            mine[step] = (keep[step][:rows], came[at : at + rows])
            crossing[step] = summed(keep[step][rows:], came[at + rows : at + 2 * rows])
        return send

    theirs = [None] * LINE
    experts(1, 0, [line[2], crossed[3]], [crossed[2], pairs[1], pairs[3]])
    theirs[1] = across(crossing[1])
    near = swap_planes([pairs[0], pairs[1], pairs[3]])
    send = experts(2, 3, [crossing[0], crossing[1]], [theirs[1], pairs[2], near])
    total = summed(*mine[1], after(theirs[1], send))
    moving = forward(total)
    theirs[2], theirs[3] = across(crossing[2]), across(crossing[3])
    far = swap_planes([after(pairs[2], *crossing[2:], total)])
    own = after(jnp.concatenate([pairs[step] for step in order], axis=0), crossing[3])
    smalls = [own, near, far, other_core(own), other_core(after(near, crossing[3])), other_core(far)]
    total = summed(*mine[2], theirs[2], after(moving, *smalls[3:]))
    moving = forward(total)
    theirs[0] = across(after(crossing[0], total))
    smalls[0] = after(own, total)
    new_keys, values = make_values(sum(arrays, []), blocks, smalls, rows, width)
    context = attend_part(queries, new_keys, values, 0, 4)
    context = attend_part(queries, new_keys, values, 1, 4, context)
    total = summed(*mine[3], theirs[3], after(moving, context))
    moving = forward(total)
    queries = after(queries, total)
    for part in range(2, 4):
        context = attend_part(queries, new_keys, values, part, 4, context)
    layer_out = summed(acts, *mine[0], theirs[0], after(moving, context))
    return context, layer_out


def on_any(acts, packed, small, queries, w_gate_up, w_down, top, capacity):
    rows, width = acts.shape
    keys, value_weight = small[:rows], small[rows:]
    gathered = lax.all_gather(packed, "seq", axis=0, tiled=True)
    all_keys = lax.all_gather(keys, "seq", axis=0, tiled=True)
    weight = lax.all_gather(value_weight, "seq", axis=0, tiled=True)
    total = gathered.shape[0]
    part = total // GROUPS
    pieces = [[(0, group * part, part)] for group in range(GROUPS)]
    (partial,) = run_experts(
        [gathered], pieces, pieces, [total], w_gate_up, w_down, top, rows, capacity
    )
    values = dot(gathered[:, :width], weight).astype(BF16)
    context = None
    for part in range(KEY_VALUE_HEADS):
        context = attend_part(queries, all_keys, values, part, KEY_VALUE_HEADS, context)
    combined = lax.psum_scatter(partial, "seq", scatter_dimension=0, tiled=True)
    return context, summed(acts, combined)


def per_device(
    activations, queries, keys, norm_gain, value_weight, expert_ids, gate_weights, w_gate_up, w_down
):
    pos_rows, sequence_count, model_width = activations.shape
    assert sequence_count == 1 and w_down.shape[0] == 1
    top = expert_ids.shape[2]
    devices = lax.axis_size("seq")
    capacity = max(2, 3 * pos_rows * top // (2 * devices))
    acts = activations.reshape(pos_rows, model_width)
    halves = 2 * devices * pos_rows == model_width and value_weight.shape[0] % (2 * pos_rows) == 0
    line = devices == 4 * LINE and lax.axis_size("grp") == 2 and halves
    packed, small = pack(
        acts,
        norm_gain,
        expert_ids.transpose(1, 2, 0).reshape(top, pos_rows),
        gate_weights.transpose(1, 2, 0).reshape(top, pos_rows),
        keys.reshape(pos_rows, -1),
        value_weight,
        2 if line else 1,
    )
    way = on_line if line else on_any
    context, layer_out = way(
        acts,
        packed,
        small,
        queries.reshape(pos_rows, -1),
        w_gate_up[0],
        w_down[0],
        top,
        capacity,
    )
    return (context.reshape(queries.shape), layer_out.reshape(activations.shape))


def solution(mesh):
    placed = (
        P("seq", "grp", None),
        P("seq", "grp", None),
        P("seq", "grp", None),
        P(),
        P("seq", None),
        P("seq", "grp", None),
        P("seq", "grp", None),
        P("seq", None, None),
        P("seq", None, None),
    )
    return jax.shard_map(
        per_device,
        mesh=mesh,
        in_specs=placed,
        out_specs=(P("seq", "grp", None), P("seq", "grp", None)),
        check_vma=False,
    )
```

```python
import functools
import math

import jax
import jax.numpy as jnp
from jax import lax
from jax.experimental import pallas as pl
from jax.experimental.pallas import tpu as pltpu
from jax.sharding import PartitionSpec as P

QUERY_HEADS = 32
KEY_VALUE_HEADS = 2
HEAD_DIMENSION = 128
GROUPS = 4
META = 128
LINE = 4
VMEM_LIMIT = 24 * 2**20
F32 = jnp.float32
BF16 = jnp.bfloat16
ANY = pl.BlockSpec(memory_space=pl.ANY)
SHORT = pl.CostEstimate(flops=1, bytes_accessed=1, transcendentals=0)
IN_VMEM = pl.BlockSpec(memory_space=pltpu.VMEM)


def dot(a, b):
    return jnp.dot(a, b, preferred_element_type=F32)


RING = (0, 1, 3, 2)


def device_index(place, y, core):
    return (RING[place % LINE] * 2 + y) * 2 + core


def swaps(flip_y, flip_core):
    return [
        (device_index(p, y, c), device_index(p, y ^ flip_y, c ^ flip_core))
        for p in range(LINE)
        for y in range(2)
        for c in range(2)
    ]


def ring_steps(steps):
    return [
        (device_index(p, y, c), device_index(p + steps, y, c))
        for p in range(LINE)
        for y in range(2)
        for c in range(2)
    ]


def forward(x):
    return lax.ppermute(x, "seq", ring_steps(1))


def backward(x):
    return lax.ppermute(x, "seq", ring_steps(LINE - 1))


def across(x):
    return lax.ppermute(x, "seq", swaps(1, 0))


def other_core(x):
    return lax.ppermute(x, "seq", swaps(0, 1))


def from_device(steps, flip_y, flip_core):
    me = lax.axis_index("seq")
    core, y, line = me % 2, me // 2 % 2, me // 4
    place = sum(jnp.where(line == RING[p], p, 0) for p in range(LINE))
    place = (place + LINE - steps) % LINE
    line = sum(jnp.where(place == p, RING[p], 0) for p in range(LINE))
    y = 1 - y if flip_y else y
    core = 1 - core if flip_core else core
    return (line * 2 + y) * 2 + core


def pack_kernel(
    act_ref, gain_ref, ids_ref, gates_ref, key_ref, weight_ref, out_ref, small_ref, meta_ref
):
    width = act_ref.shape[1]
    rows = act_ref.shape[0]
    top = ids_ref.shape[0]
    features = act_ref[...].astype(F32)
    inverse = lax.rsqrt(jnp.mean(features * features, axis=-1, keepdims=True) + 1e-06)
    out_ref[:, :width] = (features * inverse * gain_ref[...]).astype(BF16)
    gates = gates_ref[...]
    high = gates.astype(BF16).astype(F32)
    rest = gates - high
    middle = rest.astype(BF16).astype(F32)
    meta_ref[...] = jnp.zeros_like(meta_ref)
    meta_ref[0:top, 0:rows] = ids_ref[...].astype(F32)
    meta_ref[8 : 8 + top, 0:rows] = high
    meta_ref[16 : 16 + top, 0:rows] = middle
    meta_ref[24 : 24 + top, 0:rows] = rest - middle
    out_ref[:, width:] = meta_ref[...].T[:rows, :].astype(BF16)
    small_ref[:rows] = key_ref[...]
    share = small_ref.shape[0] - rows
    first = 0
    if share < weight_ref.shape[0]:
        first = pl.multiple_of(lax.axis_index("grp") * share, share)
    small_ref[rows:] = weight_ref[pl.ds(first, share)]


def pack(activations, norm_gain, ids, gates, keys, value_weight, planes):
    rows, width = activations.shape
    small_rows = rows + value_weight.shape[0] // planes
    assert rows <= META and ids.shape[0] <= 8
    return pl.pallas_call(
        pack_kernel,
        out_shape=[
            jax.ShapeDtypeStruct((rows, width + META), BF16),
            jax.ShapeDtypeStruct((small_rows, keys.shape[1]), BF16),
        ],
        scratch_shapes=[pltpu.VMEM((META, META), F32)],
        cost_estimate=SHORT,
        name="normalize_and_pack",
    )(activations, norm_gain.reshape(1, width), ids, gates, keys, value_weight)


def hold_kernel(small_ref, up_ref, down_ref, out_ref):
    out_ref[...] = small_ref[...]


def hold(small, weights):
    return pl.pallas_call(
        hold_kernel,
        out_shape=jax.ShapeDtypeStruct(small.shape, small.dtype),
        in_specs=[IN_VMEM] * 3,
        out_specs=IN_VMEM,
        compiler_params=pltpu.CompilerParams(vmem_limit_bytes=4 * 2**20),
        cost_estimate=SHORT,
        name="hold_weights",
    )(small, *weights)


def in_vmem(*arrays):
    return [pltpu.with_memory_space_constraint(x, pltpu.VMEM) for x in arrays]


def expert_kernel(top, tok_rows, capacity, direct, sources, targets, *refs):
    inputs = 1 + max(s[0] for group in sources for s in group)
    outputs = 1 + max(t[0] for group in targets for t in group)
    x_hbm = refs[:inputs]
    up_ref, down_ref = refs[inputs : inputs + 2]
    out_hbm = refs[inputs + 2 : inputs + 2 + outputs]
    slot_rows, slot_gates, places, hidden, result, *rest = refs[inputs + 2 + outputs :]
    groups, rows, _ = places.shape
    units, width = down_ref.shape
    packed = width + META
    slots = slot_rows.shape[0] // groups
    tile = 256
    me = lax.axis_index("seq").astype(F32)
    if direct:

        def read(group, columns):
            return jnp.concatenate(
                [x_hbm[operand][:, columns] for operand, _, _ in sources[group]], axis=0
            )

        def write(group, columns, value):
            at = 0
            for operand, first, count in targets[group]:
                out_hbm[operand][first : first + count, columns] = value[at : at + count]
                at += count

    else:
        x_buf, x_sem, out_sem = rest

        def read(group, columns):
            return x_buf[group, :, columns]

        def write(group, columns, value):
            x_buf[group, :, columns] = value

    def loads(group):
        copies, at = [], 0
        for number, (operand, first, count) in enumerate([] if direct else sources[group]):
            copies.append(
                pltpu.make_async_copy(
                    x_hbm[operand].at[pl.ds(first, count)],
                    x_buf.at[group, pl.ds(at, count)],
                    x_sem.at[group, number],
                )
            )
            at += count
        return copies

    def stores(group):
        copies, at = [], 0
        for number, (operand, first, count) in enumerate([] if direct else targets[group]):
            copies.append(
                pltpu.make_async_copy(
                    x_buf.at[group, pl.ds(at, count), pl.ds(0, width)],
                    out_hbm[operand].at[pl.ds(first, count)],
                    out_sem.at[group, number],
                )
            )
            at += count
        return copies

    for group in range(groups):
        for copy in loads(group):
            copy.start()

    chunk = tok_rows * META // math.gcd(tok_rows, META)
    first = lax.broadcasted_iota(jnp.int32, (chunk, chunk), 0)
    second = lax.broadcasted_iota(jnp.int32, (chunk, chunk), 1)
    earlier = ((first < second) & (first // tok_rows == second // tok_rows)).astype(F32).astype(BF16)
    block = lax.broadcasted_iota(jnp.int32, (1, rows), 1) // tok_rows
    for group in range(groups):
        for copy in loads(group):
            copy.wait()
        meta = read(group, slice(width, packed)).astype(F32).T
        gate = jnp.zeros((1, rows), F32)
        named = jnp.zeros((1, rows), F32)
        for k in range(top):
            match = meta[k : k + 1] == me
            value = meta[8 + k : 9 + k] + (meta[16 + k : 17 + k] + meta[24 + k : 25 + k])
            gate = jnp.where(match, value, gate)
            named = jnp.where(match, 1.0, named)
        marks = jnp.broadcast_to(named, (8, rows)).astype(BF16)
        rank = jnp.concatenate(
            [dot(marks[:, at : at + chunk], earlier) for at in range(0, rows, chunk)], axis=1
        )[0:1]
        slot = jnp.where(named > 0.0, (block * capacity).astype(F32) + rank, -1.0)
        spots = lax.broadcasted_iota(jnp.int32, (slots, rows), 0).astype(F32)
        chosen = spots == slot
        slot_gates[pl.ds(group * slots, slots)] = jnp.broadcast_to(
            jnp.sum(jnp.where(chosen, gate, 0.0), axis=1, keepdims=True), (slots, META)
        )
        pick = chosen.astype(F32).astype(BF16)
        for at in range(0, width, 512):
            slot_rows[pl.ds(group * slots, slots), at : at + 512] = dot(
                pick, read(group, slice(at, at + 512))
            ).astype(BF16)
        by_row = jnp.broadcast_to(slot, (META, rows)).T
        spots = lax.broadcasted_iota(jnp.int32, (rows, META), 1).astype(F32)
        places[group] = (spots == by_row).astype(F32).astype(BF16)

    for at in range(0, units, tile):
        gate = dot(slot_rows[...], up_ref[:, at : at + tile])
        up = dot(slot_rows[...], up_ref[:, units + at : units + at + tile])
        hidden[:, at : at + tile] = (gate / (1.0 + jnp.exp(-gate)) * up).astype(BF16)
    for at in range(0, width, tile):
        out = dot(hidden[...], down_ref[:, at : at + tile]).astype(BF16).astype(F32)
        result[:, at : at + tile] = (out * slot_gates[:, 0:1]).astype(BF16)
    for group in range(groups):
        for at in range(0, width, 512):
            placed = dot(
                places[group, :, :slots], result[pl.ds(group * slots, slots), at : at + 512]
            )
            write(group, slice(at, at + 512), placed.astype(BF16))
        for copy in stores(group):
            copy.start()
    for group in range(groups):
        for copy in stores(group):
            copy.wait()


def run_experts(arrays, sources, targets, out_rows, w_gate_up, w_down, top, tok_rows, capacity):
    direct = len(arrays) > 1
    groups = len(sources)
    rows = sum(count for _, _, count in sources[0])
    total = groups * rows
    units, width = w_down.shape
    packed = width + META
    slots = rows // tok_rows * capacity
    assert slots % 16 == 0 and slots <= META and units % 256 == 0 and width % 512 == 0
    all_slots = groups * slots
    held = 2 * total * (packed + META) + all_slots * (4 * width + 2 * units + 4 * META)
    scratch = [
        pltpu.VMEM((all_slots, width), BF16),
        pltpu.VMEM((all_slots, META), F32),
        pltpu.VMEM((groups, rows, META), BF16),
        pltpu.VMEM((all_slots, units), BF16),
        pltpu.VMEM((all_slots, width), BF16),
    ]
    if not direct:
        scratch += [
            pltpu.VMEM((groups, rows, packed), BF16),
            pltpu.SemaphoreType.DMA((groups, max(len(s) for s in sources))),
            pltpu.SemaphoreType.DMA((groups, max(len(t) for t in targets))),
        ]
    shape = pltpu.VMEM if direct else jax.ShapeDtypeStruct
    place = IN_VMEM if direct else ANY
    return pl.pallas_call(
        functools.partial(expert_kernel, top, tok_rows, capacity, direct, sources, targets),
        out_shape=[shape((count, width), BF16) for count in out_rows],
        in_specs=[place] * len(arrays) + [IN_VMEM] * 2,
        out_specs=[place] * len(out_rows),
        scratch_shapes=scratch,
        compiler_params=pltpu.CompilerParams(vmem_limit_bytes=held + 8 * 2**20),
        cost_estimate=SHORT,
        name="experts",
    )(*(in_vmem(*arrays) if direct else arrays), *in_vmem(w_gate_up, w_down))


def value_kernel(key_rows, blocks, *refs):
    count = len(blocks)
    x_refs, smalls = refs[:count], refs[count : count + 6]
    key_ref, value_ref, weight = refs[count + 6 :]
    width = weight.shape[0]
    share = width // count // 2
    plane = lax.axis_index("grp")
    places = [device() for _, _, _, device in blocks]

    def below(number, size):
        return pl.ds(pl.multiple_of(number * size, size), size)

    for (_, at, core, _), place in zip(blocks, places):
        own, near, far = smalls[3 * core : 3 * core + 3]
        other, there = (near, at) if at * share < near.shape[0] else (far, at - near.shape[0] // share)
        first = at * (key_rows + share)
        key_ref[below(place, key_rows)] = own[first : first + key_rows]
        weight[below(2 * place + plane, share)] = own[first + key_rows : first + key_rows + share]
        weight[below(2 * place + 1 - plane, share)] = other[there * share : (there + 1) * share]
    for start in range(0, count, 4):
        rows = [x_refs[operand][:, :width] for operand, _, _, _ in blocks[start : start + 4]]
        values = dot(jnp.concatenate(rows, axis=0), weight[...]).astype(BF16)
        for number in range(4):
            value_ref[below(places[start + number], key_rows)] = values[
                number * key_rows : (number + 1) * key_rows
            ]


def make_values(arrays, blocks, smalls, key_rows, width):
    kv_width = smalls[0].shape[1]
    kv = jax.ShapeDtypeStruct((key_rows * len(blocks), kv_width), BF16)
    return pl.pallas_call(
        functools.partial(value_kernel, key_rows, blocks),
        out_shape=[kv, kv],
        in_specs=[IN_VMEM] * (len(arrays) + len(smalls)),
        out_specs=[IN_VMEM] * 2,
        scratch_shapes=[pltpu.VMEM((width, kv_width), BF16)],
        compiler_params=pltpu.CompilerParams(vmem_limit_bytes=VMEM_LIMIT),
        cost_estimate=SHORT,
        name="values",
    )(*in_vmem(*arrays, *smalls))


def attention_kernel(chunk, q_ref, k_ref, v_ref, *refs):
    out_ref = refs[-1]
    q_rows, q_width = q_ref.shape
    heads = q_width // HEAD_DIMENSION
    together = 4
    q_start = lax.axis_index("seq") * q_rows
    factor = math.log2(math.e) / math.sqrt(HEAD_DIMENSION)
    steps = k_ref.shape[0] // chunk
    tall = together * q_rows

    def scored(rows, start):
        scores = lax.dot_general(
            rows, k_ref[pl.ds(start, chunk)], (((1,), (1,)), ((), ())), preferred_element_type=F32
        )
        q_at = q_start + lax.broadcasted_iota(jnp.int32, (q_rows, chunk), 0)
        k_at = start + lax.broadcasted_iota(jnp.int32, (q_rows, chunk), 1)
        bias = jnp.where(q_at >= k_at, 0.0, -1e30)[None]
        return (scores.reshape(together, q_rows, chunk) + bias).reshape(tall, chunk)

    for at in range(0, heads, together):
        rows = jnp.concatenate(
            [
                q_ref[:, h * HEAD_DIMENSION : (h + 1) * HEAD_DIMENSION]
                for h in range(at, at + together)
            ],
            axis=0,
        )

        def one(step, state):
            top_score, run_sum, run_acc = state
            start = pl.multiple_of(step * chunk, chunk)
            scores = scored(rows, start)
            best = jnp.maximum(jnp.max(scores, axis=1, keepdims=True), top_score)
            rescale = jnp.exp2((top_score - best) * factor)
            weights = jnp.exp2((scores - best) * factor)
            total = run_sum * rescale + jnp.sum(weights, axis=1, keepdims=True)
            added = dot(weights.astype(BF16), v_ref[pl.ds(start, chunk)])
            return (best, total, run_acc * rescale + added)

        if steps == 1:
            scores = scored(rows, 0)
            best = jnp.max(scores, axis=1, keepdims=True)
            weights = jnp.exp2((scores - best) * factor)
            total = jnp.sum(weights, axis=1, keepdims=True)
            added = dot(weights.astype(BF16), v_ref[...])
        else:
            best, total, added = lax.fori_loop(
                0,
                (q_start + q_rows + chunk - 1) // chunk,
                one,
                (
                    jnp.full((tall, 1), -1e30, F32),
                    jnp.zeros((tall, 1), F32),
                    jnp.zeros((tall, HEAD_DIMENSION), F32),
                ),
            )
        context = (added / total).astype(BF16)
        for h in range(together):
            out_ref[:, (at + h) * HEAD_DIMENSION : (at + h + 1) * HEAD_DIMENSION] = context[
                h * q_rows : (h + 1) * q_rows
            ]


def attend_part(queries, keys, values, part, parts, context=None):
    q_rows, q_width = queries.shape
    total = keys.shape[0]
    part_width = q_width // parts
    per_kv = parts // KEY_VALUE_HEADS
    chunk = math.gcd(total, 1024)
    before = () if context is None else (context,)
    return pl.pallas_call(
        functools.partial(attention_kernel, chunk),
        grid=(1,),
        out_shape=jax.ShapeDtypeStruct((q_rows, q_width), BF16),
        in_specs=[
            pl.BlockSpec((q_rows, part_width), lambda i: (0, part)),
            pl.BlockSpec((total, HEAD_DIMENSION), lambda i: (0, part // per_kv)),
            pl.BlockSpec((total, HEAD_DIMENSION), lambda i: (0, part // per_kv)),
            *[ANY for _ in before],
        ],
        out_specs=pl.BlockSpec((q_rows, part_width), lambda i: (0, part)),
        input_output_aliases={3: 0} if before else {},
        compiler_params=pltpu.CompilerParams(vmem_limit_bytes=VMEM_LIMIT),
        cost_estimate=SHORT,
        name="attention",
    )(queries, keys, values, *before)


def summed(*terms):
    return sum(term.astype(F32) for term in terms).astype(BF16)


def after(x, *others):
    return lax.optimization_barrier((x, *others))[0]


def on_line(acts, packed, small, queries, w_gate_up, w_down, top, capacity):
    rows, width = acts.shape
    line = [packed, forward(packed), None, backward(packed)]
    crossed = [across(packed), across(line[1]), None, across(line[3])]
    to_core = other_core(packed)
    small = hold(after(small, to_core), in_vmem(w_gate_up, w_down))
    pair = jnp.concatenate([small, across(small)], axis=0)
    line[2] = forward(after(line[1], pair, crossed[0]))
    crossed[2] = across(line[2])
    arrays = [
        [
            line[step],
            crossed[step],
            other_core(line[step]) if step else to_core,
            other_core(crossed[step]),
        ]
        for step in range(LINE)
    ]
    order = (0, 1, 3, 2)
    blocks = [
        (4 * step + core * 2 + y, 2 * at + y, core, functools.partial(from_device, step, y, core))
        for core in range(2)
        for at, step in enumerate(order)
        for y in range(2)
    ]

    def swap_planes(pieces):
        both = jnp.concatenate(pieces, axis=0)
        shares = both.reshape(-1, small.shape[0], both.shape[1])[:, rows:]
        return lax.ppermute(shares.reshape(-1, both.shape[1]), "grp", [(0, 1), (1, 0)])

    pair = after(pair, line[3])
    pairs = [pair, forward(pair), None, backward(pair)]
    pairs[2] = forward(pairs[1])
    keep, mine, crossing = [None] * LINE, [None] * LINE, [None] * LINE

    def experts(first, second, before, beside, split):
        ready = arrays[first] + arrays[second]
        ready = [after(ready[0], *before), *ready[1:]]
        sources = [[(4 * group + i, 0, rows) for i in range(4)] for group in range(2)]
        targets = [
            [(group, 0, 2 * rows), (3, 0, 2 * rows) if group * split else (2, group * 2 * rows, 2 * rows)]
            for group in range(2)
        ]
        keep[first], keep[second], send, *last = run_experts(
            ready,
            sources,
            targets,
            [2 * rows] * 4 if split else [2 * rows, 2 * rows, 4 * rows],
            w_gate_up,
            w_down,
            top,
            rows,
            capacity,
        )
        came = other_core(after(send, *beside))
        mine[first] = (keep[first][:rows], came[:rows])
        crossing[first] = summed(keep[first][rows:], came[rows : 2 * rows])
        if split:
            came = other_core(after(last[0], crossing[first]))
        else:
            came = came[2 * rows :]
        mine[second] = (keep[second][:rows], came[:rows])
        crossing[second] = summed(keep[second][rows:], came[rows:])
        return send

    theirs = [None] * LINE
    experts(1, 0, [line[2], crossed[3]], [crossed[2], pairs[1], pairs[3]], False)
    theirs[1] = across(crossing[1])
    near = swap_planes([pairs[0], pairs[1], pairs[3]])
    send = experts(2, 3, [crossing[0], crossing[1]], [theirs[1], pairs[2], near], True)
    total = summed(*mine[1], after(theirs[1], send))
    moving = forward(total)
    theirs[2], theirs[3] = across(crossing[2]), across(crossing[3])
    far = swap_planes([after(pairs[2], total)])
    own = after(jnp.concatenate([pairs[step] for step in order], axis=0), total)
    smalls = [own, near, far, other_core(own), other_core(after(near, total)), other_core(far)]
    total = summed(*mine[2], theirs[2], after(moving, *smalls[3:]))
    moving = forward(total)
    theirs[0] = across(after(crossing[0], total))
    smalls[0] = after(own, total)
    new_keys, values = make_values(sum(arrays, []), blocks, smalls, rows, width)
    context = attend_part(queries, new_keys, values, 0, 4)
    context = attend_part(queries, new_keys, values, 1, 4, context)
    total = summed(*mine[3], theirs[3], after(moving, context))
    moving = forward(total)
    queries = after(queries, total)
    for part in range(2, 4):
        context = attend_part(queries, new_keys, values, part, 4, context)
    layer_out = summed(acts, *mine[0], theirs[0], after(moving, context))
    return context, layer_out


def on_any(acts, packed, small, queries, w_gate_up, w_down, top, capacity):
    rows, width = acts.shape
    keys, value_weight = small[:rows], small[rows:]
    gathered = lax.all_gather(packed, "seq", axis=0, tiled=True)
    all_keys = lax.all_gather(keys, "seq", axis=0, tiled=True)
    weight = lax.all_gather(value_weight, "seq", axis=0, tiled=True)
    total = gathered.shape[0]
    part = total // GROUPS
    pieces = [[(0, group * part, part)] for group in range(GROUPS)]
    (partial,) = run_experts(
        [gathered], pieces, pieces, [total], w_gate_up, w_down, top, rows, capacity
    )
    values = dot(gathered[:, :width], weight).astype(BF16)
    context = None
    for part in range(KEY_VALUE_HEADS):
        context = attend_part(queries, all_keys, values, part, KEY_VALUE_HEADS, context)
    combined = lax.psum_scatter(partial, "seq", scatter_dimension=0, tiled=True)
    return context, summed(acts, combined)


def per_device(
    activations, queries, keys, norm_gain, value_weight, expert_ids, gate_weights, w_gate_up, w_down
):
    pos_rows, sequence_count, model_width = activations.shape
    assert sequence_count == 1 and w_down.shape[0] == 1
    top = expert_ids.shape[2]
    devices = lax.axis_size("seq")
    capacity = max(2, 3 * pos_rows * top // (2 * devices))
    acts = activations.reshape(pos_rows, model_width)
    halves = 2 * devices * pos_rows == model_width and value_weight.shape[0] % (2 * pos_rows) == 0
    line = devices == 4 * LINE and lax.axis_size("grp") == 2 and halves
    packed, small = pack(
        acts,
        norm_gain,
        expert_ids.transpose(1, 2, 0).reshape(top, pos_rows),
        gate_weights.transpose(1, 2, 0).reshape(top, pos_rows),
        keys.reshape(pos_rows, -1),
        value_weight,
        2 if line else 1,
    )
    way = on_line if line else on_any
    context, layer_out = way(
        acts,
        packed,
        small,
        queries.reshape(pos_rows, -1),
        w_gate_up[0],
        w_down[0],
        top,
        capacity,
    )
    return (context.reshape(queries.shape), layer_out.reshape(activations.shape))


def solution(mesh):
    placed = (
        P("seq", "grp", None),
        P("seq", "grp", None),
        P("seq", "grp", None),
        P(),
        P("seq", None),
        P("seq", "grp", None),
        P("seq", "grp", None),
        P("seq", None, None),
        P("seq", None, None),
    )
    return jax.shard_map(
        per_device,
        mesh=mesh,
        in_specs=placed,
        out_specs=(P("seq", "grp", None), P("seq", "grp", None)),
        check_vma=False,
    )
```

```python
import functools
import math

import jax
import jax.numpy as jnp
from jax import lax
from jax.experimental import pallas as pl
from jax.experimental.pallas import tpu as pltpu
from jax.sharding import PartitionSpec as P

QUERY_HEADS = 32
KEY_VALUE_HEADS = 2
HEAD_DIMENSION = 128
GROUPS = 4
META = 128
LINE = 4
VMEM_LIMIT = 24 * 2**20
F32 = jnp.float32
BF16 = jnp.bfloat16
ANY = pl.BlockSpec(memory_space=pl.ANY)
SHORT = pl.CostEstimate(flops=1, bytes_accessed=1, transcendentals=0)
IN_VMEM = pl.BlockSpec(memory_space=pltpu.VMEM)


def dot(a, b):
    return jnp.dot(a, b, preferred_element_type=F32)


RING = (0, 1, 3, 2)


def device_index(place, y, core):
    return (RING[place % LINE] * 2 + y) * 2 + core


def swaps(flip_y, flip_core):
    return [
        (device_index(p, y, c), device_index(p, y ^ flip_y, c ^ flip_core))
        for p in range(LINE)
        for y in range(2)
        for c in range(2)
    ]


def ring_steps(steps):
    return [
        (device_index(p, y, c), device_index(p + steps, y, c))
        for p in range(LINE)
        for y in range(2)
        for c in range(2)
    ]


def forward(x):
    return lax.ppermute(x, "seq", ring_steps(1))


def backward(x):
    return lax.ppermute(x, "seq", ring_steps(LINE - 1))


def across(x):
    return lax.ppermute(x, "seq", swaps(1, 0))


def other_core(x):
    return lax.ppermute(x, "seq", swaps(0, 1))


def from_device(steps, flip_y, flip_core):
    me = lax.axis_index("seq")
    core, y, line = me % 2, me // 2 % 2, me // 4
    place = sum(jnp.where(line == RING[p], p, 0) for p in range(LINE))
    place = (place + LINE - steps) % LINE
    line = sum(jnp.where(place == p, RING[p], 0) for p in range(LINE))
    y = 1 - y if flip_y else y
    core = 1 - core if flip_core else core
    return (line * 2 + y) * 2 + core


def pack_kernel(
    act_ref, gain_ref, ids_ref, gates_ref, key_ref, weight_ref, out_ref, small_ref, meta_ref
):
    width = act_ref.shape[1]
    rows = act_ref.shape[0]
    top = ids_ref.shape[0]
    features = act_ref[...].astype(F32)
    inverse = lax.rsqrt(jnp.mean(features * features, axis=-1, keepdims=True) + 1e-06)
    out_ref[:, :width] = (features * inverse * gain_ref[...]).astype(BF16)
    gates = gates_ref[...]
    high = gates.astype(BF16).astype(F32)
    rest = gates - high
    middle = rest.astype(BF16).astype(F32)
    meta_ref[...] = jnp.zeros_like(meta_ref)
    meta_ref[0:top, 0:rows] = ids_ref[...].astype(F32)
    meta_ref[8 : 8 + top, 0:rows] = high
    meta_ref[16 : 16 + top, 0:rows] = middle
    meta_ref[24 : 24 + top, 0:rows] = rest - middle
    out_ref[:, width:] = meta_ref[...].T[:rows, :].astype(BF16)
    small_ref[:rows] = key_ref[...]
    share = small_ref.shape[0] - rows
    first = 0
    if share < weight_ref.shape[0]:
        first = pl.multiple_of(lax.axis_index("grp") * share, share)
    small_ref[rows:] = weight_ref[pl.ds(first, share)]


def pack(activations, norm_gain, ids, gates, keys, value_weight, planes):
    rows, width = activations.shape
    small_rows = rows + value_weight.shape[0] // planes
    assert rows <= META and ids.shape[0] <= 8
    return pl.pallas_call(
        pack_kernel,
        out_shape=[
            jax.ShapeDtypeStruct((rows, width + META), BF16),
            jax.ShapeDtypeStruct((small_rows, keys.shape[1]), BF16),
        ],
        scratch_shapes=[pltpu.VMEM((META, META), F32)],
        cost_estimate=SHORT,
        name="normalize_and_pack",
    )(activations, norm_gain.reshape(1, width), ids, gates, keys, value_weight)


def hold_kernel(small_ref, up_ref, down_ref, out_ref):
    out_ref[...] = small_ref[...]


def hold(small, weights):
    return pl.pallas_call(
        hold_kernel,
        out_shape=jax.ShapeDtypeStruct(small.shape, small.dtype),
        in_specs=[IN_VMEM] * 3,
        out_specs=IN_VMEM,
        compiler_params=pltpu.CompilerParams(vmem_limit_bytes=4 * 2**20),
        cost_estimate=SHORT,
        name="hold_weights",
    )(small, *weights)


def in_vmem(*arrays):
    return [pltpu.with_memory_space_constraint(x, pltpu.VMEM) for x in arrays]


def expert_kernel(top, tok_rows, capacity, direct, sources, targets, *refs):
    inputs = 1 + max(s[0] for group in sources for s in group)
    outputs = 1 + max(t[0] for group in targets for t in group)
    x_hbm = refs[:inputs]
    up_ref, down_ref = refs[inputs : inputs + 2]
    out_hbm = refs[inputs + 2 : inputs + 2 + outputs]
    slot_rows, slot_gates, places, hidden, result, *rest = refs[inputs + 2 + outputs :]
    groups, rows, _ = places.shape
    units, width = down_ref.shape
    packed = width + META
    slots = slot_rows.shape[0] // groups
    tile = 256
    me = lax.axis_index("seq").astype(F32)
    if direct:

        def read(group, columns):
            return jnp.concatenate(
                [x_hbm[operand][:, columns] for operand, _, _ in sources[group]], axis=0
            )

        def write(group, columns, value):
            at = 0
            for operand, first, count in targets[group]:
                out_hbm[operand][first : first + count, columns] = value[at : at + count]
                at += count

    else:
        x_buf, x_sem, out_sem = rest

        def read(group, columns):
            return x_buf[group, :, columns]

        def write(group, columns, value):
            x_buf[group, :, columns] = value

    def loads(group):
        copies, at = [], 0
        for number, (operand, first, count) in enumerate([] if direct else sources[group]):
            copies.append(
                pltpu.make_async_copy(
                    x_hbm[operand].at[pl.ds(first, count)],
                    x_buf.at[group, pl.ds(at, count)],
                    x_sem.at[group, number],
                )
            )
            at += count
        return copies

    def stores(group):
        copies, at = [], 0
        for number, (operand, first, count) in enumerate([] if direct else targets[group]):
            copies.append(
                pltpu.make_async_copy(
                    x_buf.at[group, pl.ds(at, count), pl.ds(0, width)],
                    out_hbm[operand].at[pl.ds(first, count)],
                    out_sem.at[group, number],
                )
            )
            at += count
        return copies

    for group in range(groups):
        for copy in loads(group):
            copy.start()

    chunk = tok_rows * META // math.gcd(tok_rows, META)
    first = lax.broadcasted_iota(jnp.int32, (chunk, chunk), 0)
    second = lax.broadcasted_iota(jnp.int32, (chunk, chunk), 1)
    earlier = ((first < second) & (first // tok_rows == second // tok_rows)).astype(F32).astype(BF16)
    block = lax.broadcasted_iota(jnp.int32, (1, rows), 1) // tok_rows
    for group in range(groups):
        for copy in loads(group):
            copy.wait()
        meta = read(group, slice(width, packed)).astype(F32).T
        gate = jnp.zeros((1, rows), F32)
        named = jnp.zeros((1, rows), F32)
        for k in range(top):
            match = meta[k : k + 1] == me
            value = meta[8 + k : 9 + k] + (meta[16 + k : 17 + k] + meta[24 + k : 25 + k])
            gate = jnp.where(match, value, gate)
            named = jnp.where(match, 1.0, named)
        marks = jnp.broadcast_to(named, (8, rows)).astype(BF16)
        rank = jnp.concatenate(
            [dot(marks[:, at : at + chunk], earlier) for at in range(0, rows, chunk)], axis=1
        )[0:1]
        slot = jnp.where(named > 0.0, (block * capacity).astype(F32) + rank, -1.0)
        spots = lax.broadcasted_iota(jnp.int32, (slots, rows), 0).astype(F32)
        chosen = spots == slot
        slot_gates[pl.ds(group * slots, slots)] = jnp.broadcast_to(
            jnp.sum(jnp.where(chosen, gate, 0.0), axis=1, keepdims=True), (slots, META)
        )
        pick = chosen.astype(F32).astype(BF16)
        for at in range(0, width, 512):
            slot_rows[pl.ds(group * slots, slots), at : at + 512] = dot(
                pick, read(group, slice(at, at + 512))
            ).astype(BF16)
        by_row = jnp.broadcast_to(slot, (META, rows)).T
        spots = lax.broadcasted_iota(jnp.int32, (rows, META), 1).astype(F32)
        places[group] = (spots == by_row).astype(F32).astype(BF16)

    for at in range(0, units, tile):
        gate = dot(slot_rows[...], up_ref[:, at : at + tile])
        up = dot(slot_rows[...], up_ref[:, units + at : units + at + tile])
        hidden[:, at : at + tile] = (gate / (1.0 + jnp.exp(-gate)) * up).astype(BF16)
    for at in range(0, width, tile):
        out = dot(hidden[...], down_ref[:, at : at + tile]).astype(BF16).astype(F32)
        result[:, at : at + tile] = (out * slot_gates[:, 0:1]).astype(BF16)
    for group in range(groups):
        for at in range(0, width, 512):
            placed = dot(
                places[group, :, :slots], result[pl.ds(group * slots, slots), at : at + 512]
            )
            write(group, slice(at, at + 512), placed.astype(BF16))
        for copy in stores(group):
            copy.start()
    for group in range(groups):
        for copy in stores(group):
            copy.wait()


def run_experts(arrays, sources, targets, out_rows, w_gate_up, w_down, top, tok_rows, capacity):
    direct = len(arrays) > 1
    groups = len(sources)
    rows = sum(count for _, _, count in sources[0])
    total = groups * rows
    units, width = w_down.shape
    packed = width + META
    slots = rows // tok_rows * capacity
    assert slots % 16 == 0 and slots <= META and units % 256 == 0 and width % 512 == 0
    all_slots = groups * slots
    held = 2 * total * (packed + META) + all_slots * (4 * width + 2 * units + 4 * META)
    scratch = [
        pltpu.VMEM((all_slots, width), BF16),
        pltpu.VMEM((all_slots, META), F32),
        pltpu.VMEM((groups, rows, META), BF16),
        pltpu.VMEM((all_slots, units), BF16),
        pltpu.VMEM((all_slots, width), BF16),
    ]
    if not direct:
        scratch += [
            pltpu.VMEM((groups, rows, packed), BF16),
            pltpu.SemaphoreType.DMA((groups, max(len(s) for s in sources))),
            pltpu.SemaphoreType.DMA((groups, max(len(t) for t in targets))),
        ]
    shape = pltpu.VMEM if direct else jax.ShapeDtypeStruct
    place = IN_VMEM if direct else ANY
    return pl.pallas_call(
        functools.partial(expert_kernel, top, tok_rows, capacity, direct, sources, targets),
        out_shape=[shape((count, width), BF16) for count in out_rows],
        in_specs=[place] * len(arrays) + [IN_VMEM] * 2,
        out_specs=[place] * len(out_rows),
        scratch_shapes=scratch,
        compiler_params=pltpu.CompilerParams(vmem_limit_bytes=held + 8 * 2**20),
        cost_estimate=SHORT,
        name="experts",
    )(*(in_vmem(*arrays) if direct else arrays), *in_vmem(w_gate_up, w_down))


def value_kernel(key_rows, blocks, *refs):
    count = len(blocks)
    x_refs, smalls = refs[:count], refs[count : count + 6]
    key_ref, value_ref, weight = refs[count + 6 :]
    width = weight.shape[0]
    share = width // count // 2
    plane = lax.axis_index("grp")
    places = [device() for _, _, _, device in blocks]

    def below(number, size):
        return pl.ds(pl.multiple_of(number * size, size), size)

    for (_, at, core, _), place in zip(blocks, places):
        own, near, far = smalls[3 * core : 3 * core + 3]
        other, there = (near, at) if at * share < near.shape[0] else (far, at - near.shape[0] // share)
        first = at * (key_rows + share)
        key_ref[below(place, key_rows)] = own[first : first + key_rows]
        weight[below(2 * place + plane, share)] = own[first + key_rows : first + key_rows + share]
        weight[below(2 * place + 1 - plane, share)] = other[there * share : (there + 1) * share]
    for start in range(0, count, 4):
        rows = [x_refs[operand][:, :width] for operand, _, _, _ in blocks[start : start + 4]]
        values = dot(jnp.concatenate(rows, axis=0), weight[...]).astype(BF16)
        for number in range(4):
            value_ref[below(places[start + number], key_rows)] = values[
                number * key_rows : (number + 1) * key_rows
            ]


def make_values(arrays, blocks, smalls, key_rows, width):
    kv_width = smalls[0].shape[1]
    kv = jax.ShapeDtypeStruct((key_rows * len(blocks), kv_width), BF16)
    return pl.pallas_call(
        functools.partial(value_kernel, key_rows, blocks),
        out_shape=[kv, kv],
        in_specs=[IN_VMEM] * (len(arrays) + len(smalls)),
        out_specs=[IN_VMEM] * 2,
        scratch_shapes=[pltpu.VMEM((width, kv_width), BF16)],
        compiler_params=pltpu.CompilerParams(vmem_limit_bytes=VMEM_LIMIT),
        cost_estimate=SHORT,
        name="values",
    )(*in_vmem(*arrays, *smalls))


def attention_kernel(chunk, q_ref, k_ref, v_ref, *refs):
    out_ref = refs[-1]
    q_rows, q_width = q_ref.shape
    heads = q_width // HEAD_DIMENSION
    together = 4
    q_start = lax.axis_index("seq") * q_rows
    factor = math.log2(math.e) / math.sqrt(HEAD_DIMENSION)
    steps = k_ref.shape[0] // chunk
    tall = together * q_rows

    def scored(rows, start):
        scores = lax.dot_general(
            rows, k_ref[pl.ds(start, chunk)], (((1,), (1,)), ((), ())), preferred_element_type=F32
        )
        q_at = q_start + lax.broadcasted_iota(jnp.int32, (q_rows, chunk), 0)
        k_at = start + lax.broadcasted_iota(jnp.int32, (q_rows, chunk), 1)
        bias = jnp.where(q_at >= k_at, 0.0, -1e30)[None]
        return (scores.reshape(together, q_rows, chunk) + bias).reshape(tall, chunk)

    for at in range(0, heads, together):
        rows = jnp.concatenate(
            [
                q_ref[:, h * HEAD_DIMENSION : (h + 1) * HEAD_DIMENSION]
                for h in range(at, at + together)
            ],
            axis=0,
        )

        def one(step, state):
            top_score, run_sum, run_acc = state
            start = pl.multiple_of(step * chunk, chunk)
            scores = scored(rows, start)
            best = jnp.maximum(jnp.max(scores, axis=1, keepdims=True), top_score)
            rescale = jnp.exp2((top_score - best) * factor)
            weights = jnp.exp2((scores - best) * factor)
            total = run_sum * rescale + jnp.sum(weights, axis=1, keepdims=True)
            added = dot(weights.astype(BF16), v_ref[pl.ds(start, chunk)])
            return (best, total, run_acc * rescale + added)

        if steps == 1:
            scores = scored(rows, 0)
            best = jnp.max(scores, axis=1, keepdims=True)
            weights = jnp.exp2((scores - best) * factor)
            total = jnp.sum(weights, axis=1, keepdims=True)
            added = dot(weights.astype(BF16), v_ref[...])
        else:
            best, total, added = lax.fori_loop(
                0,
                (q_start + q_rows + chunk - 1) // chunk,
                one,
                (
                    jnp.full((tall, 1), -1e30, F32),
                    jnp.zeros((tall, 1), F32),
                    jnp.zeros((tall, HEAD_DIMENSION), F32),
                ),
            )
        context = (added / total).astype(BF16)
        for h in range(together):
            out_ref[:, (at + h) * HEAD_DIMENSION : (at + h + 1) * HEAD_DIMENSION] = context[
                h * q_rows : (h + 1) * q_rows
            ]


def attend_part(queries, keys, values, part, parts, context=None):
    q_rows, q_width = queries.shape
    total = keys.shape[0]
    part_width = q_width // parts
    per_kv = parts // KEY_VALUE_HEADS
    chunk = math.gcd(total, 1024)
    before = () if context is None else (context,)
    return pl.pallas_call(
        functools.partial(attention_kernel, chunk),
        grid=(1,),
        out_shape=jax.ShapeDtypeStruct((q_rows, q_width), BF16),
        in_specs=[
            pl.BlockSpec((q_rows, part_width), lambda i: (0, part)),
            pl.BlockSpec((total, HEAD_DIMENSION), lambda i: (0, part // per_kv)),
            pl.BlockSpec((total, HEAD_DIMENSION), lambda i: (0, part // per_kv)),
            *[ANY for _ in before],
        ],
        out_specs=pl.BlockSpec((q_rows, part_width), lambda i: (0, part)),
        input_output_aliases={3: 0} if before else {},
        compiler_params=pltpu.CompilerParams(vmem_limit_bytes=VMEM_LIMIT),
        cost_estimate=SHORT,
        name="attention",
    )(queries, keys, values, *before)


def summed(*terms):
    return sum(term.astype(F32) for term in terms).astype(BF16)


def after(x, *others):
    return lax.optimization_barrier((x, *others))[0]


def on_line(acts, packed, small, queries, w_gate_up, w_down, top, capacity):
    rows, width = acts.shape
    line = [packed, forward(packed), None, backward(packed)]
    crossed = [across(packed), across(line[1]), None, across(line[3])]
    to_core = other_core(packed)
    small = hold(after(small, to_core), in_vmem(w_gate_up, w_down))
    pair = jnp.concatenate([small, across(small)], axis=0)
    line[2] = forward(after(line[1], pair, crossed[0]))
    crossed[2] = across(line[2])
    arrays = [
        [
            line[step],
            crossed[step],
            other_core(line[step]) if step else to_core,
            other_core(crossed[step]),
        ]
        for step in range(LINE)
    ]
    order = (0, 1, 3, 2)
    blocks = [
        (4 * step + core * 2 + y, 2 * at + y, core, functools.partial(from_device, step, y, core))
        for core in range(2)
        for at, step in enumerate(order)
        for y in range(2)
    ]

    def swap_planes(pieces):
        both = jnp.concatenate(pieces, axis=0)
        shares = both.reshape(-1, small.shape[0], both.shape[1])[:, rows:]
        return lax.ppermute(shares.reshape(-1, both.shape[1]), "grp", [(0, 1), (1, 0)])

    pair = after(pair, line[3])
    pairs = [pair, forward(pair), None, backward(pair)]
    pairs[2] = forward(pairs[1])
    keep, mine, crossing = [None] * LINE, [None] * LINE, [None] * LINE

    def experts(first, second, before, beside, split):
        ready = arrays[first] + arrays[second]
        ready = [after(ready[0], *before), *ready[1:]]
        sources = [[(4 * group + i, 0, rows) for i in range(4)] for group in range(2)]
        targets = [
            [(group, 0, 2 * rows), (3, 0, 2 * rows) if group * split else (2, group * 2 * rows, 2 * rows)]
            for group in range(2)
        ]
        keep[first], keep[second], send, *last = run_experts(
            ready,
            sources,
            targets,
            [2 * rows] * 4 if split else [2 * rows, 2 * rows, 4 * rows],
            w_gate_up,
            w_down,
            top,
            rows,
            capacity,
        )
        came = other_core(after(send, *beside))
        mine[first] = (keep[first][:rows], came[:rows])
        crossing[first] = summed(keep[first][rows:], came[rows : 2 * rows])
        if split:
            came = other_core(after(last[0], crossing[first]))
        else:
            came = came[2 * rows :]
        mine[second] = (keep[second][:rows], came[:rows])
        crossing[second] = summed(keep[second][rows:], came[rows:])
        return send

    theirs = [None] * LINE
    experts(1, 0, [line[2], crossed[3]], [crossed[2], pairs[1], pairs[3]], False)
    theirs[1] = across(crossing[1])
    near = swap_planes([pairs[0], pairs[1], pairs[3]])
    send = experts(2, 3, [crossing[0], crossing[1]], [theirs[1], pairs[2], near], True)
    total = summed(*mine[1], after(theirs[1], send))
    moving = forward(total)
    theirs[2], theirs[3] = across(crossing[2]), across(crossing[3])
    far = swap_planes([after(pairs[2], total)])
    own = after(jnp.concatenate([pairs[step] for step in order], axis=0), total)
    smalls = [own, near, far, other_core(own), other_core(after(near, total)), other_core(far)]
    total = summed(*mine[2], theirs[2], after(moving, far, *smalls[3:5]))
    moving = forward(total)
    theirs[0] = across(after(crossing[0], total))
    smalls[0] = after(own, total)
    new_keys, values = make_values(sum(arrays, []), blocks, smalls, rows, width)
    context = attend_part(queries, new_keys, values, 0, 4)
    context = attend_part(queries, new_keys, values, 1, 4, context)
    total = summed(*mine[3], theirs[3], after(moving, context))
    moving = forward(total)
    queries = after(queries, total)
    for part in range(2, 4):
        context = attend_part(queries, new_keys, values, part, 4, context)
    layer_out = summed(acts, *mine[0], theirs[0], after(moving, context))
    return context, layer_out


def on_any(acts, packed, small, queries, w_gate_up, w_down, top, capacity):
    rows, width = acts.shape
    keys, value_weight = small[:rows], small[rows:]
    gathered = lax.all_gather(packed, "seq", axis=0, tiled=True)
    all_keys = lax.all_gather(keys, "seq", axis=0, tiled=True)
    weight = lax.all_gather(value_weight, "seq", axis=0, tiled=True)
    total = gathered.shape[0]
    part = total // GROUPS
    pieces = [[(0, group * part, part)] for group in range(GROUPS)]
    (partial,) = run_experts(
        [gathered], pieces, pieces, [total], w_gate_up, w_down, top, rows, capacity
    )
    values = dot(gathered[:, :width], weight).astype(BF16)
    context = None
    for part in range(KEY_VALUE_HEADS):
        context = attend_part(queries, all_keys, values, part, KEY_VALUE_HEADS, context)
    combined = lax.psum_scatter(partial, "seq", scatter_dimension=0, tiled=True)
    return context, summed(acts, combined)


def per_device(
    activations, queries, keys, norm_gain, value_weight, expert_ids, gate_weights, w_gate_up, w_down
):
    pos_rows, sequence_count, model_width = activations.shape
    assert sequence_count == 1 and w_down.shape[0] == 1
    top = expert_ids.shape[2]
    devices = lax.axis_size("seq")
    capacity = max(2, 3 * pos_rows * top // (2 * devices))
    acts = activations.reshape(pos_rows, model_width)
    halves = 2 * devices * pos_rows == model_width and value_weight.shape[0] % (2 * pos_rows) == 0
    line = devices == 4 * LINE and lax.axis_size("grp") == 2 and halves
    packed, small = pack(
        acts,
        norm_gain,
        expert_ids.transpose(1, 2, 0).reshape(top, pos_rows),
        gate_weights.transpose(1, 2, 0).reshape(top, pos_rows),
        keys.reshape(pos_rows, -1),
        value_weight,
        2 if line else 1,
    )
    way = on_line if line else on_any
    context, layer_out = way(
        acts,
        packed,
        small,
        queries.reshape(pos_rows, -1),
        w_gate_up[0],
        w_down[0],
        top,
        capacity,
    )
    return (context.reshape(queries.shape), layer_out.reshape(activations.shape))


def solution(mesh):
    placed = (
        P("seq", "grp", None),
        P("seq", "grp", None),
        P("seq", "grp", None),
        P(),
        P("seq", None),
        P("seq", "grp", None),
        P("seq", "grp", None),
        P("seq", None, None),
        P("seq", None, None),
    )
    return jax.shard_map(
        per_device,
        mesh=mesh,
        in_specs=placed,
        out_specs=(P("seq", "grp", None), P("seq", "grp", None)),
        check_vma=False,
    )
```

```python
import functools
import math

import jax
import jax.numpy as jnp
from jax import lax
from jax.experimental import pallas as pl
from jax.experimental.pallas import tpu as pltpu
from jax.sharding import PartitionSpec as P

QUERY_HEADS = 32
KEY_VALUE_HEADS = 2
HEAD_DIMENSION = 128
GROUPS = 4
META = 128
LINE = 4
VMEM_LIMIT = 24 * 2**20
F32 = jnp.float32
BF16 = jnp.bfloat16
ANY = pl.BlockSpec(memory_space=pl.ANY)
SHORT = pl.CostEstimate(flops=1, bytes_accessed=1, transcendentals=0)
IN_VMEM = pl.BlockSpec(memory_space=pltpu.VMEM)


def dot(a, b):
    return jnp.dot(a, b, preferred_element_type=F32)


RING = (0, 1, 3, 2)


def device_index(place, y, core):
    return (RING[place % LINE] * 2 + y) * 2 + core


def swaps(flip_y, flip_core):
    return [
        (device_index(p, y, c), device_index(p, y ^ flip_y, c ^ flip_core))
        for p in range(LINE)
        for y in range(2)
        for c in range(2)
    ]


def ring_steps(steps):
    return [
        (device_index(p, y, c), device_index(p + steps, y, c))
        for p in range(LINE)
        for y in range(2)
        for c in range(2)
    ]


def forward(x):
    return lax.ppermute(x, "seq", ring_steps(1))


def backward(x):
    return lax.ppermute(x, "seq", ring_steps(LINE - 1))


def across(x):
    return lax.ppermute(x, "seq", swaps(1, 0))


def other_core(x):
    return lax.ppermute(x, "seq", swaps(0, 1))


def from_device(steps, flip_y, flip_core):
    me = lax.axis_index("seq")
    core, y, line = me % 2, me // 2 % 2, me // 4
    place = sum(jnp.where(line == RING[p], p, 0) for p in range(LINE))
    place = (place + LINE - steps) % LINE
    line = sum(jnp.where(place == p, RING[p], 0) for p in range(LINE))
    y = 1 - y if flip_y else y
    core = 1 - core if flip_core else core
    return (line * 2 + y) * 2 + core


def pack_kernel(
    act_ref, gain_ref, ids_ref, gates_ref, key_ref, weight_ref, out_ref, small_ref, meta_ref
):
    width = act_ref.shape[1]
    rows = act_ref.shape[0]
    top = ids_ref.shape[0]
    features = act_ref[...].astype(F32)
    inverse = lax.rsqrt(jnp.mean(features * features, axis=-1, keepdims=True) + 1e-06)
    out_ref[:, :width] = (features * inverse * gain_ref[...]).astype(BF16)
    gates = gates_ref[...]
    high = gates.astype(BF16).astype(F32)
    rest = gates - high
    middle = rest.astype(BF16).astype(F32)
    meta_ref[...] = jnp.zeros_like(meta_ref)
    meta_ref[0:top, 0:rows] = ids_ref[...].astype(F32)
    meta_ref[8 : 8 + top, 0:rows] = high
    meta_ref[16 : 16 + top, 0:rows] = middle
    meta_ref[24 : 24 + top, 0:rows] = rest - middle
    out_ref[:, width:] = meta_ref[...].T[:rows, :].astype(BF16)
    small_ref[:rows] = key_ref[...]
    share = small_ref.shape[0] - rows
    first = 0
    if share < weight_ref.shape[0]:
        first = pl.multiple_of(lax.axis_index("grp") * share, share)
    small_ref[rows:] = weight_ref[pl.ds(first, share)]


def pack(activations, norm_gain, ids, gates, keys, value_weight, planes):
    rows, width = activations.shape
    small_rows = rows + value_weight.shape[0] // planes
    assert rows <= META and ids.shape[0] <= 8
    return pl.pallas_call(
        pack_kernel,
        out_shape=[
            jax.ShapeDtypeStruct((rows, width + META), BF16),
            jax.ShapeDtypeStruct((small_rows, keys.shape[1]), BF16),
        ],
        scratch_shapes=[pltpu.VMEM((META, META), F32)],
        cost_estimate=SHORT,
        name="normalize_and_pack",
    )(activations, norm_gain.reshape(1, width), ids, gates, keys, value_weight)


def hold_kernel(small_ref, up_ref, down_ref, out_ref):
    out_ref[...] = small_ref[...]


def hold(small, weights):
    return pl.pallas_call(
        hold_kernel,
        out_shape=jax.ShapeDtypeStruct(small.shape, small.dtype),
        in_specs=[IN_VMEM] * 3,
        out_specs=IN_VMEM,
        compiler_params=pltpu.CompilerParams(vmem_limit_bytes=4 * 2**20),
        cost_estimate=SHORT,
        name="hold_weights",
    )(small, *weights)


def in_vmem(*arrays):
    return [pltpu.with_memory_space_constraint(x, pltpu.VMEM) for x in arrays]


def expert_kernel(top, tok_rows, capacity, direct, sources, targets, *refs):
    inputs = 1 + max(s[0] for group in sources for s in group)
    outputs = 1 + max(t[0] for group in targets for t in group)
    x_hbm = refs[:inputs]
    up_ref, down_ref = refs[inputs : inputs + 2]
    out_hbm = refs[inputs + 2 : inputs + 2 + outputs]
    slot_rows, slot_gates, places, hidden, result, *rest = refs[inputs + 2 + outputs :]
    groups, rows, _ = places.shape
    units, width = down_ref.shape
    packed = width + META
    slots = slot_rows.shape[0] // groups
    tile = 256
    me = lax.axis_index("seq").astype(F32)
    if direct:

        def read(group, columns):
            return jnp.concatenate(
                [x_hbm[operand][:, columns] for operand, _, _ in sources[group]], axis=0
            )

        def write(group, columns, value):
            at = 0
            for operand, first, count in targets[group]:
                out_hbm[operand][first : first + count, columns] = value[at : at + count]
                at += count

    else:
        x_buf, x_sem, out_sem = rest

        def read(group, columns):
            return x_buf[group, :, columns]

        def write(group, columns, value):
            x_buf[group, :, columns] = value

    def loads(group):
        copies, at = [], 0
        for number, (operand, first, count) in enumerate([] if direct else sources[group]):
            copies.append(
                pltpu.make_async_copy(
                    x_hbm[operand].at[pl.ds(first, count)],
                    x_buf.at[group, pl.ds(at, count)],
                    x_sem.at[group, number],
                )
            )
            at += count
        return copies

    def stores(group):
        copies, at = [], 0
        for number, (operand, first, count) in enumerate([] if direct else targets[group]):
            copies.append(
                pltpu.make_async_copy(
                    x_buf.at[group, pl.ds(at, count), pl.ds(0, width)],
                    out_hbm[operand].at[pl.ds(first, count)],
                    out_sem.at[group, number],
                )
            )
            at += count
        return copies

    for group in range(groups):
        for copy in loads(group):
            copy.start()

    chunk = tok_rows * META // math.gcd(tok_rows, META)
    first = lax.broadcasted_iota(jnp.int32, (chunk, chunk), 0)
    second = lax.broadcasted_iota(jnp.int32, (chunk, chunk), 1)
    earlier = ((first < second) & (first // tok_rows == second // tok_rows)).astype(F32).astype(BF16)
    block = lax.broadcasted_iota(jnp.int32, (1, rows), 1) // tok_rows
    for group in range(groups):
        for copy in loads(group):
            copy.wait()
        meta = read(group, slice(width, packed)).astype(F32).T
        gate = jnp.zeros((1, rows), F32)
        named = jnp.zeros((1, rows), F32)
        for k in range(top):
            match = meta[k : k + 1] == me
            value = meta[8 + k : 9 + k] + (meta[16 + k : 17 + k] + meta[24 + k : 25 + k])
            gate = jnp.where(match, value, gate)
            named = jnp.where(match, 1.0, named)
        marks = jnp.broadcast_to(named, (8, rows)).astype(BF16)
        rank = jnp.concatenate(
            [dot(marks[:, at : at + chunk], earlier) for at in range(0, rows, chunk)], axis=1
        )[0:1]
        slot = jnp.where(named > 0.0, (block * capacity).astype(F32) + rank, -1.0)
        spots = lax.broadcasted_iota(jnp.int32, (slots, rows), 0).astype(F32)
        chosen = spots == slot
        slot_gates[pl.ds(group * slots, slots)] = jnp.broadcast_to(
            jnp.sum(jnp.where(chosen, gate, 0.0), axis=1, keepdims=True), (slots, META)
        )
        pick = chosen.astype(F32).astype(BF16)
        for at in range(0, width, 512):
            slot_rows[pl.ds(group * slots, slots), at : at + 512] = dot(
                pick, read(group, slice(at, at + 512))
            ).astype(BF16)
        by_row = jnp.broadcast_to(slot, (META, rows)).T
        spots = lax.broadcasted_iota(jnp.int32, (rows, META), 1).astype(F32)
        places[group] = (spots == by_row).astype(F32).astype(BF16)

    for at in range(0, units, tile):
        gate = dot(slot_rows[...], up_ref[:, at : at + tile])
        up = dot(slot_rows[...], up_ref[:, units + at : units + at + tile])
        hidden[:, at : at + tile] = (gate / (1.0 + jnp.exp(-gate)) * up).astype(BF16)
    for at in range(0, width, tile):
        out = dot(hidden[...], down_ref[:, at : at + tile]).astype(BF16).astype(F32)
        result[:, at : at + tile] = (out * slot_gates[:, 0:1]).astype(BF16)
    for group in range(groups):
        for at in range(0, width, 512):
            placed = dot(
                places[group, :, :slots], result[pl.ds(group * slots, slots), at : at + 512]
            )
            write(group, slice(at, at + 512), placed.astype(BF16))
        for copy in stores(group):
            copy.start()
    for group in range(groups):
        for copy in stores(group):
            copy.wait()


def run_experts(arrays, sources, targets, out_rows, w_gate_up, w_down, top, tok_rows, capacity):
    direct = len(arrays) > 1
    groups = len(sources)
    rows = sum(count for _, _, count in sources[0])
    total = groups * rows
    units, width = w_down.shape
    packed = width + META
    slots = rows // tok_rows * capacity
    assert slots % 16 == 0 and slots <= META and units % 256 == 0 and width % 512 == 0
    all_slots = groups * slots
    held = 2 * total * (packed + META) + all_slots * (4 * width + 2 * units + 4 * META)
    scratch = [
        pltpu.VMEM((all_slots, width), BF16),
        pltpu.VMEM((all_slots, META), F32),
        pltpu.VMEM((groups, rows, META), BF16),
        pltpu.VMEM((all_slots, units), BF16),
        pltpu.VMEM((all_slots, width), BF16),
    ]
    if not direct:
        scratch += [
            pltpu.VMEM((groups, rows, packed), BF16),
            pltpu.SemaphoreType.DMA((groups, max(len(s) for s in sources))),
            pltpu.SemaphoreType.DMA((groups, max(len(t) for t in targets))),
        ]
    shape = pltpu.VMEM if direct else jax.ShapeDtypeStruct
    place = IN_VMEM if direct else ANY
    return pl.pallas_call(
        functools.partial(expert_kernel, top, tok_rows, capacity, direct, sources, targets),
        out_shape=[shape((count, width), BF16) for count in out_rows],
        in_specs=[place] * len(arrays) + [IN_VMEM] * 2,
        out_specs=[place] * len(out_rows),
        scratch_shapes=scratch,
        compiler_params=pltpu.CompilerParams(vmem_limit_bytes=held + 8 * 2**20),
        cost_estimate=SHORT,
        name="experts",
    )(*(in_vmem(*arrays) if direct else arrays), *in_vmem(w_gate_up, w_down))


def value_kernel(key_rows, blocks, *refs):
    count = len(blocks)
    x_refs, smalls = refs[:count], refs[count : count + 6]
    key_ref, value_ref, weight = refs[count + 6 :]
    width = weight.shape[0]
    share = width // count // 2
    plane = lax.axis_index("grp")
    places = [device() for _, _, _, device in blocks]

    def below(number, size):
        return pl.ds(pl.multiple_of(number * size, size), size)

    for (_, at, core, _), place in zip(blocks, places):
        own, near, far = smalls[3 * core : 3 * core + 3]
        other, there = (near, at) if at * share < near.shape[0] else (far, at - near.shape[0] // share)
        first = at * (key_rows + share)
        key_ref[below(place, key_rows)] = own[first : first + key_rows]
        weight[below(2 * place + plane, share)] = own[first + key_rows : first + key_rows + share]
        weight[below(2 * place + 1 - plane, share)] = other[there * share : (there + 1) * share]
    for start in range(0, count, 4):
        rows = [x_refs[operand][:, :width] for operand, _, _, _ in blocks[start : start + 4]]
        values = dot(jnp.concatenate(rows, axis=0), weight[...]).astype(BF16)
        for number in range(4):
            value_ref[below(places[start + number], key_rows)] = values[
                number * key_rows : (number + 1) * key_rows
            ]


def make_values(arrays, blocks, smalls, key_rows, width):
    kv_width = smalls[0].shape[1]
    kv = jax.ShapeDtypeStruct((key_rows * len(blocks), kv_width), BF16)
    return pl.pallas_call(
        functools.partial(value_kernel, key_rows, blocks),
        out_shape=[kv, kv],
        in_specs=[IN_VMEM] * (len(arrays) + len(smalls)),
        out_specs=[IN_VMEM] * 2,
        scratch_shapes=[pltpu.VMEM((width, kv_width), BF16)],
        compiler_params=pltpu.CompilerParams(vmem_limit_bytes=VMEM_LIMIT),
        cost_estimate=SHORT,
        name="values",
    )(*in_vmem(*arrays, *smalls))


def attention_kernel(chunk, q_ref, k_ref, v_ref, *refs):
    out_ref = refs[-1]
    q_rows, q_width = q_ref.shape
    heads = q_width // HEAD_DIMENSION
    together = 4
    q_start = lax.axis_index("seq") * q_rows
    factor = math.log2(math.e) / math.sqrt(HEAD_DIMENSION)
    steps = k_ref.shape[0] // chunk
    tall = together * q_rows

    def scored(rows, start):
        scores = lax.dot_general(
            rows, k_ref[pl.ds(start, chunk)], (((1,), (1,)), ((), ())), preferred_element_type=F32
        )
        q_at = q_start + lax.broadcasted_iota(jnp.int32, (q_rows, chunk), 0)
        k_at = start + lax.broadcasted_iota(jnp.int32, (q_rows, chunk), 1)
        bias = jnp.where(q_at >= k_at, 0.0, -1e30)[None]
        return (scores.reshape(together, q_rows, chunk) + bias).reshape(tall, chunk)

    for at in range(0, heads, together):
        rows = jnp.concatenate(
            [
                q_ref[:, h * HEAD_DIMENSION : (h + 1) * HEAD_DIMENSION]
                for h in range(at, at + together)
            ],
            axis=0,
        )

        def one(step, state):
            top_score, run_sum, run_acc = state
            start = pl.multiple_of(step * chunk, chunk)
            scores = scored(rows, start)
            best = jnp.maximum(jnp.max(scores, axis=1, keepdims=True), top_score)
            rescale = jnp.exp2((top_score - best) * factor)
            weights = jnp.exp2((scores - best) * factor)
            total = run_sum * rescale + jnp.sum(weights, axis=1, keepdims=True)
            added = dot(weights.astype(BF16), v_ref[pl.ds(start, chunk)])
            return (best, total, run_acc * rescale + added)

        if steps == 1:
            scores = scored(rows, 0)
            best = jnp.max(scores, axis=1, keepdims=True)
            weights = jnp.exp2((scores - best) * factor)
            total = jnp.sum(weights, axis=1, keepdims=True)
            added = dot(weights.astype(BF16), v_ref[...])
        else:
            best, total, added = lax.fori_loop(
                0,
                (q_start + q_rows + chunk - 1) // chunk,
                one,
                (
                    jnp.full((tall, 1), -1e30, F32),
                    jnp.zeros((tall, 1), F32),
                    jnp.zeros((tall, HEAD_DIMENSION), F32),
                ),
            )
        context = (added / total).astype(BF16)
        for h in range(together):
            out_ref[:, (at + h) * HEAD_DIMENSION : (at + h + 1) * HEAD_DIMENSION] = context[
                h * q_rows : (h + 1) * q_rows
            ]


def attend_part(queries, keys, values, part, parts, context=None):
    q_rows, q_width = queries.shape
    total = keys.shape[0]
    part_width = q_width // parts
    per_kv = parts // KEY_VALUE_HEADS
    chunk = math.gcd(total, 1024)
    before = () if context is None else (context,)
    return pl.pallas_call(
        functools.partial(attention_kernel, chunk),
        grid=(1,),
        out_shape=jax.ShapeDtypeStruct((q_rows, q_width), BF16),
        in_specs=[
            pl.BlockSpec((q_rows, part_width), lambda i: (0, part)),
            pl.BlockSpec((total, HEAD_DIMENSION), lambda i: (0, part // per_kv)),
            pl.BlockSpec((total, HEAD_DIMENSION), lambda i: (0, part // per_kv)),
            *[ANY for _ in before],
        ],
        out_specs=pl.BlockSpec((q_rows, part_width), lambda i: (0, part)),
        input_output_aliases={3: 0} if before else {},
        compiler_params=pltpu.CompilerParams(vmem_limit_bytes=VMEM_LIMIT),
        cost_estimate=SHORT,
        name="attention",
    )(queries, keys, values, *before)


def summed(*terms):
    return sum(term.astype(F32) for term in terms).astype(BF16)


def after(x, *others):
    return lax.optimization_barrier((x, *others))[0]


def on_line(acts, packed, small, queries, w_gate_up, w_down, top, capacity):
    rows, width = acts.shape
    line = [packed, forward(packed), None, backward(packed)]
    crossed = [across(packed), across(line[1]), None, across(line[3])]
    to_core = other_core(packed)
    small = hold(after(small, to_core), in_vmem(w_gate_up, w_down))
    pair = jnp.concatenate([small, across(small)], axis=0)
    line[2] = forward(after(line[1], pair, crossed[0]))
    crossed[2] = across(line[2])
    arrays = [
        [
            line[step],
            crossed[step],
            other_core(line[step]) if step else to_core,
            other_core(crossed[step]),
        ]
        for step in range(LINE)
    ]
    order = (0, 1, 3, 2)
    blocks = [
        (4 * step + core * 2 + y, 2 * at + y, core, functools.partial(from_device, step, y, core))
        for core in range(2)
        for at, step in enumerate(order)
        for y in range(2)
    ]

    def swap_planes(pieces):
        both = jnp.concatenate(pieces, axis=0)
        shares = both.reshape(-1, small.shape[0], both.shape[1])[:, rows:]
        return lax.ppermute(shares.reshape(-1, both.shape[1]), "grp", [(0, 1), (1, 0)])

    pair = after(pair, line[3])
    pairs = [pair, forward(pair), None, backward(pair)]
    pairs[2] = forward(pairs[1])
    keep, mine, crossing = [None] * LINE, [None] * LINE, [None] * LINE

    def experts(first, second, before, beside, split):
        ready = arrays[first] + arrays[second]
        ready = [after(ready[0], *before), *ready[1:]]
        sources = [[(4 * group + i, 0, rows) for i in range(4)] for group in range(2)]
        targets = [
            [(group, 0, 2 * rows), (3, 0, 2 * rows) if group * split else (2, group * 2 * rows, 2 * rows)]
            for group in range(2)
        ]
        keep[first], keep[second], send, *last = run_experts(
            ready,
            sources,
            targets,
            [2 * rows] * 4 if split else [2 * rows, 2 * rows, 4 * rows],
            w_gate_up,
            w_down,
            top,
            rows,
            capacity,
        )
        came = other_core(after(send, *beside))
        mine[first] = (keep[first][:rows], came[:rows])
        crossing[first] = summed(keep[first][rows:], came[rows : 2 * rows])
        if split:
            came = other_core(after(last[0], crossing[first]))
        else:
            came = came[2 * rows :]
        mine[second] = (keep[second][:rows], came[:rows])
        crossing[second] = summed(keep[second][rows:], came[rows:])
        return send

    theirs = [None] * LINE
    experts(1, 0, [line[2], crossed[3]], [crossed[2], pairs[1], pairs[3]], False)
    theirs[1] = across(crossing[1])
    send = experts(2, 3, [crossing[0], crossing[1]], [theirs[1], pairs[2]], True)
    total = summed(*mine[1], after(theirs[1], send))
    moving = forward(total)
    theirs[2], theirs[3] = across(crossing[2]), across(crossing[3])
    own = after(jnp.concatenate([pairs[step] for step in order], axis=0), crossing[2], total)
    other = swap_planes([own])
    swapped = other_core(other)
    smalls = [own, other, other, other_core(own), swapped, swapped]
    total = summed(*mine[2], theirs[2], after(moving, other, smalls[3]))
    moving = forward(total)
    theirs[0] = across(after(crossing[0], total))
    smalls[0] = after(own, total)
    new_keys, values = make_values(sum(arrays, []), blocks, smalls, rows, width)
    context = attend_part(queries, new_keys, values, 0, 4)
    context = attend_part(queries, new_keys, values, 1, 4, context)
    total = summed(*mine[3], theirs[3], after(moving, context))
    moving = forward(total)
    queries = after(queries, total)
    for part in range(2, 4):
        context = attend_part(queries, new_keys, values, part, 4, context)
    layer_out = summed(acts, *mine[0], theirs[0], after(moving, context))
    return context, layer_out


def on_any(acts, packed, small, queries, w_gate_up, w_down, top, capacity):
    rows, width = acts.shape
    keys, value_weight = small[:rows], small[rows:]
    gathered = lax.all_gather(packed, "seq", axis=0, tiled=True)
    all_keys = lax.all_gather(keys, "seq", axis=0, tiled=True)
    weight = lax.all_gather(value_weight, "seq", axis=0, tiled=True)
    total = gathered.shape[0]
    part = total // GROUPS
    pieces = [[(0, group * part, part)] for group in range(GROUPS)]
    (partial,) = run_experts(
        [gathered], pieces, pieces, [total], w_gate_up, w_down, top, rows, capacity
    )
    values = dot(gathered[:, :width], weight).astype(BF16)
    context = None
    for part in range(KEY_VALUE_HEADS):
        context = attend_part(queries, all_keys, values, part, KEY_VALUE_HEADS, context)
    combined = lax.psum_scatter(partial, "seq", scatter_dimension=0, tiled=True)
    return context, summed(acts, combined)


def per_device(
    activations, queries, keys, norm_gain, value_weight, expert_ids, gate_weights, w_gate_up, w_down
):
    pos_rows, sequence_count, model_width = activations.shape
    assert sequence_count == 1 and w_down.shape[0] == 1
    top = expert_ids.shape[2]
    devices = lax.axis_size("seq")
    capacity = max(2, 3 * pos_rows * top // (2 * devices))
    acts = activations.reshape(pos_rows, model_width)
    halves = 2 * devices * pos_rows == model_width and value_weight.shape[0] % (2 * pos_rows) == 0
    line = devices == 4 * LINE and lax.axis_size("grp") == 2 and halves
    packed, small = pack(
        acts,
        norm_gain,
        expert_ids.transpose(1, 2, 0).reshape(top, pos_rows),
        gate_weights.transpose(1, 2, 0).reshape(top, pos_rows),
        keys.reshape(pos_rows, -1),
        value_weight,
        2 if line else 1,
    )
    way = on_line if line else on_any
    context, layer_out = way(
        acts,
        packed,
        small,
        queries.reshape(pos_rows, -1),
        w_gate_up[0],
        w_down[0],
        top,
        capacity,
    )
    return (context.reshape(queries.shape), layer_out.reshape(activations.shape))


def solution(mesh):
    placed = (
        P("seq", "grp", None),
        P("seq", "grp", None),
        P("seq", "grp", None),
        P(),
        P("seq", None),
        P("seq", "grp", None),
        P("seq", "grp", None),
        P("seq", None, None),
        P("seq", None, None),
    )
    return jax.shard_map(
        per_device,
        mesh=mesh,
        in_specs=placed,
        out_specs=(P("seq", "grp", None), P("seq", "grp", None)),
        check_vma=False,
    )
```
